32 devices in a mesh: rep: 4 (over z), shard: 8 (over y, x, core).
Axes of the slice: x: 2, y: 2, z: 4, core: 2. Of those that a mesh axis runs over, the one named last changes fastest.
Arguments:
- inputs: bfloat16 [13312, 1152], P(('rep', 'shard')), may hold values from -6 to 6
- cotangent: bfloat16 [13312, 1152], P(('rep', 'shard')), may hold values from -6 to 6
- attention_gain: bfloat16 [1152], P('shard'), may hold values from 0.5 to 1.5
- hidden_gain: bfloat16 [1152], P('shard'), may hold values from 0.5 to 1.5
- query_weight: bfloat16 [1152, 1152], P('shard'), may hold values from -0.1875 to 0.1875
- key_weight: bfloat16 [1152, 384], P('shard'), may hold values from -0.1875 to 0.1875
- value_weight: bfloat16 [1152, 384], P('shard'), may hold values from -0.1875 to 0.1875
- out_weight: bfloat16 [1152, 1152], P('shard'), may hold values from -0.75 to 0.75
- gate_weight: bfloat16 [1152, 3072], P('shard'), may hold values from -0.1875 to 0.1875
- up_weight: bfloat16 [1152, 3072], P('shard'), may hold values from -0.1875 to 0.1875
- down_weight: bfloat16 [3072, 1152], P('shard'), may hold values from -0.109375 to 0.109375
- query_reduce: bfloat16 [1152, 128], P('shard'), may hold values from -0.1875 to 0.1875
- query_expand: bfloat16 [1152, 128], P('shard'), may hold values from -0.75 to 0.75
- key_reduce: bfloat16 [1152, 128], P('shard'), may hold values from -0.1875 to 0.1875
- key_expand: bfloat16 [384, 128], P('shard'), may hold values from -0.75 to 0.75
- value_reduce: bfloat16 [1152, 128], P('shard'), may hold values from -0.1875 to 0.1875
- value_expand: bfloat16 [384, 128], P('shard'), may hold values from -0.75 to 0.75
- out_reduce: bfloat16 [1152, 128], P('shard'), may hold values from -0.1875 to 0.1875
- out_expand: bfloat16 [1152, 128], P('shard'), may hold values from -3 to 3
- gate_reduce: bfloat16 [1152, 128], P('shard'), may hold values from -0.1875 to 0.1875
- gate_expand: bfloat16 [3072, 128], P('shard'), may hold values from -0.75 to 0.75
- up_reduce: bfloat16 [1152, 128], P('shard'), may hold values from -0.1875 to 0.1875
- up_expand: bfloat16 [3072, 128], P('shard'), may hold values from -0.75 to 0.75
- down_reduce: bfloat16 [3072, 128], P('shard'), may hold values from -0.109375 to 0.109375
- down_expand: bfloat16 [1152, 128], P('shard'), may hold values from -0.75 to 0.75
- parent_segments: int32 [32, 13], P(('rep', 'shard')), may hold values from 0 to 4, as said below
- device_tree: int32 [32], replicated, may hold values from 0 to 31, each once
- tree_adapter: int32 [32], replicated, may hold values from 0 to 7
Outputs:
- layer_output: bfloat16 [13312, 1152], P(('rep', 'shard'))
- input_grad: float32 [13312, 1152], P(('rep', 'shard'))
- query_reduce_grad: float32 [1152, 128], P('shard')
- query_expand_grad: float32 [1152, 128], P('shard')
- key_reduce_grad: float32 [1152, 128], P('shard')
- key_expand_grad: float32 [384, 128], P('shard')
- value_reduce_grad: float32 [1152, 128], P('shard')
- value_expand_grad: float32 [384, 128], P('shard')
- out_reduce_grad: float32 [1152, 128], P('shard')
- out_expand_grad: float32 [1152, 128], P('shard')
- gate_reduce_grad: float32 [1152, 128], P('shard')
- gate_expand_grad: float32 [3072, 128], P('shard')
- up_reduce_grad: float32 [1152, 128], P('shard')
- up_expand_grad: float32 [3072, 128], P('shard')
- down_reduce_grad: float32 [3072, 128], P('shard')
- down_expand_grad: float32 [1152, 128], P('shard')
The draws below stay inside these ranges and needn't reach their ends.
Inputs may be any that keep to these rules, and one draw needn't show every extreme that they name: `parent_segments`: columns 0 to 4 (trunk and four branches) hold 0; columns 5 to 12 (the eight leaves in token order) name the branch 1 to 4 that each leaf follows, each branch named by exactly two leaves. `device_tree`: A permutation of the tree numbers.
All inputs are finite; a program needn't handle non-finite values.
Results may differ from the reference program's by a relative error of at most 0.02.
Values may be sent and summed in bfloat16 or wider, within the bound.
No kernel may reach another device: no remote copies, remote signals or barrier semaphores. Data moves between devices by JAX's collectives and lax.ppermute only.
A program may use at most 256 MiB of HBM per device.

```python
import jax
import jax.numpy as jnp
from jax import lax

D = 1152
Q_HEADS = 18
KV_HEADS = 6
HEAD_DIM = 64
FF = 3072
RANK = 16
ADAPTERS = 8
TRUNK = 128
BRANCH = 24
LEAF = 24
KVW = 384
TREE = 416
TREES = 32
TOKENS = 13312


def draw_parent_segments(key, part):
    key = jax.random.fold_in(key, 11)
    branches = jnp.array([1, 1, 2, 2, 3, 3, 4, 4], jnp.int32)
    tree_keys = jax.random.split(key, TREES)
    leaves = jax.vmap(lambda tree_key: jax.random.permutation(tree_key, branches))(tree_keys)
    return jnp.concatenate([jnp.zeros((TREES, 5), jnp.int32), leaves.astype(jnp.int32)], axis=1)


def plant(values, rng, low, high):
    spot = [jax.random.randint(jax.random.fold_in(rng, axis), (), 0, length) for axis, length in enumerate(values.shape)]
    widest = values.shape.index(max(values.shape))
    neighbour = spot[:widest] + [(spot[widest] + 1) % values.shape[widest]] + spot[widest + 1:]
    return values.at[tuple(spot)].set(low).at[tuple(neighbour)].set(high)


def levels(rng, dims, pieces, smallest, high):
    loudness = 1.0
    for dim, parts in pieces:
        steps = jax.random.uniform(jax.random.fold_in(jax.random.fold_in(rng, 6), dim), (parts,), jnp.float32, smallest / len(pieces), high / len(pieces))
        loudness = loudness * jnp.repeat(jnp.exp(steps), dims[dim] // parts).reshape((-1,) + (1,) * (len(dims) - 1 - dim))
    return loudness


def scatter_about(rng, extent, scale, bound, pieces=(), kind=jnp.bfloat16):
    values = jax.random.normal(rng, extent, jnp.float32) * scale
    if len(pieces) > 0:
        values = levels(rng, extent, pieces, -0.22, 0.18) * values
    return jnp.clip(values, min=-bound, max=bound).astype(kind)


def setup_inputs(seed: int = 0) -> dict:
    seeds = jax.random.split(jax.random.key(seed), 29)
    inputs = scatter_about(seeds[0], (TOKENS, D), 1.0, 6.0, ((0, 32),))
    cotangent = scatter_about(seeds[1], (TOKENS, D), 1.0, 6.0, ((0, 32),))
    attention_gain = jnp.clip(1.0 + 0.1 * jax.random.normal(seeds[2], (D,), jnp.float32), 0.5, 1.5).astype(jnp.bfloat16)
    hidden_gain = jnp.clip(1.0 + 0.1 * jax.random.normal(seeds[3], (D,), jnp.float32), 0.5, 1.5).astype(jnp.bfloat16)
    query_weight = scatter_about(seeds[4], (D, D), D ** -0.5, 0.1875, ((0, 8),))
    key_weight = scatter_about(seeds[5], (D, KVW), D ** -0.5, 0.1875, ((0, 8),))
    value_weight = scatter_about(seeds[6], (D, KVW), D ** -0.5, 0.1875, ((0, 8),))
    out_weight = scatter_about(seeds[7], (D, D), (D // 16) ** -0.5, 0.75, ((0, 8),))
    gate_weight = scatter_about(seeds[8], (D, FF), D ** -0.5, 0.1875, ((0, 8),))
    up_weight = scatter_about(seeds[9], (D, FF), D ** -0.5, 0.1875, ((0, 8),))
    down_weight = scatter_about(seeds[10], (FF, D), FF ** -0.5, 0.109375, ((0, 8),))
    query_reduce = scatter_about(seeds[11], (D, ADAPTERS * RANK), D ** -0.5, 0.1875, ((0, 8),))
    query_expand = scatter_about(seeds[12], (D, ADAPTERS * RANK), (4 * RANK) ** -0.5, 0.75, ((0, 8),))
    key_reduce = scatter_about(seeds[13], (D, ADAPTERS * RANK), D ** -0.5, 0.1875, ((0, 8),))
    key_expand = scatter_about(seeds[14], (KVW, ADAPTERS * RANK), (4 * RANK) ** -0.5, 0.75, ((0, 8),))
    value_reduce = scatter_about(seeds[15], (D, ADAPTERS * RANK), D ** -0.5, 0.1875, ((0, 8),))
    value_expand = scatter_about(seeds[16], (KVW, ADAPTERS * RANK), (4 * RANK) ** -0.5, 0.75, ((0, 8),))
    out_reduce = scatter_about(seeds[17], (D, ADAPTERS * RANK), D ** -0.5, 0.1875, ((0, 8),))
    out_expand = scatter_about(seeds[18], (D, ADAPTERS * RANK), (max(RANK // 4, 1)) ** -0.5, 3.0, ((0, 8),))
    gate_reduce = scatter_about(seeds[19], (D, ADAPTERS * RANK), D ** -0.5, 0.1875, ((0, 8),))
    gate_expand = scatter_about(seeds[20], (FF, ADAPTERS * RANK), (4 * RANK) ** -0.5, 0.75, ((0, 8),))
    up_reduce = scatter_about(seeds[21], (D, ADAPTERS * RANK), D ** -0.5, 0.1875, ((0, 8),))
    up_expand = scatter_about(seeds[22], (FF, ADAPTERS * RANK), (4 * RANK) ** -0.5, 0.75, ((0, 8),))
    down_reduce = scatter_about(seeds[23], (FF, ADAPTERS * RANK), FF ** -0.5, 0.109375, ((0, 8),))
    down_expand = scatter_about(seeds[24], (D, ADAPTERS * RANK), (4 * RANK) ** -0.5, 0.75, ((0, 8),))
    parent_segments = draw_parent_segments(jax.random.fold_in(seeds[28], 71), 0)
    device_tree = jax.random.permutation(seeds[26], TREES).astype(jnp.int32)
    tree_adapter = plant(jax.random.randint(seeds[27], (TREES,), 0, ADAPTERS), jax.random.fold_in(seeds[27], 1), 0, ADAPTERS - 1).astype(jnp.int32)
    return {"inputs": inputs, "cotangent": cotangent, "attention_gain": attention_gain, "hidden_gain": hidden_gain, "query_weight": query_weight, "key_weight": key_weight, "value_weight": value_weight, "out_weight": out_weight, "gate_weight": gate_weight, "up_weight": up_weight, "down_weight": down_weight, "query_reduce": query_reduce, "query_expand": query_expand, "key_reduce": key_reduce, "key_expand": key_expand, "value_reduce": value_reduce, "value_expand": value_expand, "out_reduce": out_reduce, "out_expand": out_expand, "gate_reduce": gate_reduce, "gate_expand": gate_expand, "up_reduce": up_reduce, "up_expand": up_expand, "down_reduce": down_reduce, "down_expand": down_expand, "parent_segments": parent_segments, "device_tree": device_tree, "tree_adapter": tree_adapter}


@jax.custom_vjp
def low(v):
    return lax.optimization_barrier(v.astype(jnp.bfloat16)).astype(jnp.float32)

@jax.custom_vjp
def low_back(v):
    return v

def low_keep(v):
    return (low(v), None)

def low_pass(kept, grad):
    return (grad,)

def back_keep(v):
    return (v, None)

def back_low(kept, grad):
    return (low(grad),)
low.defvjp(low_keep, low_pass)
low_back.defvjp(back_keep, back_low)
eps = 1e-05
highest = lax.Precision.HIGHEST

def matmul(left, right):
    return jnp.dot(left, right, precision=highest)

def tree_layout(parents_row, row_count):
    index = jnp.arange(row_count, dtype=jnp.int32)
    after = index - TRUNK
    leaf_start = TRUNK + 4 * BRANCH
    in_branch = (index >= TRUNK) & (index < leaf_start)
    in_leaf = index >= leaf_start
    segment = jnp.where(in_leaf, 5 + (index - leaf_start) // LEAF, jnp.where(in_branch, 1 + after // BRANCH, 0))
    positions = jnp.where(in_leaf, TRUNK + BRANCH + (index - leaf_start) % LEAF, jnp.where(in_branch, TRUNK + after % BRANCH, index))
    numbers = jnp.arange(13, dtype=jnp.int32)
    parent = lax.optimization_barrier(jnp.sum(jnp.where(segment[:, None] == numbers[None, :], parents_row[None, :], 0), axis=1))
    grand = lax.optimization_barrier(jnp.sum(jnp.where(parent[:, None] == numbers[None, :], parents_row[None, :], 0), axis=1))
    same = (segment[:, None] == segment[None, :]) & (index[None, :] <= index[:, None])
    above = (segment[:, None] != 0) & ((segment[None, :] == parent[:, None]) | (segment[None, :] == grand[:, None]))
    return (same | above, positions)

def rope_tables(positions):
    halfway = HEAD_DIM // 2
    frequency = 10000.0 ** (-jnp.arange(halfway, dtype=jnp.float32) / halfway)
    angles = positions.astype(jnp.float32)[:, None] * frequency[None, :]
    return (jnp.cos(angles), jnp.sin(angles))

def rotate(source, cosine, sine):
    halfway = HEAD_DIM // 2
    first = source[..., :halfway]
    second = source[..., halfway:]
    cos_part = cosine[:, None, :]
    sin_part = sine[:, None, :]
    return jnp.concatenate([first * cos_part - second * sin_part, second * cos_part + first * sin_part], axis=-1)

def rms_norm(source, gain):
    return source * lax.rsqrt(lax.optimization_barrier(jnp.mean(source * source, axis=1, keepdims=True)) + eps) * gain

def adapter_apply(source, reduce_cols, expand_cols):
    reduced = low(low_back(matmul(source, reduce_cols)))
    return matmul(reduced, expand_cols.T)

def layer(source, frozen, adapters, parents_row, adapter_slot):
    gain_attention, gain_hidden, query_full, key_full, value_full, out_full, gate_full, up_full, down_full = frozen
    offset = (adapter_slot * RANK).astype(jnp.int32)
    columns = [lax.dynamic_slice_in_dim(member, offset, RANK, 1) for member in adapters]
    row_count = source.shape[0]
    group_size = Q_HEADS // KV_HEADS
    allowed, positions = tree_layout(parents_row, row_count)
    cosine, sine = rope_tables(positions)
    hidden_one = low(rms_norm(source, gain_attention))
    query_pre = low_back(matmul(hidden_one, query_full) + adapter_apply(hidden_one, columns[0], columns[1]))
    key_pre = low_back(matmul(hidden_one, key_full) + adapter_apply(hidden_one, columns[2], columns[3]))
    value_pre = low_back(matmul(hidden_one, value_full) + adapter_apply(hidden_one, columns[4], columns[5]))
    queries = low(rotate(query_pre.reshape(row_count, Q_HEADS, HEAD_DIM), cosine, sine)).reshape(row_count, KV_HEADS, group_size, HEAD_DIM)
    key_heads = low(rotate(key_pre.reshape(row_count, KV_HEADS, HEAD_DIM), cosine, sine))
    value_heads = low(value_pre).reshape(row_count, KV_HEADS, HEAD_DIM)
    scores = jnp.einsum('igrd,jgd->grij', queries, key_heads, precision=highest) * HEAD_DIM ** (-0.5)
    scores = low_back(jnp.where(allowed[None, None], scores, -1e+30))
    weights = low(jax.nn.softmax(scores, axis=-1))
    attended = jnp.einsum('grij,jgd->igrd', weights, value_heads, precision=highest).reshape(row_count, D)
    attended = low(low_back(attended))
    residual = source + low_back(matmul(attended, out_full) + adapter_apply(attended, columns[6], columns[7]))
    hidden_two = low(rms_norm(residual, gain_hidden))
    gate_pre = low_back(matmul(hidden_two, gate_full) + adapter_apply(hidden_two, columns[8], columns[9]))
    up_pre = low_back(matmul(hidden_two, up_full) + adapter_apply(hidden_two, columns[10], columns[11]))
    middle = low(jax.nn.silu(gate_pre) * up_pre)
    return residual + low_back(matmul(middle, down_full) + adapter_apply(middle, columns[12], columns[13]))

def reference(inputs, cotangent, attention_gain, hidden_gain, query_weight, key_weight, value_weight, out_weight, gate_weight, up_weight, down_weight, query_reduce, query_expand, key_reduce, key_expand, value_reduce, value_expand, out_reduce, out_expand, gate_reduce, gate_expand, up_reduce, up_expand, down_reduce, down_expand, parent_segments, device_tree, tree_adapter):
    frozen = tuple((member.astype(jnp.float32) for member in (attention_gain, hidden_gain, query_weight, key_weight, value_weight, out_weight, gate_weight, up_weight, down_weight)))
    adapters = tuple((member.astype(jnp.float32) for member in (query_reduce, query_expand, key_reduce, key_expand, value_reduce, value_expand, out_reduce, out_expand, gate_reduce, gate_expand, up_reduce, up_expand, down_reduce, down_expand)))
    slots = tree_adapter[device_tree].astype(jnp.int32)
    sources = inputs.reshape(TREES, TREE, D)
    upstreams = cotangent.reshape(TREES, TREE, D)

    def one_tree(totals, items):
        source, upstream, parents_row, adapter_slot = items

        def forward(source_f, adapters_f):
            return layer(source_f, frozen, adapters_f, parents_row, adapter_slot)
        result, pull = jax.vjp(forward, source.astype(jnp.float32), adapters)
        grad_source, grad_adapters = pull(upstream.astype(jnp.float32))
        totals = tuple((total + update for total, update in zip(totals, grad_adapters)))
        return (totals, (result.astype(jnp.bfloat16), grad_source))
    zeros = tuple((jnp.zeros(member.shape, jnp.float32) for member in adapters))
    totals, (outputs, gradients) = lax.scan(one_tree, zeros, (sources, upstreams, parent_segments, slots))
    return (outputs.reshape(TOKENS, D), gradients.reshape(TOKENS, D), totals[0], totals[1], totals[2], totals[3], totals[4], totals[5], totals[6], totals[7], totals[8], totals[9], totals[10], totals[11], totals[12], totals[13])
```

```python
import functools

import jax
import jax.numpy as jnp
from jax import lax
from jax.experimental import pallas as pl
from jax.experimental.pallas import tpu as pltpu
from jax.sharding import PartitionSpec as P

D = 1152
Q_HEADS = 18
KV_HEADS = 6
HEAD_DIM = 64
FF = 3072
RANK = 16
ADAPTERS = 8
TRUNK = 128
BRANCH = 24
LEAF = 24
KVW = 384
PARTS = 8
ROWS = D // PARTS
FROWS = FF // PARTS
SLICES = 3
SL = FF // SLICES
WIDE = D + 128
QKV = D + 2 * KVW
MSG = 3072
eps = 1e-05
F = jnp.float32
B = jnp.bfloat16
VMEM_LIMIT = 58 * 1024 * 1024

NAMES = ("qr", "qe", "kr", "ke", "vr", "ve", "or", "oe", "gr", "ge", "ur", "ue", "dr", "de")
SEG_ROWS = {name: ROWS for name in NAMES}
SEG_ROWS.update(ke=KVW // PARTS, ve=KVW // PARTS, ge=FROWS, ue=FROWS, dr=FROWS)


def lay_out(names):
    offsets = {}
    total = 0
    for name in names:
        offsets[name] = total
        total += -(-SEG_ROWS[name] // 128) * 128
    return offsets, total


SEG_ROWS["gain"] = ROWS
OFF, LANES = lay_out(NAMES + ("gain",))
EARLY = ("ge", "ue", "dr", "gr", "ur", "de")
LATE = ("or", "oe", "qr", "qe", "kr", "ke", "vr", "ve")
EARLY_OFF, EARLY_LANES = lay_out(EARLY)
LATE_OFF, LATE_LANES = lay_out(LATE)
BLOCKS = ((0, 128, 128), (128, 224, 256), (224, 416, 416))


def nn(left, right):
    return lax.dot_general(left, right, (((1,), (0,)), ((), ())), preferred_element_type=F)


def nt(left, right):
    return lax.dot_general(left, right, (((1,), (1,)), ((), ())), preferred_element_type=F)


def tn(left, right):
    return lax.dot_general(left, right, (((0,), (0,)), ((), ())), preferred_element_type=F)


def call(kernel, out_shape, args, spaces=None, scratch=(), flops=0, bytes_accessed=0, name=None):
    in_specs = [
        pl.BlockSpec(memory_space=(spaces or {}).get(i, pltpu.VMEM)) for i in range(len(args))
    ]
    return pl.pallas_call(
        kernel,
        out_shape=[jax.ShapeDtypeStruct(s, d) for s, d in out_shape],
        in_specs=in_specs,
        out_specs=[pl.BlockSpec(memory_space=pltpu.VMEM) for _ in out_shape],
        scratch_shapes=list(scratch),
        compiler_params=pltpu.CompilerParams(vmem_limit_bytes=VMEM_LIMIT),
        cost_estimate=pl.CostEstimate(
            flops=flops, bytes_accessed=bytes_accessed, transcendentals=0
        ),
        name=name,
    )(*args)


def tree_layout(parents_row, row_count):
    index = jnp.arange(row_count, dtype=jnp.int32)
    after = index - TRUNK
    leaf_start = TRUNK + 4 * BRANCH
    in_branch = (index >= TRUNK) & (index < leaf_start)
    in_leaf = index >= leaf_start
    segment = jnp.where(
        in_leaf, 5 + (index - leaf_start) // LEAF, jnp.where(in_branch, 1 + after // BRANCH, 0)
    )
    positions = jnp.where(
        in_leaf,
        TRUNK + BRANCH + (index - leaf_start) % LEAF,
        jnp.where(in_branch, TRUNK + after % BRANCH, index),
    )
    numbers = jnp.arange(13, dtype=jnp.int32)
    parent = jnp.sum(
        jnp.where(segment[:, None] == numbers[None, :], parents_row[None, :], 0), axis=1
    )
    grand = jnp.sum(jnp.where(parent[:, None] == numbers[None, :], parents_row[None, :], 0), axis=1)
    same = (segment[:, None] == segment[None, :]) & (index[None, :] <= index[:, None])
    above = (segment[:, None] != 0) & (
        (segment[None, :] == parent[:, None]) | (segment[None, :] == grand[:, None])
    )
    return (same | above, positions)


def rope_tables(positions):
    halfway = HEAD_DIM // 2
    frequency = 10000.0 ** (-jnp.arange(halfway, dtype=F) / halfway)
    angles = positions.astype(F)[:, None] * frequency[None, :]
    cosine, sine = jnp.cos(angles), jnp.sin(angles)
    return (
        jnp.concatenate([cosine] * 4, axis=1),
        jnp.concatenate([-sine, sine, -sine, sine], axis=1),
    )


def pack_attention_kernel(q, k, v, o, out):
    out[:, :D] = q[...]
    out[:, D : D + KVW] = k[...]
    out[:, D + KVW : QKV] = v[...]
    out[:, QKV:] = o[...]


def pack_hidden_kernel(g, u, d, *outs):
    for f, out in enumerate(outs):
        for s in range(PARTS):
            out[:, s * 128 : (s + 1) * 128] = g[:, s * FROWS + f * 128 : s * FROWS + (f + 1) * 128]
            out[:, SL + s * 128 : SL + (s + 1) * 128] = u[
                :, s * FROWS + f * 128 : s * FROWS + (f + 1) * 128
            ]
        out[:128, 2 * SL :] = d[f * 128 : (f + 1) * 128, :SL]
        for b in range(8):
            out[128:, 2 * SL + b * 128 : 2 * SL + (b + 1) * 128] = d[
                f * 128 + b * 16 : f * 128 + (b + 1) * 16, SL:
            ]


def pack_attention(q, k, v, o):
    return call(pack_attention_kernel, [((ROWS, MSG), B)], (q, k, v, o), name="pack_attention")[0]


def pack_hidden(g, u, d):
    return call(pack_hidden_kernel, [((ROWS, MSG), B)] * SLICES, (g, u, d), name="pack_hidden")


def pack_adapters_kernel(chosen, gains, *refs):
    parts, out = refs[:-1], refs[-1]
    out[...] = jnp.zeros(out.shape, B)
    for name, part in zip(NAMES, parts):
        rows = SEG_ROWS[name]
        out[:, OFF[name] : OFF[name] + rows] = nt(chosen[...], part[...]).astype(B)
    for d in range(PARTS):
        out[d * RANK : (d + 1) * RANK, OFF["gain"] : OFF["gain"] + ROWS] = gains[...]


def prepare_kernel(
    packed, x, cot, acat, ebd, ao, eo, agu, ed, egu, ad, gains, h1a, cota, line
):
    def rows_of(name, width=None, start=0):
        rows = SEG_ROWS[name] if width is None else width
        for j in range(PARTS):
            low = OFF[name] + start
            line[:, j * rows : (j + 1) * rows] = packed[j, :, low : low + rows].astype(F)
        return line[:, : PARTS * rows]

    for ref in (acat, ebd, ao, eo, agu, ed, egu):
        ref[...] = jnp.zeros(ref.shape, B)
    acat[:16, :] = rows_of("qr").astype(B)
    acat[16:32, :] = rows_of("kr").astype(B)
    acat[32:48, :] = rows_of("vr").astype(B)
    ebd[:16, :D] = rows_of("qe").astype(B)
    ebd[16:32, D : D + KVW] = rows_of("ke").astype(B)
    ebd[32:48, D + KVW :] = rows_of("ve").astype(B)
    ao[:16, :] = rows_of("or").astype(B)
    eo[:16, :] = rows_of("oe").astype(B)
    agu[:16, :] = rows_of("gr").astype(B)
    agu[16:32, :] = rows_of("ur").astype(B)
    ed[:16, :] = rows_of("de").astype(B)
    for f in range(SLICES):
        egu[f, :16, :SL] = rows_of("ge", 128, f * 128).astype(B)
        egu[f, 16:32, SL:] = rows_of("ue", 128, f * 128).astype(B)
        down = rows_of("dr", 128, f * 128)
        ad[f] = jnp.concatenate([down, jnp.zeros((112, SL), F)], axis=0).T.astype(B)
    gains[...] = rows_of("gain")
    source = x[...].astype(F)
    scale = lax.rsqrt(jnp.mean(source * source, axis=1, keepdims=True) + eps)
    h1 = (source * scale * gains[0:1, :]).astype(B)
    h1a[:, :D] = h1
    h1a[:, D:] = nt(h1, acat[...]).astype(B)
    cota[:, :D] = cot[...]
    cota[:, D:] = nt(cot[...], ed[...]).astype(B)


def row_at(pos, m, rows):
    return pl.ds(pl.multiple_of(pos[m] * rows, rows), rows)


def swap_halves(value, first):
    return jnp.where(first, pltpu.roll(value, 96, 1), pltpu.roll(value, 32, 1))


def lane_facts(rows):
    lane = lax.broadcasted_iota(jnp.int32, (rows, 128), 1)
    return lane < 64, lane % 64 < 32, lane


def half_masks():
    lane = lax.broadcasted_iota(jnp.int32, (1, 128), 1)
    low = jnp.where(lane < 64, 1.0, 0.0)
    return low, 1.0 - low


def project_kernel(pos, h1a, ebd, cosine, sine, *refs):
    pieces, (q_out, k_out, v_out, weight, sems) = refs[:PARTS], refs[PARTS:]
    copies = [
        pltpu.make_async_copy(
            piece.at[:, pl.ds(0, QKV)], weight.at[row_at(pos, m, ROWS), :], sems.at[m]
        )
        for m, piece in enumerate(pieces)
    ]
    for copy in copies:
        copy.start()
    weight[D:, :] = ebd[...]
    for copy in copies:
        copy.wait()
    rows = h1a.shape[0]
    low, first, _ = lane_facts(rows)
    for block in range(5):
        value = nn(h1a[...], weight[:, block * 384 : (block + 1) * 384])
        for t in range(3):
            part = value[:, t * 128 : (t + 1) * 128]
            if block < 4:
                part = part * cosine[...] + swap_halves(part, first) * sine[...]
            if block < 3:
                at = block * 384 + t * 128
                q_out[:, at : at + 128] = (part * HEAD_DIM**-0.5).astype(B)
            else:
                out = k_out if block == 3 else v_out
                rolled = pltpu.roll(part, 64, 1)
                out[:, t * 256 : t * 256 + 128] = jnp.where(low, part, rolled).astype(B)
                out[:, t * 256 + 128 : (t + 1) * 256] = jnp.where(low, rolled, part).astype(B)


def attend_kernel(pos, x, q, kd, vd, bias, ao, eo, agu, gains, *refs):
    pieces, (oa, lse, x2, h2a, weight, sems) = refs[:PARTS], refs[PARTS:]
    copies = [
        pltpu.make_async_copy(
            piece.at[:, pl.ds(QKV, D)], weight.at[row_at(pos, m, ROWS), :], sems.at[m]
        )
        for m, piece in enumerate(pieces)
    ]
    for copy in copies:
        copy.start()
    weight[D:, :] = eo[...]
    masks = [mask.astype(B) for mask in half_masks()]

    def tile(i, _):
        totals = {}
        for t in range(3):
            at = pl.ds(pl.multiple_of((3 * i + t) * 128, 128), 128)
            for low_row, high_row, keys in BLOCKS:
                rows = high_row - low_row
                lane = lax.broadcasted_iota(jnp.int32, (rows, 128), 1)
                part = q[low_row:high_row, at]
                halves = []
                for half in range(2):
                    head = 2 * t + half
                    group = pl.ds(pl.multiple_of((2 * i + head // 3) * 128, 128), 128)
                    scores = (
                        nt(part * masks[half], kd[:keys, group]) + bias[low_row:high_row, :keys]
                    )
                    top = jnp.max(scores, axis=1, keepdims=True)
                    weights = jnp.exp(scores - top)
                    summed = jnp.sum(weights, axis=1, keepdims=True)
                    halves.append(nn(weights.astype(B), vd[:keys, group]) * (1.0 / summed))
                    total = top + jnp.log(summed)
                    before = totals.get(low_row, jnp.zeros((rows, 128), F))
                    totals[low_row] = jnp.where(lane == head, total, before)
                oa[low_row:high_row, at] = jnp.where(lane < 64, halves[0], halves[1]).astype(B)
        for low_row, high_row, _ in BLOCKS:
            lse[i, low_row:high_row, :] = totals[low_row]
        return 0

    lax.fori_loop(0, 3, tile, 0)
    for copy in copies:
        copy.wait()
    oa[:, D:] = nt(oa[:, :D], ao[...]).astype(B)
    square = jnp.zeros((x.shape[0], 1), F)
    for block in range(3):
        at = slice(block * 384, (block + 1) * 384)
        value = x[:, at].astype(F) + nn(oa[...], weight[:, at])
        x2[:, at] = value
        square += jnp.sum(value * value, axis=1, keepdims=True)
    scale = lax.rsqrt(square / D + eps)
    h2a[:, :D] = (x2[...] * scale * gains[1:2, :]).astype(B)
    h2a[:, D:] = nt(h2a[:, :D], agu[...]).astype(B)


def put(grads, offsets, name, line, value, row, width=None, start=0):
    width = SEG_ROWS[name] if width is None else width
    line[:, : PARTS * width] = value[row : row + RANK, :]
    for j in range(PARTS):
        low = offsets[name] + start
        grads[j, :, low : low + width] = line[:, j * width : (j + 1) * width].astype(B)


def hidden_kernel(f, pos, h2a, cota, egu, ad, *refs):
    refs = list(refs)
    taken = lambda count: [refs.pop(0) for _ in range(count)]
    last = f == SLICES - 1
    y_in, g_in, e_in = taken(3) if f else (None, None, None)
    x2, agu, ed = taken(3) if last else (None, None, None)
    pieces = taken(PARTS)
    y, g, early = taken(3)
    wgu, wd, tail, mid, ggt, gup, line = taken(7)
    y_acc, g_acc = taken(2) if last else (y, g)
    (sems,) = refs
    copies = []
    for m, piece in enumerate(pieces):
        copies.append(
            (
                pltpu.make_async_copy(
                    piece.at[:, pl.ds(0, 2 * SL)],
                    wgu.at[row_at(pos, m, ROWS), :],
                    sems.at[m],
                ),
                pltpu.make_async_copy(
                    piece.at[pl.ds(0, 128), pl.ds(2 * SL, SL)],
                    wd.at[row_at(pos, m, 128), pl.ds(0, SL)],
                    sems.at[PARTS + m],
                ),
                pltpu.make_async_copy(
                    piece.at[pl.ds(128, 16), pl.ds(2 * SL, SL)], tail.at[m], sems.at[2 * PARTS + m]
                ),
            )
        )
    for kind in range(3):
        for copy in copies:
            copy[kind].start()
    wgu[D:, :] = egu[...]
    wd[:, D:] = ad[...]
    if f:
        early[...] = e_in[...]
    else:
        early[...] = jnp.zeros(early.shape, B)
    for kind in range(3):
        for copy in copies:
            copy[kind].wait()
    for m in range(PARTS):
        for b in range(8):
            wd[pl.ds(pl.multiple_of(pos[m] * 128 + b * 16, 16), 16), SL:D] = tail[
                m, :, b * 128 : (b + 1) * 128
            ]

    for c in range(SL // 256):
        at = slice(c * 256, (c + 1) * 256)
        gate = nn(h2a[...], wgu[:, at])
        up = nn(h2a[...], wgu[:, SL + c * 256 : SL + (c + 1) * 256])
        gmid = nt(cota[...], wd[at, :])
        sig = jax.nn.sigmoid(gate)
        silu = gate * sig
        mid[:, at] = (silu * up).astype(B)
        ggt[:, at] = (gmid * up * sig * (1.0 + gate * (1.0 - sig))).astype(B)
        gup[:, at] = (gmid * silu).astype(B)
    for c in range(5):
        at = slice(c * 256, (c + 1) * 256)
        value = nn(mid[...], wd[:, at])
        y_acc[:, at] = value + y_in[:, at] if f else value
        value = nt(ggt[...], wgu[at, :SL]) + nt(gup[...], wgu[at, SL:])
        g_acc[:, at] = value + g_in[:, at] if f else value
    lanes = slice(D, WIDE)
    grow = functools.partial(put, early, EARLY_OFF)
    grow("ge", line, tn(h2a[:, lanes], ggt[...]), 0, 128, f * 128)
    grow("ue", line, tn(h2a[:, lanes], gup[...]), 16, 128, f * 128)
    grow("dr", line, tn(cota[:, lanes], mid[...]), 0, 128, f * 128)
    if last:
        down_red = y_acc[:, lanes].astype(B)
        y[...] = (y_acc[:, :D] + x2[...] + nn(down_red, ed[...])).astype(B)
        grow("de", line, tn(down_red, cota[:, :D]), 0)
        red = g_acc[:, lanes].astype(B)
        g[...] = g_acc[:, :D] + nn(red, agu[...])
        value = tn(red, h2a[:, :D])
        grow("gr", line, value, 0)
        grow("ur", line, value, 16)


def attend_back_kernel(
    pos, gh2, x2, cot, oa, q, kd, vd, lse, bias, cosine, sine, h1a, acat, ebd, ao, eo, gains, *refs
):
    pieces = refs[:PARTS]
    gx2, gqkv, gred, late, weight, go, gk, gv, line, sems = refs[PARTS:]
    copies = [
        pltpu.make_async_copy(
            piece.at[:, pl.ds(QKV, D)], weight.at[row_at(pos, m, ROWS), :], sems.at[m]
        )
        for m, piece in enumerate(pieces)
    ]
    for copy in copies:
        copy.start()
    weight[D:, :] = eo[...]
    late[...] = jnp.zeros(late.shape, B)
    residual = x2[...]
    scale = lax.rsqrt(jnp.mean(residual * residual, axis=1, keepdims=True) + eps)
    weighted = gh2[...] * gains[1:2, :]
    inner = jnp.mean(residual * weighted, axis=1, keepdims=True)
    gx2[...] = (
        cot[...].astype(F) + scale * weighted - residual * (scale * scale * scale) * inner
    )
    branch = gx2[...].astype(B)
    for copy in copies:
        copy.wait()
    red = nt(branch, eo[...]).astype(B)
    for block in range(3):
        at = slice(block * 384, (block + 1) * 384)
        go[:, at] = (nt(branch, weight[at, :]) + nn(red, ao[:, at])).astype(B)
    grow = functools.partial(put, late, LATE_OFF)
    grow("or", line, tn(red, oa[:, :D]), 0)
    grow("oe", line, tn(oa[:, D:], branch), 0)
    masks = [mask.astype(B) for mask in half_masks()]
    wide_masks = half_masks()

    def turn_back(value, low_row, high_row):
        first = lax.broadcasted_iota(jnp.int32, value.shape, 1) % 64 < 32
        return (
            value * cosine[low_row:high_row, :]
            - swap_halves(value, first) * sine[low_row:high_row, :]
        )

    def tile(i, _):
        gk[...] = jnp.zeros(gk.shape, F)
        gv[...] = jnp.zeros(gv.shape, F)
        for t in range(3):
            at = pl.ds(pl.multiple_of((3 * i + t) * 128, 128), 128)
            for low_row, high_row, keys in BLOCKS:
                rows = high_row - low_row
                part = q[low_row:high_row, at]
                upstream = go[low_row:high_row, at]
                product = upstream.astype(F) * oa[low_row:high_row, at].astype(F)
                halves = []
                for half in range(2):
                    head = 2 * t + half
                    side = head // 3
                    group = pl.ds(pl.multiple_of((2 * i + side) * 128, 128), 128)
                    query = part * masks[half]
                    grad = upstream * masks[half]
                    scores = nt(query, kd[:keys, group]) + bias[low_row:high_row, :keys]
                    probs = jnp.exp(scores - lse[i, low_row:high_row, head : head + 1])
                    inner = jnp.sum(product * wide_masks[half], axis=1, keepdims=True)
                    grad_probs = nt(grad, vd[:keys, group])
                    ds = (probs * (grad_probs - inner)).astype(B)
                    gv[side, :keys, :] += tn(probs.astype(B), grad)
                    gk[side, :keys, :] += tn(ds, query)
                    halves.append(nn(ds, kd[:keys, group]))
                low = lax.broadcasted_iota(jnp.int32, (rows, 128), 1) < 64
                value = jnp.where(low, halves[0], halves[1]) * HEAD_DIM**-0.5
                gqkv[low_row:high_row, at] = turn_back(value, low_row, high_row).astype(B)
        rows = gk.shape[1]
        low = lax.broadcasted_iota(jnp.int32, (rows, 128), 1) < 64

        def fold(ref):
            both = [ref[s] + pltpu.roll(ref[s], 64, 1) for s in range(2)]
            return jnp.where(low, both[0], both[1])

        at = pl.multiple_of(i * 128, 128)
        gqkv[:, pl.ds(D + at, 128)] = turn_back(fold(gk), 0, rows).astype(B)
        gqkv[:, pl.ds(D + KVW + at, 128)] = fold(gv).astype(B)
        return 0

    lax.fori_loop(0, 3, tile, 0)
    red = nt(gqkv[...], ebd[...]).astype(B)
    gred[...] = red
    value = tn(red, h1a[:, :D])
    grow("qr", line, value, 0)
    grow("kr", line, value, 16)
    grow("vr", line, value, 32)
    value = tn(h1a[:, D:], gqkv[...])
    grow("qe", line, value[:, :D], 0)
    grow("ke", line, value[:, D : D + KVW], 16)
    grow("ve", line, value[:, D + KVW :], 32)


def finish_kernel(pos, gqkv, gred, acat, x, gx2, gains, *refs):
    pieces, (out, weight, sems) = refs[:PARTS], refs[PARTS:]
    copies = [
        pltpu.make_async_copy(
            piece.at[:, pl.ds(0, QKV)], weight.at[row_at(pos, m, ROWS), :], sems.at[m]
        )
        for m, piece in enumerate(pieces)
    ]
    for copy in copies:
        copy.start()
    source = x[...].astype(F)
    scale = lax.rsqrt(jnp.mean(source * source, axis=1, keepdims=True) + eps)
    for copy in copies:
        copy.wait()
    inner = jnp.zeros((x.shape[0], 1), F)
    for block in range(3):
        at = slice(block * 384, (block + 1) * 384)
        value = nt(gqkv[...], weight[at, :]) + nn(gred[...], acat[:, at])
        value = value * gains[0:1, at]
        out[:, at] = value
        inner += jnp.sum(value * x[:, at].astype(F), axis=1, keepdims=True)
    inner = inner / D
    out[...] = gx2[...] + scale * out[...] - source * (scale * scale * scale) * inner


def gather_by_permutes(messages):
    def swap(value, bit):
        return lax.ppermute(value, "shard", [(i, i ^ bit) for i in range(PARTS)])

    out = []
    for number, message in enumerate(messages):
        near = {0: message, 2: swap(message, 2), 4: swap(message, 4)}
        near[6] = swap(near[4], 2) if number % 2 == 0 else swap(near[2], 4)
        blocks = [None] * PARTS
        for mask, value in near.items():
            blocks[mask] = value
            blocks[mask ^ 1] = swap(value, 1)
        out.append(blocks)
    return out


def rep_sum(value):
    count = lax.axis_size("rep")
    sent = value.astype(B)
    total = value
    for step in range(1, count):
        total = total + lax.ppermute(
            sent, "rep", [(i, (i + step) % count) for i in range(count)]
        ).astype(F)
    return total


def on_device(*args):
    x, cot, gain_a, gain_h = args[:4]
    weights = args[4:11]
    adapters = args[11:25]
    parents, device_tree, tree_adapter = args[25:]
    count = lax.axis_size("shard")
    shard = lax.axis_index("shard")
    group = lax.axis_index("rep") * count
    rows = x.shape[0]
    direct = count == PARTS

    if direct:
        message = pack_attention(*weights[:4])
        messages = [message] + list(pack_hidden(*weights[4:]))
        blocks = gather_by_permutes(messages)
        pos = jnp.bitwise_xor(shard, jnp.arange(PARTS, dtype=jnp.int32)).astype(jnp.int32)
        slots = tree_adapter[lax.dynamic_slice_in_dim(device_tree, group, PARTS)]
        wanted = (slots[:, None] * RANK + jnp.arange(RANK, dtype=jnp.int32)[None, :]).reshape(-1)
        chosen = (
            wanted[:, None] == jnp.arange(ADAPTERS * RANK, dtype=jnp.int32)[None, :]
        ).astype(B)
        gains = jnp.concatenate(
            [gain_a[None], gain_h[None], jnp.zeros((RANK - 2, ROWS), B)], axis=0
        )
        sent = call(
            pack_adapters_kernel,
            [((PARTS * RANK, LANES), B)],
            (chosen, gains) + tuple(adapters),
            name="pack_adapters",
        )[0]
        packed = lax.all_to_all(sent.reshape(PARTS, RANK, LANES), "shard", 0, 0)
    else:
        whole = [lax.all_gather(w, "shard", axis=0, tiled=True) for w in weights]
        cut = lambda w, j: lax.slice_in_dim(
            w, j * (w.shape[0] // PARTS), (j + 1) * (w.shape[0] // PARTS)
        )
        attention = [pack_attention(*(cut(w, j) for w in whole[:4])) for j in range(PARTS)]
        hidden = [pack_hidden(*(cut(w, j) for w in whole[4:])) for j in range(PARTS)]
        blocks = [attention] + [[hidden[j][f] for j in range(PARTS)] for f in range(SLICES)]
        pos = jnp.arange(PARTS, dtype=jnp.int32)
        offset = tree_adapter[device_tree[group + shard]] * RANK
        segments = []
        for name, part in zip(NAMES, adapters):
            full = lax.all_gather(part, "shard", axis=0, tiled=True)
            own = lax.dynamic_slice_in_dim(full, offset, RANK, 1)
            segments.append(own.reshape(PARTS, -1, RANK).transpose(0, 2, 1))
        both = jnp.stack(
            [lax.all_gather(g, "shard", axis=0, tiled=True) for g in (gain_a, gain_h)]
        )
        both = both.reshape(2, PARTS, ROWS).transpose(1, 0, 2)
        segments.append(jnp.pad(both, ((0, 0), (0, RANK - 2), (0, 0))))
        packed = jnp.concatenate(
            [jnp.pad(s, ((0, 0), (0, 0), (0, -s.shape[2] % 128))) for s in segments], axis=2
        )

    allowed, positions = tree_layout(parents[0], rows)
    bias = jnp.where(allowed, 0.0, -1e30).astype(F)
    cosine, sine = rope_tables(positions)

    acat, ebd, ao, eo, agu, ed, egu, ad, gains, h1a, cota = call(
        prepare_kernel,
        [
            ((128, D), B),
            ((128, QKV), B),
            ((128, D), B),
            ((128, D), B),
            ((128, D), B),
            ((128, D), B),
            ((SLICES, 128, 2 * SL), B),
            ((SLICES, SL, 128), B),
            ((RANK, D), F),
            ((rows, WIDE), B),
            ((rows, WIDE), B),
        ],
        (packed, x, cot),
        scratch=[pltpu.VMEM((RANK, PARTS * ROWS), F)],
        flops=2 * rows * D * 256,
        bytes_accessed=8 << 20,
        name="prepare",
    )
    smem = {0: pltpu.SMEM}

    def anywhere(start):
        return {**smem, **{start + i: pl.ANY for i in range(PARTS)}}

    dma = pltpu.SemaphoreType.DMA
    q, kd, vd = call(
        project_kernel,
        [((rows, D), B), ((rows, 2 * KVW), B), ((rows, 2 * KVW), B)],
        (pos, h1a, ebd, cosine, sine, *blocks[0]),
        spaces=anywhere(5),
        scratch=[pltpu.VMEM((WIDE, QKV), B), dma((PARTS,))],
        flops=2 * rows * WIDE * QKV,
        bytes_accessed=8 << 20,
        name="project",
    )
    oa, lse, x2, h2a = call(
        attend_kernel,
        [((rows, WIDE), B), ((3, rows, 128), F), ((rows, D), F), ((rows, WIDE), B)],
        (pos, x, q, kd, vd, bias, ao, eo, agu, gains, *blocks[0]),
        spaces=anywhere(10),
        scratch=[pltpu.VMEM((WIDE, D), B), dma((PARTS,))],
        flops=12 * rows * WIDE * D,
        bytes_accessed=16 << 20,
        name="attend",
    )
    early = None
    for f in range(SLICES):
        last = f == SLICES - 1
        operands = [pos, h2a, cota, egu[f], ad[f]]
        if f:
            operands += [y, g, early]
        if last:
            operands += [x2, agu, ed]
        start = len(operands)
        shapes = (
            [((rows, D), B), ((rows, D), F)]
            if last
            else [((rows, WIDE), F), ((rows, WIDE), F)]
        )
        scratch = [
            pltpu.VMEM((WIDE, 2 * SL), B),
            pltpu.VMEM((SL, WIDE), B),
            pltpu.VMEM((PARTS, 16, SL), B),
            pltpu.VMEM((rows, SL), B),
            pltpu.VMEM((rows, SL), B),
            pltpu.VMEM((rows, SL), B),
            pltpu.VMEM((RANK, D), F),
        ]
        if last:
            scratch += [pltpu.VMEM((rows, WIDE), F), pltpu.VMEM((rows, WIDE), F)]
        y, g, early = call(
            functools.partial(hidden_kernel, f),
            shapes + [((PARTS, RANK, EARLY_LANES), B)],
            (*operands, *blocks[1 + f]),
            spaces=anywhere(start),
            scratch=scratch + [dma((3 * PARTS,))],
            flops=12 * rows * WIDE * SL,
            bytes_accessed=20 << 20,
            name="hidden_%d" % f,
        )
    layer_output, gh2 = y, g
    gx2, gqkv, gred, late = call(
        attend_back_kernel,
        [
            ((rows, D), F),
            ((rows, QKV), B),
            ((rows, 128), B),
            ((PARTS, RANK, LATE_LANES), B),
        ],
        (
            pos, gh2, x2, cot, oa, q, kd, vd, lse, bias, cosine, sine, h1a, acat, ebd, ao, eo,
            gains, *blocks[0],
        ),
        spaces=anywhere(18),
        scratch=[
            pltpu.VMEM((WIDE, D), B),
            pltpu.VMEM((rows, D), B),
            pltpu.VMEM((2, rows, 128), F),
            pltpu.VMEM((2, rows, 128), F),
            pltpu.VMEM((RANK, D), F),
            dma((PARTS,)),
        ],
        flops=24 * rows * WIDE * D,
        bytes_accessed=20 << 20,
        name="attend_back",
    )
    (input_grad,) = call(
        finish_kernel,
        [((rows, D), F)],
        (pos, gqkv, gred, acat, x, gx2, gains, *blocks[0]),
        spaces=anywhere(7),
        scratch=[pltpu.VMEM((D, QKV), B), dma((PARTS,))],
        flops=2 * rows * D * QKV,
        bytes_accessed=12 << 20,
        name="finish",
    )
    owned = {}
    for grads, names, offsets in ((early, EARLY, EARLY_OFF), (late, LATE, LATE_OFF)):
        if direct:
            received = lax.all_to_all(grads, "shard", 0, 0)
            lanes = grads.shape[2]
            total = rep_sum(tn(received.reshape(PARTS * RANK, lanes), chosen))
            for name in names:
                owned[name] = lax.slice_in_dim(
                    total, offsets[name], offsets[name] + SEG_ROWS[name]
                )
        else:
            for name in names:
                part = grads[:, :, offsets[name] : offsets[name] + SEG_ROWS[name]]
                part = part.transpose(0, 2, 1).reshape(-1, RANK)
                wide = lax.dynamic_update_slice_in_dim(
                    jnp.zeros((part.shape[0], ADAPTERS * RANK), B), part, offset, 1
                )
                wide = lax.psum_scatter(wide, "shard", scatter_dimension=0, tiled=True)
                owned[name] = lax.psum(wide, "rep").astype(F)
    return (layer_output, input_grad) + tuple(owned[name] for name in NAMES)


def solution(mesh):
    token = P(("rep", "shard"), None)
    row = P("shard", None)
    return jax.shard_map(
        on_device,
        mesh=mesh,
        in_specs=(token, token, P("shard"), P("shard")) + (row,) * 21 + (token, P(), P()),
        out_specs=(token, token) + (row,) * 14,
        check_vma=False,
    )
```

```python
import functools

import jax
import jax.numpy as jnp
from jax import lax
from jax.experimental import pallas as pl
from jax.experimental.pallas import tpu as pltpu
from jax.sharding import PartitionSpec as P

D = 1152
Q_HEADS = 18
KV_HEADS = 6
HEAD_DIM = 64
FF = 3072
RANK = 16
ADAPTERS = 8
TRUNK = 128
BRANCH = 24
LEAF = 24
KVW = 384
PARTS = 8
ROWS = D // PARTS
FROWS = FF // PARTS
SLICES = 3
SL = FF // SLICES
WIDE = D + 128
QKV = D + 2 * KVW
MSG = 3072
eps = 1e-05
F = jnp.float32
B = jnp.bfloat16


class Words:
    def __getattr__(self, word):
        return word


N = Words()
VMEM_LIMIT = 58 * 1024 * 1024

NAMES = (N.qr, N.qe, N.kr, N.ke, N.vr, N.ve, N.wr, N.oe, N.gr, N.ge, N.ur, N.ue, N.dr, N.de)
SEG_ROWS = {name: ROWS for name in NAMES}
SEG_ROWS.update(ke=KVW // PARTS, ve=KVW // PARTS, ge=FROWS, ue=FROWS, dr=FROWS)


SEG_ROWS[N.gain] = ROWS
EARLY = (N.ge, N.ue, N.dr, N.gr, N.ur, N.de)
LATE = (N.wr, N.oe, N.qr, N.qe, N.kr, N.ke, N.vr, N.ve)
QUARTERS = 4


def lay_out(names, unit):
    offsets = {}
    total = 0
    for name in names:
        offsets[name] = total
        total += SEG_ROWS[name]
    return offsets, -(-total // unit) * unit


EARLY_OFF, EARLY_LANES = lay_out(EARLY, QUARTERS * 128)
LATE_OFF, LATE_LANES = lay_out(LATE, QUARTERS * 128)
OFF, LANES = lay_out(EARLY + LATE + (N.gain,), 128)
BLOCKS = ((0, 128, 128), (128, 224, 256), (224, 416, 416))


def nn(left, right):
    return lax.dot_general(left, right, (((1,), (0,)), ((), ())), preferred_element_type=F)


def nt(left, right):
    return lax.dot_general(left, right, (((1,), (1,)), ((), ())), preferred_element_type=F)


def tn(left, right):
    return lax.dot_general(left, right, (((0,), (0,)), ((), ())), preferred_element_type=F)


RUNS = ((0, 1), (2,))
COST = dict(flops=1 << 20, bytes_accessed=1 << 16, transcendentals=0)


def call(kernel, out_shape, args, spaces=None, scratch=(), name=None):
    in_specs = [
        pl.BlockSpec(memory_space=(spaces or {}).get(i, pltpu.VMEM)) for i in range(len(args))
    ]
    return pl.pallas_call(
        kernel,
        out_shape=[jax.ShapeDtypeStruct(s, d) for s, d in out_shape],
        in_specs=in_specs,
        out_specs=[pl.BlockSpec(memory_space=pltpu.VMEM) for _ in out_shape],
        scratch_shapes=list(scratch),
        compiler_params=pltpu.CompilerParams(vmem_limit_bytes=VMEM_LIMIT),
        cost_estimate=pl.CostEstimate(**COST),
        name=name,
    )(*args)


class Frame:
    def __init__(self, pos, near, far, outs, sems):
        self.pos, self.near, self.far, self.outs, self.sems = pos, near, far, outs, sems
        self.used = 0
        self.coming = {}
        self.leaving = []

    def copy(self, source, target):
        moved = pltpu.make_async_copy(source, target, self.sems.at[self.used])
        self.used += 1
        moved.start()
        return moved

    def fetch(self, *names):
        for name in names:
            self.coming[name] = [self.copy(self.far[name], self.near[name])]

    def fetch_into(self, key, source, target):
        self.coming.setdefault(key, []).append(self.copy(source, target))

    def fetch_rows(self, key, pieces, low, lanes, target, rows=ROWS, start=0, to=0):
        for piece, (m, begin, end) in zip(pieces, HELD):
            a, b = max(low, begin), min(low + lanes, end)
            if a < b:
                self.fetch_into(
                    key,
                    piece.at[pl.ds(start, rows), pl.ds(a - begin, b - a)],
                    target.at[row_at(self.pos, m, rows), pl.ds(to + a - low, b - a)],
                )

    def wait(self, *keys):
        for key in keys:
            for moved in self.coming.pop(key, ()):
                moved.wait()

    def __getitem__(self, name):
        self.wait(name)
        return self.near[name]

    def send(self, name, at=None):
        near, far = self.near[name], self.outs[name]
        if at is not None:
            near, far = near.at[:, at], far.at[:, at]
        self.leaving.append(self.copy(near, far))

    def close(self):
        for moved in self.leaving:
            moved.wait()


def launch(
    name, body, outs, ins, pieces=(), pos=None, scratch=None, sems=64, weigh=None
):
    scratch = scratch or {}
    operands = ([] if pos is None else [pos]) + list(ins.values()) + list(pieces)

    def kernel(*refs):
        refs = list(refs)
        take = lambda count: [refs.pop(0) for _ in range(count)]
        where = None if pos is None else take(1)[0]
        far = dict(zip(ins, take(len(ins))))
        parts = take(len(pieces))
        results = dict(zip(outs, take(len(outs))))
        near = dict(zip(ins, take(len(ins))))
        near.update(zip(outs, take(len(outs))))
        near.update(zip(scratch, take(len(scratch))))
        frame = Frame(where, near, far, results, refs[0])
        body(frame, parts)
        frame.close()

    hbm = pl.BlockSpec(memory_space=pltpu.HBM)
    specs = [hbm] * (len(ins) + len(pieces))
    if pos is not None:
        specs = [pl.BlockSpec(memory_space=pltpu.SMEM)] + specs
    results = pl.pallas_call(
        kernel,
        out_shape=[jax.ShapeDtypeStruct(s, d) for s, d in outs.values()],
        in_specs=specs,
        out_specs=[hbm] * len(outs),
        scratch_shapes=[pltpu.VMEM(v.shape, v.dtype) for v in ins.values()]
        + [pltpu.VMEM(s, d) for s, d in outs.values()]
        + [pltpu.VMEM(s, d) for s, d in scratch.values()]
        + [pltpu.SemaphoreType.DMA((sems,))],
        compiler_params=pltpu.CompilerParams(vmem_limit_bytes=VMEM_LIMIT),
        cost_estimate=pl.CostEstimate(**(weigh or COST)),
        name=name,
    )(*operands)
    return dict(zip(outs, results))


def tree_layout(parents_row, row_count):
    index = jnp.arange(row_count, dtype=jnp.int32)
    after = index - TRUNK
    leaf_start = TRUNK + 4 * BRANCH
    in_branch = (index >= TRUNK) & (index < leaf_start)
    in_leaf = index >= leaf_start
    segment = jnp.where(
        in_leaf, 5 + (index - leaf_start) // LEAF, jnp.where(in_branch, 1 + after // BRANCH, 0)
    )
    positions = jnp.where(
        in_leaf,
        TRUNK + BRANCH + (index - leaf_start) % LEAF,
        jnp.where(in_branch, TRUNK + after % BRANCH, index),
    )
    numbers = jnp.arange(13, dtype=jnp.int32)
    parent = jnp.sum(
        jnp.where(segment[:, None] == numbers[None, :], parents_row[None, :], 0), axis=1
    )
    grand = jnp.sum(jnp.where(parent[:, None] == numbers[None, :], parents_row[None, :], 0), axis=1)
    same = (segment[:, None] == segment[None, :]) & (index[None, :] <= index[:, None])
    above = (segment[:, None] != 0) & (
        (segment[None, :] == parent[:, None]) | (segment[None, :] == grand[:, None])
    )
    return (same | above, positions)


def rope_tables(positions):
    halfway = HEAD_DIM // 2
    frequency = 10000.0 ** (-jnp.arange(halfway, dtype=F) / halfway)
    angles = positions.astype(F)[:, None] * frequency[None, :]
    cosine, sine = jnp.cos(angles), jnp.sin(angles)
    return (
        jnp.concatenate([cosine] * 4, axis=1),
        jnp.concatenate([-sine, sine, -sine, sine], axis=1),
    )


def attention_copies(weights, out):
    copies = []
    at = 0
    for weight in weights:
        copies.append((weight, out.at[:, pl.ds(at, weight.shape[1])]))
        at += weight.shape[1]
    return copies


def slice_copies(f, g, u, d, out):
    at = pl.multiple_of(f * 128, 128)
    copies = []
    for s in range(PARTS):
        lanes = pl.ds(pl.multiple_of(s * FROWS + at, 128), 128)
        copies.append((g.at[:, lanes], out.at[:, pl.ds(s * 128, 128)]))
        copies.append((u.at[:, lanes], out.at[:, pl.ds(SL + s * 128, 128)]))
    copies.append(
        (d.at[pl.ds(at, 128), pl.ds(0, SL)], out.at[pl.ds(0, 128), pl.ds(2 * SL, SL)])
    )
    for b in range(8):
        rows = pl.ds(pl.multiple_of(at + b * 16, 16), 16)
        copies.append(
            (
                d.at[rows, pl.ds(SL, 128)],
                out.at[pl.ds(128, 16), pl.ds(2 * SL + b * 128, 128)],
            )
        )
    return copies


def start_all(copies, sems, first=0):
    moved = [
        pltpu.make_async_copy(source, target, sems.at[first + k])
        for k, (source, target) in enumerate(copies)
    ]
    for copy in moved:
        copy.start()
    return moved


SLICE_COPIES = 2 * PARTS + 9


def pack_attention_kernel(q, k, v, o, out, sems):
    for copy in start_all(attention_copies((q, k, v, o), out), sems):
        copy.wait()


def pack_slices_kernel(numbers, g, u, d, *refs):
    outs, sems = refs[:-1], refs[-1]
    moved = []
    for n, out in enumerate(outs):
        moved += start_all(slice_copies(numbers[n], g, u, d, out), sems, n * SLICE_COPIES)
    for copy in moved:
        copy.wait()


def pack_attention(weights):
    return call(
        pack_attention_kernel,
        [((ROWS, MSG), B)],
        weights,
        spaces={n: pltpu.HBM for n in range(4)},
        scratch=[pltpu.SemaphoreType.DMA((4,))],
        name=N.pack_attention,
    )[0]


def pack_slices(numbers, weights):
    numbers = jnp.stack([jnp.asarray(f, jnp.int32) for f in numbers])
    return call(
        pack_slices_kernel,
        [((ROWS, MSG), B)] * numbers.shape[0],
        (numbers, *weights),
        spaces={0: pltpu.SMEM, 1: pltpu.HBM, 2: pltpu.HBM, 3: pltpu.HBM},
        scratch=[pltpu.SemaphoreType.DMA((numbers.shape[0] * SLICE_COPIES,))],
        name=N.pack_slices,
    )


def choose(trees, slots, first, count):
    column = lax.broadcasted_iota(jnp.int32, (RANK, ADAPTERS * RANK), 1)
    row = lax.broadcasted_iota(jnp.int32, (RANK, ADAPTERS * RANK), 0)
    parts = [
        jnp.where(column == slots[trees[first + d]] * RANK + row, 1.0, 0.0) for d in range(count)
    ]
    return jnp.concatenate(parts, axis=0).astype(B)


def pack_first_kernel(facts, trees, slots, *refs):
    weights, gains, parts = refs[:7], refs[7:9], refs[9:23]
    first, attention, out, wide, sems = refs[23:]
    moved = start_all(slice_copies(facts[1], *weights[4:], first), sems)
    moved += start_all(attention_copies(weights[:4], attention), sems, SLICE_COPIES)
    chosen = choose(trees, slots, facts[0], PARTS)
    for name, part in zip(NAMES, parts):
        wide[:, OFF[name] : OFF[name] + SEG_ROWS[name]] = nt(chosen, part[...])
    row = lax.broadcasted_iota(jnp.int32, (RANK, ROWS), 0)
    both = jnp.where(
        row == 0, gains[0][...].astype(F), jnp.where(row == 1, gains[1][...].astype(F), 0.0)
    )
    for d in range(PARTS):
        wide[d * RANK : (d + 1) * RANK, OFF[N.gain] : OFF[N.gain] + ROWS] = both
    out[...] = wide[...].astype(B)
    for copy in moved:
        copy.wait()


HALF = MSG // 2
HELD = [(m, 0, MSG) for m in range(6)] + [
    (m, low, low + HALF) for m in (6, 7) for low in (0, HALF)
]
HELD_COUNT = len(HELD)


def row_at(pos, m, rows):
    return pl.ds(pl.multiple_of(pos[m] * rows, rows), rows)


def swap_halves(value, first):
    return jnp.where(first, pltpu.roll(value, 96, 1), pltpu.roll(value, 32, 1))


def half_masks():
    lane = lax.broadcasted_iota(jnp.int32, (1, 128), 1)
    low = jnp.where(lane < 64, 1.0, 0.0)
    return low, 1.0 - low


def prepare_body(c, _):
    c.fetch(N.x, N.cot, N.packed)
    near = c.near
    for name in (N.acat, N.ebd, N.ao, N.eo, N.agu, N.ed, N.egu):
        near[name][...] = jnp.zeros(near[name].shape, B)
    source = c[N.x][...].astype(F)
    scale = lax.rsqrt(jnp.mean(source * source, axis=1, keepdims=True) + eps)
    wide = near[N.wide]
    wide[...] = c[N.packed][...].astype(F)
    line = near[N.line]

    def rows_of(name, width=None, start=0):
        rows = SEG_ROWS[name] if width is None else width
        low = OFF[name] + start
        for j in range(PARTS):
            line[:, j * rows : (j + 1) * rows] = wide[j, :, low : low + rows]
        return line[:, : PARTS * rows]

    near[N.gains][...] = rows_of(N.gain)
    acat = near[N.acat]
    acat[:16, :] = rows_of(N.qr).astype(B)
    acat[16:32, :] = rows_of(N.kr).astype(B)
    acat[32:48, :] = rows_of(N.vr).astype(B)
    near[N.ed][:16, :] = rows_of(N.de).astype(B)
    h1 = (source * scale * near[N.gains][0:1, :]).astype(B)
    near[N.h1a][:, :D] = h1
    near[N.h1a][:, D:] = nt(h1, acat[...]).astype(B)
    near[N.cota][:, :D] = c[N.cot][...]
    near[N.cota][:, D:] = nt(c[N.cot][...], near[N.ed][...]).astype(B)
    ebd, agu, egu = near[N.ebd], near[N.agu], near[N.egu]
    ebd[:16, :D] = rows_of(N.qe).astype(B)
    ebd[16:32, D : D + KVW] = rows_of(N.ke).astype(B)
    ebd[32:48, D + KVW :] = rows_of(N.ve).astype(B)
    for name in (N.h1a, N.cota, N.acat, N.ebd, N.gains, N.ed):
        c.send(name)
    near[N.ao][:16, :] = rows_of(N.wr).astype(B)
    near[N.eo][:16, :] = rows_of(N.oe).astype(B)
    agu[:16, :] = rows_of(N.gr).astype(B)
    agu[16:32, :] = rows_of(N.ur).astype(B)
    for name in (N.ao, N.eo, N.agu):
        c.send(name)
    for f in range(SLICES):
        egu[f, :16, :SL] = rows_of(N.ge, 128, f * 128).astype(B)
        egu[f, 16:32, SL:] = rows_of(N.ue, 128, f * 128).astype(B)
        down = rows_of(N.dr, 128, f * 128)
        near[N.ad][f] = jnp.concatenate([down, jnp.zeros((112, SL), F)], axis=0).T.astype(B)
    c.send(N.egu)
    c.send(N.ad)


def project_body(c, pieces):
    near = c.near
    weight = near[N.weight]
    c.fetch(N.h1a)
    c.fetch_rows(N.w0, pieces, 0, 768, weight)
    c.fetch_into(N.w0, c.far[N.ebd], weight.at[pl.ds(D, 128), :])
    c.fetch(N.cosine, N.sine)
    c.fetch_rows(N.w1, pieces, 768, QKV - 768, weight, to=768)
    h1a = c[N.h1a]
    rows = h1a.shape[0]
    lane = lax.broadcasted_iota(jnp.int32, (rows, 128), 1)
    low, first = lane < 64, lane % 64 < 32
    q, kd, vd = near[N.q], near[N.kd], near[N.vd]
    c.wait(N.w0)
    for block in range(5):
        if block == 2:
            c.wait(N.w1)
        value = nn(h1a[...], weight[:, block * 384 : (block + 1) * 384])
        for t in range(3):
            part = value[:, t * 128 : (t + 1) * 128]
            if block < 4:
                part = part * c[N.cosine][...] + swap_halves(part, first) * c[N.sine][...]
            if block < 3:
                at = block * 384 + t * 128
                q[:, at : at + 128] = (part * HEAD_DIM**-0.5).astype(B)
            else:
                out = kd if block == 3 else vd
                rolled = pltpu.roll(part, 64, 1)
                out[:, t * 256 : t * 256 + 128] = jnp.where(low, part, rolled).astype(B)
                out[:, t * 256 + 128 : (t + 1) * 256] = jnp.where(low, rolled, part).astype(B)
    for name in (N.q, N.kd, N.vd):
        c.send(name)


def attend_body(c, pieces):
    near = c.near
    wout = near[N.wout]
    c.fetch(N.q, N.kd, N.bias, N.vd)
    c.fetch_rows(N.wout, pieces, QKV, D, wout)
    c.fetch_into(N.wout, c.far[N.eo], wout.at[pl.ds(D, 128), :])
    c.fetch(N.x, N.ao, N.agu, N.gains)
    q, kd, vd = c[N.q], c[N.kd], c[N.vd]
    rows = q.shape[0]
    masks = [mask.astype(B) for mask in half_masks()]
    bias, oa, lse, x2, h2a = c[N.bias], near[N.oa], near[N.lse], near[N.x2], near[N.h2a]

    def tile(i, _):
        totals = {}
        values = []
        for side in range(2):
            group = pl.ds(pl.multiple_of((2 * i + side) * 128, 128), 128)
            both = vd[:, group]
            values.append([both * masks[0] + masks[1], both * masks[1] + masks[0]])
        for t in range(3):
            at = pl.ds(pl.multiple_of((3 * i + t) * 128, 128), 128)
            for low_row, high_row, keys in BLOCKS:
                lane = lax.broadcasted_iota(jnp.int32, (high_row - low_row, 128), 1)
                part = q[low_row:high_row, at]
                halves = []
                tops = []
                for half in range(2):
                    head = 2 * t + half
                    side = head // 3
                    group = pl.ds(pl.multiple_of((2 * i + side) * 128, 128), 128)
                    scores = (
                        nt(part * masks[half], kd[:keys, group]) + bias[low_row:high_row, :keys]
                    )
                    top = jnp.max(scores, axis=1, keepdims=True)
                    weights = jnp.exp(scores - top).astype(B)
                    halves.append(nn(weights, values[side][half][:keys]))
                    tops.append(top)
                summed = pltpu.roll(jnp.where(lane < 64, halves[1], halves[0]), 64, 1)
                oa[low_row:high_row, at] = (
                    jnp.where(lane < 64, halves[0], halves[1]) / summed
                ).astype(B)
                lse[i, t, low_row:high_row, :] = jnp.where(
                    lane < 64, tops[0], tops[1]
                ) + jnp.log(summed)
        return 0

    lax.fori_loop(0, 3, tile, 0)
    c.send(N.lse)
    oa[:, D:] = nt(oa[:, :D], c[N.ao][...]).astype(B)
    c.send(N.oa)
    c.wait(N.wout)
    square = jnp.zeros((rows, 1), F)
    for block in range(3):
        at = slice(block * 384, (block + 1) * 384)
        value = c[N.x][:, at].astype(F) + nn(oa[...], wout[:, at])
        x2[:, at] = value
        square += jnp.sum(value * value, axis=1, keepdims=True)
    c.send(N.x2)
    scale = lax.rsqrt(square / D + eps)
    h2a[:, :D] = (x2[...] * scale * c[N.gains][1:2, :]).astype(B)
    h2a[:, D:] = nt(h2a[:, :D], c[N.agu][...]).astype(B)
    c.send(N.h2a)


def put(grads, offsets, name, line, value, row, width=None, start=0):
    width = SEG_ROWS[name] if width is None else width
    line[:, : PARTS * width] = value[row : row + RANK, :]
    for j in range(PARTS):
        at = pl.ds(offsets[name] + start, width)
        if not isinstance(start, int):
            at = pl.ds(pl.multiple_of(offsets[name] + start, 128), width)
        grads[j, :, at] = line[:, j * width : (j + 1) * width]


def hand_out(grads, out):
    part = out.shape[3]
    for q in range(QUARTERS):
        out[q] = grads[:, :, q * part : (q + 1) * part].astype(B)


def hidden_body(slices, c, pieces):
    first, last = slices[0] == 0, slices[-1] == SLICES - 1
    near = c.near
    mid, ggt, gup, line = near[N.mid], near[N.ggt], near[N.gup], near[N.line]
    c.fetch(N.h2a)
    number = [c.pos[PARTS], 1 - c.pos[PARTS]] if first else slices
    for n, f in enumerate(slices):
        wgu, wd, tail = near[N.wgu].at[n], near[N.wd].at[n], near[N.tail].at[n]
        own = pieces[n * HELD_COUNT : (n + 1) * HELD_COUNT]
        for part in range(2):
            for side in range(2):
                at = side * SL + part * 512
                c.fetch_rows((N.gu, f, part), own, at, 512, wgu, to=at)
            if part == 0:
                c.fetch_into((N.gu, f, 0), c.far[N.egu].at[number[n]], wgu.at[pl.ds(D, 128), :])
                if n == 0:
                    c.fetch(N.cota)
                c.fetch_rows((N.wd, f), own, 2 * SL, SL, wd, 128)
                c.fetch_rows((N.wd, f), own, 2 * SL, SL, tail, 16, 128)
                c.fetch_into((N.wd, f), c.far[N.ad].at[number[n]], wd.at[:, pl.ds(D, 128)])
    if not first:
        c.fetch(N.y_in, N.g_in, N.early_in)
    if last:
        c.fetch(N.x2, N.agu, N.ed)
    h2a = c[N.h2a]
    y_acc, g_acc = (near[N.y_acc], near[N.g_acc]) if last else (near[N.y], near[N.g])
    early = near[N.early_acc] if last else near[N.early]
    grow = functools.partial(put, early, EARLY_OFF)
    lanes = slice(D, WIDE)
    for n, f in enumerate(slices):
        wgu, wd, tail = near[N.wgu].at[n], near[N.wd].at[n], near[N.tail].at[n]
        for k in range(SL // 256):
            at = slice(k * 256, (k + 1) * 256)
            if k % 2 == 0:
                c.wait((N.gu, f, k // 2))
            gate = nn(h2a[...], wgu[:, at])
            up = nn(h2a[...], wgu[:, SL + k * 256 : SL + (k + 1) * 256])
            sig = jax.nn.sigmoid(gate)
            silu = gate * sig
            if k == 0:
                cota = c[N.cota]
                c.wait((N.wd, f))
                for m in range(PARTS):
                    for b in range(8):
                        wd[m * 128 + b * 16 : m * 128 + (b + 1) * 16, SL:D] = tail[
                            m * 16 : (m + 1) * 16, b * 128 : (b + 1) * 128
                        ]
            gmid = nt(cota[...], wd[at, :])
            mid[:, at] = (silu * up).astype(B)
            ggt[:, at] = (gmid * up * sig * (1.0 + gate * (1.0 - sig))).astype(B)
            gup[:, at] = (gmid * silu).astype(B)
        for k in range(5):
            at = slice(k * 256, (k + 1) * 256)
            value = nn(mid[...], wd[:, at])
            if n:
                value += y_acc[:, at]
            elif not first:
                value += c[N.y_in][:, at]
            y_acc[:, at] = value
            value = nt(ggt[...], wgu[at, :SL]) + nt(gup[...], wgu[at, SL:])
            if n:
                value += g_acc[:, at]
            elif not first:
                value += c[N.g_in][:, at]
            g_acc[:, at] = value
            if not last and n == len(slices) - 1:
                c.send(N.y, at)
                c.send(N.g, at)
        if n == 0:
            early[...] = jnp.zeros(early.shape, F) if first else c[N.early_in][...]
        grow(N.ge, line, tn(h2a[:, lanes], ggt[...]), 0, 128, number[n] * 128)
        grow(N.ue, line, tn(h2a[:, lanes], gup[...]), 16, 128, number[n] * 128)
        grow(N.dr, line, tn(cota[:, lanes], mid[...]), 0, 128, number[n] * 128)
    if last:
        red = g_acc[:, lanes].astype(B)
        near[N.g][...] = g_acc[:, :D] + nn(red, c[N.agu][...])
        c.send(N.g)
        down_red = y_acc[:, lanes].astype(B)
        grow(N.de, line, tn(down_red, cota[:, :D]), 0)
        value = tn(red, h2a[:, :D])
        grow(N.gr, line, value, 0)
        grow(N.ur, line, value, 16)
        hand_out(early, near[N.early])
        c.send(N.early)
        near[N.y][...] = (y_acc[:, :D] + c[N.x2][...] + nn(down_red, c[N.ed][...])).astype(B)
        c.send(N.y)
    else:
        c.send(N.early)


def back_body(c, pieces):
    near, far = c.near, c.far
    c.fetch(N.gh2, N.x2, N.gains, N.cot)
    weight, gx2, go, late, line = (near[k] for k in (N.weight, N.gx2, N.go, N.late_acc, N.line))
    c.fetch_into(N.eo, far[N.eo], weight.at[pl.ds(D, 128), :])
    c.fetch_rows(N.weight, pieces, QKV, D, weight)
    c.fetch(N.ao, N.oa, N.bias, N.q, N.kd, N.vd, N.lse, N.cosine, N.sine, N.h1a, N.ebd)
    late[...] = jnp.zeros(late.shape, F)
    residual = c[N.x2][...]
    scale = lax.rsqrt(jnp.mean(residual * residual, axis=1, keepdims=True) + eps)
    weighted = c[N.gh2][...] * c[N.gains][1:2, :]
    inner = jnp.mean(residual * weighted, axis=1, keepdims=True)
    gx2[...] = (
        c[N.cot][...].astype(F) + scale * weighted - residual * (scale * scale * scale) * inner
    )
    c.send(N.gx2)
    branch = gx2[...].astype(B)
    c.wait(N.eo)
    red = nt(branch, weight[D:, :]).astype(B)
    c.wait(N.weight)
    for block in range(3):
        at = slice(block * 384, (block + 1) * 384)
        go[:, at] = (nt(branch, weight[at, :]) + nn(red, c[N.ao][:, at])).astype(B)
    grow = functools.partial(put, late, LATE_OFF)
    oa = c[N.oa]
    grow(N.wr, line, tn(red, oa[:, :D]), 0)
    grow(N.oe, line, tn(oa[:, D:], branch), 0)
    gqkv, gk, gv = near[N.gqkv], near[N.gk], near[N.gv]
    q, kd, vd, lse, bias, cosine, sine = (
        c[k] for k in (N.q, N.kd, N.vd, N.lse, N.bias, N.cosine, N.sine)
    )
    masks = [mask.astype(B) for mask in half_masks()]
    wide_masks = half_masks()

    def turn_back(value, low_row, high_row):
        first = lax.broadcasted_iota(jnp.int32, value.shape, 1) % 64 < 32
        return (
            value * cosine[low_row:high_row, :]
            - swap_halves(value, first) * sine[low_row:high_row, :]
        )

    def tile(i, _):
        gk[...] = jnp.zeros(gk.shape, F)
        gv[...] = jnp.zeros(gv.shape, F)
        for t in range(3):
            at = pl.ds(pl.multiple_of((3 * i + t) * 128, 128), 128)
            for low_row, high_row, keys in BLOCKS:
                rows = high_row - low_row
                part = q[low_row:high_row, at]
                upstream = go[low_row:high_row, at]
                product = upstream.astype(F) * oa[low_row:high_row, at].astype(F)
                halves = []
                for half in range(2):
                    head = 2 * t + half
                    side = head // 3
                    group = pl.ds(pl.multiple_of((2 * i + side) * 128, 128), 128)
                    query = part * masks[half]
                    grad = upstream * masks[half]
                    scores = nt(query, kd[:keys, group]) + bias[low_row:high_row, :keys]
                    total = lse[i, t, low_row:high_row, half * 64 : half * 64 + 1]
                    probs = jnp.exp(scores - total)
                    inner = jnp.sum(product * wide_masks[half], axis=1, keepdims=True)
                    grad_probs = nt(grad, vd[:keys, group])
                    ds = (probs * (grad_probs - inner)).astype(B)
                    gv[side, :keys, :] += tn(probs.astype(B), grad)
                    gk[side, :keys, :] += tn(ds, query)
                    halves.append(nn(ds, kd[:keys, group]))
                low = lax.broadcasted_iota(jnp.int32, (rows, 128), 1) < 64
                value = jnp.where(low, halves[0], halves[1]) * HEAD_DIM**-0.5
                gqkv[low_row:high_row, at] = turn_back(value, low_row, high_row).astype(B)
        rows = gk.shape[1]
        low = lax.broadcasted_iota(jnp.int32, (rows, 128), 1) < 64

        def fold(ref):
            both = [ref[s] + pltpu.roll(ref[s], 64, 1) for s in range(2)]
            return jnp.where(low, both[0], both[1])

        at = pl.multiple_of(i * 128, 128)
        gqkv[:, pl.ds(D + at, 128)] = turn_back(fold(gk), 0, rows).astype(B)
        gqkv[:, pl.ds(D + KVW + at, 128)] = fold(gv).astype(B)
        return 0

    h1a, ebd = c[N.h1a], c[N.ebd]
    lax.fori_loop(0, 3, tile, 0)
    c.send(N.gqkv)
    red = nt(gqkv[...], ebd[...]).astype(B)
    near[N.gred][...] = red
    c.send(N.gred)
    value = tn(red, h1a[:, :D])
    grow(N.qr, line, value, 0)
    grow(N.kr, line, value, 16)
    grow(N.vr, line, value, 32)
    value = tn(h1a[:, D:], gqkv[...])
    grow(N.qe, line, value[:, :D], 0)
    grow(N.ke, line, value[:, D : D + KVW], 16)
    grow(N.ve, line, value[:, D + KVW :], 32)
    hand_out(late, near[N.late])
    c.send(N.late)


def finish_body(c, pieces):
    near = c.near
    weight, out = near[N.weight], near[N.out]
    c.fetch(N.x, N.gqkv, N.gred, N.acat, N.gains)
    c.fetch_rows(N.wq, pieces, 0, D, weight)
    c.fetch_rows(N.wkv, pieces, D, 2 * KVW, weight, to=D)
    c.fetch(N.gx2)
    source = c[N.x][...].astype(F)
    scale = lax.rsqrt(jnp.mean(source * source, axis=1, keepdims=True) + eps)
    inner = jnp.zeros((source.shape[0], 1), F)
    gqkv = c[N.gqkv]
    c.wait(N.wq)
    for block in range(3):
        at = slice(block * 384, (block + 1) * 384)
        out[:, at] = nt(gqkv[:, :D], weight[at, :D]) + nn(c[N.gred][...], c[N.acat][:, at])
    c.wait(N.wkv)
    for block in range(3):
        at = slice(block * 384, (block + 1) * 384)
        value = out[:, at] + nt(gqkv[:, D:], weight[at, D:])
        value = value * c[N.gains][0:1, at]
        out[:, at] = value
        inner += jnp.sum(value * c[N.x][:, at].astype(F), axis=1, keepdims=True)
    inner = inner / D
    out[...] = c[N.gx2][...] + scale * out[...] - source * (scale * scale * scale) * inner
    c.send(N.out)


def after(value, *earlier):
    return lax.optimization_barrier((value, earlier))[0]


def swap(value, bit, what):
    with jax.named_scope(what):
        return lax.ppermute(value, N.shard, [(i, i ^ bit) for i in range(PARTS)])


def halves_kernel(y, x, y_out, x_out, sems):
    copies = [
        pltpu.make_async_copy(y.at[:, pl.ds(0, HALF)], y_out, sems.at[0]),
        pltpu.make_async_copy(x.at[:, pl.ds(HALF, HALF)], x_out, sems.at[1]),
    ]
    for copy in copies:
        copy.start()
    for copy in copies:
        copy.wait()


class Gather:
    def __init__(self):
        self.held = {}
        self.last = None

    def links(self, n, message, *earlier):
        message = after(message, *earlier) if earlier else message
        self.held[n, 2] = swap(message, 2, "x%d" % n)
        self.held[n, 4] = swap(message, 4, "y%d" % n)

    def across(self, n, source, at, *earlier):
        value = self.held[source, at]
        value = after(value, *earlier) if earlier else value
        with jax.named_scope("z%d_%d" % (at, n)):
            pairs = [(i, i ^ 1) for i in range(lax.axis_size(N.rep))]
            self.held[n, at] = lax.ppermute(value, N.rep, pairs)

    def corner(self, n, *earlier):
        x, y = self.held[n, 2], self.held[n, 4]
        if earlier:
            x, y = after(x, *earlier), after(y, *earlier)
        y, x = call(
            halves_kernel,
            [((ROWS, HALF), B)] * 2,
            (y, x),
            spaces={0: pltpu.HBM, 1: pltpu.HBM},
            scratch=[pltpu.SemaphoreType.DMA((2,))],
            name=N.halves,
        )
        self.held[n, 6] = swap(y, 2, "dx%d" % n)
        self.held[n, 8] = swap(x, 4, "dy%d" % n)

    def core(self, n, at, *earlier):
        value = after(self.held[n, at], *earlier) if earlier else self.held[n, at]
        self.held[n, at + 1] = swap(value, 1, "c%d_%d" % (at, n))

    def blocks(self, n):
        return [self.held[n, at] for at in (0, 1, 2, 3, 4, 5, 6, 8, 7, 9)]


def exchange(grads):
    count = PARTS * QUARTERS
    lanes = grads.shape[3]
    received = lax.all_to_all(grads.reshape(count, RANK, lanes), (N.rep, N.shard), 0, 0)
    return received.reshape(count * RANK, lanes)


def add_up(received, trees, slots):
    return call(
        add_up_kernel,
        [((received.shape[1], ADAPTERS * RANK), B)],
        (trees, slots, received),
        spaces={0: pltpu.SMEM, 1: pltpu.SMEM},
        name=N.add_up,
    )[0]


def add_up_kernel(trees, slots, received, out):
    chosen = choose(trees, slots, 0, PARTS * QUARTERS)
    out[...] = tn(received[...], chosen).astype(B)


def share(quarter):
    return [quarter] + [
        lax.ppermute(quarter, N.rep, [(i, i ^ step) for i in range(QUARTERS)])
        for step in range(1, QUARTERS)
    ]


def deliver_kernel(names, offsets, rep, *refs):
    parts, outs, whole = refs[:QUARTERS], refs[QUARTERS:-1], refs[-1]
    rows = parts[0].shape[0]
    for step, part in enumerate(parts):
        at = pl.multiple_of((rep[0] ^ step) * rows, rows)
        whole[pl.ds(at, rows), :] = part[...].astype(F)
    for name, out in zip(names, outs):
        out[...] = whole[offsets[name] : offsets[name] + SEG_ROWS[name], :]


def on_device(*args):
    x, cot, gain_a, gain_h = args[:4]
    weights = args[4:11]
    adapters = args[11:25]
    parents, device_tree, tree_adapter = args[25:]
    count = lax.axis_size(N.shard)
    shard = lax.axis_index(N.shard)
    group = lax.axis_index(N.rep) * count
    rows = x.shape[0]
    direct = count == PARTS and lax.axis_size(N.rep) == QUARTERS

    if direct:
        parity = lax.axis_index(N.rep) % 2
        gather = Gather()
        held = gather.held
        facts = jnp.stack([group, parity]).astype(jnp.int32)
        held[1, 0], held[0, 0], sent = call(
            pack_first_kernel,
            [((ROWS, MSG), B), ((ROWS, MSG), B), ((PARTS * RANK, LANES), B)],
            (facts, device_tree, tree_adapter, *weights, gain_a[None], gain_h[None], *adapters),
            spaces={
                **{n: pltpu.SMEM for n in range(3)},
                **{n: pltpu.HBM for n in range(3, 10)},
            },
            scratch=[
                pltpu.VMEM((PARTS * RANK, LANES), F),
                pltpu.SemaphoreType.DMA((SLICE_COPIES + 4,)),
            ],
            name=N.pack_first,
        )
        held[2, 0], held[3, 0] = pack_slices((1 - parity, 2), weights[4:])
        pos = jnp.bitwise_xor(shard, jnp.arange(PARTS, dtype=jnp.int32))
        pos = jnp.concatenate([pos, jnp.full((PARTS,), parity)]).astype(jnp.int32)
        packed = lax.all_to_all(sent.reshape(PARTS, RANK, LANES), N.shard, 0, 0)
        gather.links(1, held[1, 0])
        gather.links(0, held[0, 0], packed)
        for n in range(4):
            gather.core(n, 0)
        early_on = [held[n, 1] for n in range(4)]
        for at in (2, 4):
            gather.across(2, 1, at, held[1, 2], held[1, 4], *early_on)
        gather.corner(0, held[0, 2], held[0, 4], held[2, 2])
    else:
        whole = [lax.all_gather(w, N.shard, axis=0, tiled=True) for w in weights]
        cut = lambda w, j: lax.slice_in_dim(
            w, j * (w.shape[0] // PARTS), (j + 1) * (w.shape[0] // PARTS)
        )
        attention = [pack_attention([cut(w, j) for w in whole[:4]]) for j in range(PARTS)]
        hidden = [
            pack_slices(range(SLICES), [cut(w, j) for w in whole[4:]]) for j in range(PARTS)
        ]
        blocks = [attention] + [[hidden[j][f] for j in range(PARTS)] for f in range(SLICES)]
        blocks = [
            [b[m][:, low:high] if high - low < MSG else b[m] for m, low, high in HELD]
            for b in blocks
        ]
        pos = jnp.arange(PARTS, dtype=jnp.int32)
        pos = jnp.concatenate([pos, jnp.zeros_like(pos)])
        offset = tree_adapter[device_tree[group + shard]] * RANK
        segments = {}
        for name, part in zip(NAMES, adapters):
            full = lax.all_gather(part, N.shard, axis=0, tiled=True)
            own = lax.dynamic_slice_in_dim(full, offset, RANK, 1)
            segments[name] = own.reshape(PARTS, -1, RANK).transpose(0, 2, 1)
        both = jnp.stack(
            [lax.all_gather(g, N.shard, axis=0, tiled=True) for g in (gain_a, gain_h)]
        )
        both = both.reshape(2, PARTS, ROWS).transpose(1, 0, 2)
        segments[N.gain] = jnp.pad(both, ((0, 0), (0, RANK - 2), (0, 0)))
        packed = jnp.concatenate([segments[name] for name in OFF], axis=2)
        packed = jnp.pad(packed, ((0, 0), (0, 0), (0, LANES - packed.shape[2])))

    allowed, positions = tree_layout(parents[0], rows)
    bias = jnp.where(allowed, 0.0, -1e30).astype(F)
    cosine, sine = rope_tables(positions)
    ready = launch(
        N.prepare,
        prepare_body,
        dict(
            acat=((128, D), B),
            ebd=((128, QKV), B),
            ao=((128, D), B),
            eo=((128, D), B),
            agu=((128, D), B),
            ed=((128, D), B),
            egu=((SLICES, 128, 2 * SL), B),
            ad=((SLICES, SL, 128), B),
            gains=((RANK, D), F),
            h1a=((rows, WIDE), B),
            cota=((rows, WIDE), B),
        ),
        dict(packed=packed, x=x, cot=cot),
        scratch=dict(line=((RANK, D), F), wide=((PARTS, RANK, LANES), F)),
    )
    if direct:
        gather.corner(1, held[0, 2], held[0, 4], held[2, 2], ready[N.h1a], bias, cosine, sine)
        for at in (2, 4):
            gather.core(0, at, ready[N.h1a], bias, cosine, sine)
        for at in (6, 8):
            gather.core(0, at)
        blocks = [gather.blocks(0)]
    tables = dict(bias=bias, cosine=cosine, sine=sine)
    some = lambda *names: {name: ready[name] for name in names}
    front = launch(
        N.project,
        project_body,
        dict(q=((rows, D), B), kd=((rows, 2 * KVW), B), vd=((rows, 2 * KVW), B)),
        dict(cosine=cosine, sine=sine, **some(N.h1a, N.ebd)),
        blocks[0],
        pos,
        scratch=dict(weight=((WIDE, QKV), B)),
    )
    if direct:
        ahead = [front[N.q], held[1, 6], held[1, 8], held[2, 4]]
        gather.links(3, held[3, 0], *ahead)
        for at in (6, 8):
            gather.across(2, 1, at, *ahead)
    front.update(
        launch(
            N.attend,
            attend_body,
            dict(
                oa=((rows, WIDE), B),
                lse=((3, 3, rows, 128), F),
                x2=((rows, D), F),
                h2a=((rows, WIDE), B),
            ),
            dict(x=x, bias=bias, **front, **some(N.ao, N.eo, N.agu, N.gains)),
            blocks[0],
            pos,
            scratch=dict(wout=((WIDE, D), B)),
        )
    )
    h2a, x2 = front[N.h2a], front[N.x2]
    if direct:
        both = [held[3, at] for at in (2, 4)]
        gather.corner(3, h2a, *both)
        for n in (1, 2):
            for at in (2, 4, 6, 8):
                gather.core(n, at, h2a, *both)
    state = None
    for slices in RUNS:
        first, last = slices[0] == 0, slices[-1] == SLICES - 1
        if direct:
            if last:
                for at in (2, 4, 6, 8):
                    gather.core(3, at, state[N.early])
            for f in slices:
                if len(blocks) < f + 2:
                    blocks.append(gather.blocks(1 + f))
        ins = dict(h2a=h2a, **some(N.cota, N.egu, N.ad))
        count = len(slices)
        scratch = dict(
            wgu=((count, WIDE, 2 * SL), B),
            wd=((count, SL, WIDE), B),
            tail=((count, PARTS * 16, SL), B),
            mid=((rows, SL), B),
            ggt=((rows, SL), B),
            gup=((rows, SL), B),
            line=((RANK, D), F),
        )
        outs = dict(
            y=((rows, WIDE), F), g=((rows, WIDE), F), early=((PARTS, RANK, EARLY_LANES), F)
        )
        if not first:
            ins.update(y_in=state[N.y], g_in=state[N.g], early_in=state[N.early])
        if last:
            ins.update(x2=x2, **some(N.agu, N.ed))
            scratch.update(y_acc=outs[N.y], g_acc=outs[N.g], early_acc=outs[N.early])
            outs = dict(
                y=((rows, D), B),
                g=((rows, D), F),
                early=((QUARTERS, PARTS, RANK, EARLY_LANES // QUARTERS), B),
            )
        state = launch(
            "hidden_%d" % slices[0],
            functools.partial(hidden_body, slices),
            outs,
            ins,
            [piece for f in slices for piece in blocks[1 + f]],
            pos,
            scratch,
            sems=64 + 80 * count,
        )
    layer_output, gh2, early = state[N.y], state[N.g], state[N.early]
    if direct:
        early_come = exchange(early)
    operands = dict(gh2=gh2, x2=x2, cot=cot, **tables, **some(N.ao, N.eo, N.gains, N.h1a, N.ebd))
    operands.update({name: front[name] for name in (N.q, N.kd, N.vd, N.oa, N.lse)})
    back = launch(
        N.back,
        back_body,
        dict(
            gx2=((rows, D), F),
            gqkv=((rows, QKV), B),
            gred=((rows, 128), B),
            late=((QUARTERS, PARTS, RANK, LATE_LANES // QUARTERS), B),
        ),
        operands,
        blocks[0],
        pos,
        dict(
            weight=((WIDE, D), B),
            go=((rows, D), B),
            gk=((2, rows, 128), F),
            gv=((2, rows, 128), F),
            line=((RANK, D), F),
            late_acc=((PARTS, RANK, LATE_LANES), F),
        ),
    )
    late = back[N.late]
    if direct:
        early_come, late = lax.optimization_barrier((early_come, late))
        late_come = exchange(late)
        early_parts = share(add_up(early_come, device_tree, tree_adapter))
        late_quarter = add_up(late_come, device_tree, tree_adapter)
    input_grad = launch(
        N.finish,
        finish_body,
        dict(out=((rows, D), F)),
        dict(
            x=x, gx2=back[N.gx2], gqkv=back[N.gqkv], gred=back[N.gred], **some(N.acat, N.gains)
        ),
        blocks[0],
        pos,
        dict(weight=((D, QKV), B)),
    )[N.out]
    owned = {}
    if direct:
        rep = lax.axis_index(N.rep).astype(jnp.int32).reshape(1)
        late_parts = share(late_quarter)
    for grads, names, offsets in ((early, EARLY, EARLY_OFF), (late, LATE, LATE_OFF)):
        if direct:
            parts = early_parts if names is EARLY else late_parts
            received = call(
                functools.partial(deliver_kernel, names, offsets),
                [((SEG_ROWS[name], ADAPTERS * RANK), F) for name in names],
                (rep, *parts),
                spaces={0: pltpu.SMEM},
                scratch=[pltpu.VMEM((QUARTERS * parts[0].shape[0], ADAPTERS * RANK), F)],
                name=N.deliver,
            )
            owned.update(zip(names, received))
        else:
            grads = grads.transpose(1, 2, 0, 3).reshape(PARTS, RANK, -1)
            for name in names:
                part = grads[:, :, offsets[name] : offsets[name] + SEG_ROWS[name]]
                part = part.transpose(0, 2, 1).reshape(-1, RANK)
                wide = lax.dynamic_update_slice_in_dim(
                    jnp.zeros((part.shape[0], ADAPTERS * RANK), B), part, offset, 1
                )
                wide = lax.psum_scatter(wide, N.shard, scatter_dimension=0, tiled=True)
                owned[name] = lax.psum(wide, N.rep).astype(F)
    return (layer_output, input_grad) + tuple(owned[name] for name in NAMES)


def solution(mesh):
    token = P((N.rep, N.shard), None)
    row = P(N.shard, None)
    return jax.shard_map(
        on_device,
        mesh=mesh,
        in_specs=(token, token, P(N.shard), P(N.shard)) + (row,) * 21 + (token, P(), P()),
        out_specs=(token, token) + (row,) * 14,
        check_vma=False,
    )
```

```python
import functools

import jax
import jax.numpy as jnp
from jax import lax
from jax.experimental import pallas as pl
from jax.experimental.pallas import tpu as pltpu
from jax.sharding import PartitionSpec as P

D = 1152
Q_HEADS = 18
KV_HEADS = 6
HEAD_DIM = 64
FF = 3072
RANK = 16
ADAPTERS = 8
TRUNK = 128
BRANCH = 24
LEAF = 24
KVW = 384
PARTS = 8
ROWS = D // PARTS
FROWS = FF // PARTS
SLICES = 3
SL = FF // SLICES
WIDE = D + 128
QKV = D + 2 * KVW
MSG = 3072
eps = 1e-05
F = jnp.float32
B = jnp.bfloat16


class Words:
    def __getattr__(self, word):
        return word


N = Words()
VMEM_LIMIT = 58 * 1024 * 1024

NAMES = (N.qr, N.qe, N.kr, N.ke, N.vr, N.ve, N.wr, N.oe, N.gr, N.ge, N.ur, N.ue, N.dr, N.de)
SEG_ROWS = {name: ROWS for name in NAMES}
SEG_ROWS.update(ke=KVW // PARTS, ve=KVW // PARTS, ge=FROWS, ue=FROWS, dr=FROWS)


SEG_ROWS[N.gain] = ROWS
EARLY = (N.ge, N.ue, N.dr, N.gr, N.ur, N.de)
LATE = (N.wr, N.oe, N.qr, N.qe, N.kr, N.ke, N.vr, N.ve)
QUARTERS = 4


def lay_out(names, unit):
    offsets = {}
    total = 0
    for name in names:
        offsets[name] = total
        total += SEG_ROWS[name]
    return offsets, -(-total // unit) * unit


EARLY_OFF, EARLY_LANES = lay_out(EARLY, QUARTERS * 128)
LATE_OFF, LATE_LANES = lay_out(LATE, QUARTERS * 128)
OFF, LANES = lay_out(EARLY + LATE + (N.gain,), 128)
BLOCKS = ((0, 128, 128), (128, 224, 256), (224, 416, 416))


def nn(left, right):
    return lax.dot_general(left, right, (((1,), (0,)), ((), ())), preferred_element_type=F)


def nt(left, right):
    return lax.dot_general(left, right, (((1,), (1,)), ((), ())), preferred_element_type=F)


def tn(left, right):
    return lax.dot_general(left, right, (((0,), (0,)), ((), ())), preferred_element_type=F)


RUNS = ((0, 1), (2,))
COST = dict(flops=1 << 20, bytes_accessed=1 << 16, transcendentals=0)


def call(kernel, out_shape, args, spaces=None, scratch=(), name=None):
    in_specs = [
        pl.BlockSpec(memory_space=(spaces or {}).get(i, pltpu.VMEM)) for i in range(len(args))
    ]
    return pl.pallas_call(
        kernel,
        out_shape=[jax.ShapeDtypeStruct(s, d) for s, d in out_shape],
        in_specs=in_specs,
        out_specs=[pl.BlockSpec(memory_space=pltpu.VMEM) for _ in out_shape],
        scratch_shapes=list(scratch),
        compiler_params=pltpu.CompilerParams(vmem_limit_bytes=VMEM_LIMIT),
        cost_estimate=pl.CostEstimate(**COST),
        name=name,
    )(*args)


class Frame:
    def __init__(self, pos, near, far, outs, sems):
        self.pos, self.near, self.far, self.outs, self.sems = pos, near, far, outs, sems
        self.used = 0
        self.coming = {}
        self.leaving = []

    def copy(self, source, target):
        moved = pltpu.make_async_copy(source, target, self.sems.at[self.used])
        self.used += 1
        moved.start()
        return moved

    def fetch(self, *names):
        for name in names:
            self.coming[name] = [self.copy(self.far[name], self.near[name])]

    def fetch_into(self, key, source, target):
        self.coming.setdefault(key, []).append(self.copy(source, target))

    def fetch_rows(self, key, pieces, low, lanes, target, rows=ROWS, start=0, to=0):
        for piece, (m, begin, end) in zip(pieces, HELD):
            a, b = max(low, begin), min(low + lanes, end)
            if a < b:
                self.fetch_into(
                    key,
                    piece.at[pl.ds(start, rows), pl.ds(a - begin, b - a)],
                    target.at[row_at(self.pos, m, rows), pl.ds(to + a - low, b - a)],
                )

    def wait(self, *keys):
        for key in keys:
            for moved in self.coming.pop(key, ()):
                moved.wait()

    def __getitem__(self, name):
        self.wait(name)
        return self.near[name]

    def send(self, name, at=None):
        near, far = self.near[name], self.outs[name]
        if at is not None:
            near, far = near.at[:, at], far.at[:, at]
        self.leaving.append(self.copy(near, far))

    def close(self):
        for moved in self.leaving:
            moved.wait()


def launch(
    name, body, outs, ins, pieces=(), pos=None, scratch=None, sems=64, weigh=None
):
    scratch = scratch or {}
    operands = ([] if pos is None else [pos]) + list(ins.values()) + list(pieces)

    def kernel(*refs):
        refs = list(refs)
        take = lambda count: [refs.pop(0) for _ in range(count)]
        where = None if pos is None else take(1)[0]
        far = dict(zip(ins, take(len(ins))))
        parts = take(len(pieces))
        results = dict(zip(outs, take(len(outs))))
        near = dict(zip(ins, take(len(ins))))
        near.update(zip(outs, take(len(outs))))
        near.update(zip(scratch, take(len(scratch))))
        frame = Frame(where, near, far, results, refs[0])
        body(frame, parts)
        frame.close()

    hbm = pl.BlockSpec(memory_space=pltpu.HBM)
    specs = [hbm] * (len(ins) + len(pieces))
    if pos is not None:
        specs = [pl.BlockSpec(memory_space=pltpu.SMEM)] + specs
    results = pl.pallas_call(
        kernel,
        out_shape=[jax.ShapeDtypeStruct(s, d) for s, d in outs.values()],
        in_specs=specs,
        out_specs=[hbm] * len(outs),
        scratch_shapes=[pltpu.VMEM(v.shape, v.dtype) for v in ins.values()]
        + [pltpu.VMEM(s, d) for s, d in outs.values()]
        + [pltpu.VMEM(s, d) for s, d in scratch.values()]
        + [pltpu.SemaphoreType.DMA((sems,))],
        compiler_params=pltpu.CompilerParams(vmem_limit_bytes=VMEM_LIMIT),
        cost_estimate=pl.CostEstimate(**(weigh or COST)),
        name=name,
    )(*operands)
    return dict(zip(outs, results))


def tree_layout(parents_row, row_count):
    index = jnp.arange(row_count, dtype=jnp.int32)
    after = index - TRUNK
    leaf_start = TRUNK + 4 * BRANCH
    in_branch = (index >= TRUNK) & (index < leaf_start)
    in_leaf = index >= leaf_start
    segment = jnp.where(
        in_leaf, 5 + (index - leaf_start) // LEAF, jnp.where(in_branch, 1 + after // BRANCH, 0)
    )
    positions = jnp.where(
        in_leaf,
        TRUNK + BRANCH + (index - leaf_start) % LEAF,
        jnp.where(in_branch, TRUNK + after % BRANCH, index),
    )
    numbers = jnp.arange(13, dtype=jnp.int32)
    parent = jnp.sum(
        jnp.where(segment[:, None] == numbers[None, :], parents_row[None, :], 0), axis=1
    )
    grand = jnp.sum(jnp.where(parent[:, None] == numbers[None, :], parents_row[None, :], 0), axis=1)
    same = (segment[:, None] == segment[None, :]) & (index[None, :] <= index[:, None])
    above = (segment[:, None] != 0) & (
        (segment[None, :] == parent[:, None]) | (segment[None, :] == grand[:, None])
    )
    return (same | above, positions)


def rope_tables(positions):
    halfway = HEAD_DIM // 2
    frequency = 10000.0 ** (-jnp.arange(halfway, dtype=F) / halfway)
    angles = positions.astype(F)[:, None] * frequency[None, :]
    cosine, sine = jnp.cos(angles), jnp.sin(angles)
    return (
        jnp.concatenate([cosine] * 4, axis=1),
        jnp.concatenate([-sine, sine, -sine, sine], axis=1),
    )


def attention_copies(weights, out):
    copies = []
    at = 0
    for weight in weights:
        copies.append((weight, out.at[:, pl.ds(at, weight.shape[1])]))
        at += weight.shape[1]
    return copies


def slice_copies(f, g, u, d, out):
    at = pl.multiple_of(f * 128, 128)
    copies = []
    for s in range(PARTS):
        lanes = pl.ds(pl.multiple_of(s * FROWS + at, 128), 128)
        copies.append((g.at[:, lanes], out.at[:, pl.ds(s * 128, 128)]))
        copies.append((u.at[:, lanes], out.at[:, pl.ds(SL + s * 128, 128)]))
    copies.append(
        (d.at[pl.ds(at, 128), pl.ds(0, SL)], out.at[pl.ds(0, 128), pl.ds(2 * SL, SL)])
    )
    for b in range(8):
        rows = pl.ds(pl.multiple_of(at + b * 16, 16), 16)
        copies.append(
            (
                d.at[rows, pl.ds(SL, 128)],
                out.at[pl.ds(128, 16), pl.ds(2 * SL + b * 128, 128)],
            )
        )
    return copies


def start_all(copies, sems, first=0):
    moved = [
        pltpu.make_async_copy(source, target, sems.at[first + k])
        for k, (source, target) in enumerate(copies)
    ]
    for copy in moved:
        copy.start()
    return moved


SLICE_COPIES = 2 * PARTS + 9


def pack_attention_kernel(q, k, v, o, out, sems):
    for copy in start_all(attention_copies((q, k, v, o), out), sems):
        copy.wait()


def pack_slices_kernel(numbers, g, u, d, *refs):
    outs, sems = refs[:-1], refs[-1]
    moved = []
    for n, out in enumerate(outs):
        moved += start_all(slice_copies(numbers[n], g, u, d, out), sems, n * SLICE_COPIES)
    for copy in moved:
        copy.wait()


def pack_attention(weights):
    return call(
        pack_attention_kernel,
        [((ROWS, MSG), B)],
        weights,
        spaces={n: pltpu.HBM for n in range(4)},
        scratch=[pltpu.SemaphoreType.DMA((4,))],
        name=N.pack_attention,
    )[0]


def pack_slices(numbers, weights):
    numbers = jnp.stack([jnp.asarray(f, jnp.int32) for f in numbers])
    return call(
        pack_slices_kernel,
        [((ROWS, MSG), B)] * numbers.shape[0],
        (numbers, *weights),
        spaces={0: pltpu.SMEM, 1: pltpu.HBM, 2: pltpu.HBM, 3: pltpu.HBM},
        scratch=[pltpu.SemaphoreType.DMA((numbers.shape[0] * SLICE_COPIES,))],
        name=N.pack_slices,
    )


def choose(trees, slots, first, count):
    column = lax.broadcasted_iota(jnp.int32, (RANK, ADAPTERS * RANK), 1)
    row = lax.broadcasted_iota(jnp.int32, (RANK, ADAPTERS * RANK), 0)
    parts = [
        jnp.where(column == slots[trees[first + d]] * RANK + row, 1.0, 0.0) for d in range(count)
    ]
    return jnp.concatenate(parts, axis=0).astype(B)


def pack_first_kernel(facts, trees, slots, *refs):
    weights, gains, parts = refs[:7], refs[7:9], refs[9:23]
    first, attention, out, wide, sems = refs[23:]
    moved = start_all(slice_copies(facts[1], *weights[4:], first), sems)
    moved += start_all(attention_copies(weights[:4], attention), sems, SLICE_COPIES)
    chosen = choose(trees, slots, facts[0], PARTS)
    for name, part in zip(NAMES, parts):
        wide[:, OFF[name] : OFF[name] + SEG_ROWS[name]] = nt(chosen, part[...])
    row = lax.broadcasted_iota(jnp.int32, (RANK, ROWS), 0)
    both = jnp.where(
        row == 0,
        gains[0][...].astype(F).reshape(1, ROWS),
        jnp.where(row == 1, gains[1][...].astype(F).reshape(1, ROWS), 0.0),
    )
    for d in range(PARTS):
        wide[d * RANK : (d + 1) * RANK, OFF[N.gain] : OFF[N.gain] + ROWS] = both
    out[...] = wide[...].astype(B)
    for copy in moved:
        copy.wait()


HALF = MSG // 2
HELD = [(m, 0, MSG) for m in range(6)] + [
    (m, low, low + HALF) for m in (6, 7) for low in (0, HALF)
]
HELD_COUNT = len(HELD)


def row_at(pos, m, rows):
    return pl.ds(pl.multiple_of(pos[m] * rows, rows), rows)


def swap_halves(value, first):
    return jnp.where(first, pltpu.roll(value, 96, 1), pltpu.roll(value, 32, 1))


def half_masks():
    lane = lax.broadcasted_iota(jnp.int32, (1, 128), 1)
    low = jnp.where(lane < 64, 1.0, 0.0)
    return low, 1.0 - low


def prepare_body(c, _):
    c.fetch(N.x, N.cot, N.packed)
    near = c.near
    for name in (N.acat, N.ebd, N.ao, N.eo, N.agu, N.ed, N.egu):
        near[name][...] = jnp.zeros(near[name].shape, B)
    source = c[N.x][...].astype(F)
    scale = lax.rsqrt(jnp.mean(source * source, axis=1, keepdims=True) + eps)
    wide = near[N.wide]
    wide[...] = c[N.packed][...].astype(F)
    line = near[N.line]

    def rows_of(name, width=None, start=0):
        rows = SEG_ROWS[name] if width is None else width
        low = OFF[name] + start
        for j in range(PARTS):
            line[:, j * rows : (j + 1) * rows] = wide[j, :, low : low + rows]
        return line[:, : PARTS * rows]

    near[N.gains][...] = rows_of(N.gain)
    acat = near[N.acat]
    acat[:16, :] = rows_of(N.qr).astype(B)
    acat[16:32, :] = rows_of(N.kr).astype(B)
    acat[32:48, :] = rows_of(N.vr).astype(B)
    near[N.ed][:16, :] = rows_of(N.de).astype(B)
    h1 = (source * scale * near[N.gains][0:1, :]).astype(B)
    near[N.h1a][:, :D] = h1
    near[N.h1a][:, D:] = nt(h1, acat[...]).astype(B)
    near[N.cota][:, :D] = c[N.cot][...]
    near[N.cota][:, D:] = nt(c[N.cot][...], near[N.ed][...]).astype(B)
    ebd, agu, egu = near[N.ebd], near[N.agu], near[N.egu]
    ebd[:16, :D] = rows_of(N.qe).astype(B)
    ebd[16:32, D : D + KVW] = rows_of(N.ke).astype(B)
    ebd[32:48, D + KVW :] = rows_of(N.ve).astype(B)
    for name in (N.h1a, N.cota, N.acat, N.ebd, N.gains, N.ed):
        c.send(name)
    near[N.ao][:16, :] = rows_of(N.wr).astype(B)
    near[N.eo][:16, :] = rows_of(N.oe).astype(B)
    agu[:16, :] = rows_of(N.gr).astype(B)
    agu[16:32, :] = rows_of(N.ur).astype(B)
    for name in (N.ao, N.eo, N.agu):
        c.send(name)
    for f in range(SLICES):
        egu[f, :16, :SL] = rows_of(N.ge, 128, f * 128).astype(B)
        egu[f, 16:32, SL:] = rows_of(N.ue, 128, f * 128).astype(B)
        down = rows_of(N.dr, 128, f * 128)
        near[N.ad][f] = jnp.concatenate([down, jnp.zeros((112, SL), F)], axis=0).T.astype(B)
    c.send(N.egu)
    c.send(N.ad)


def project_body(c, pieces):
    near = c.near
    weight = near[N.weight]
    c.fetch(N.h1a)
    c.fetch_rows(N.w0, pieces, 0, 768, weight)
    c.fetch_into(N.w0, c.far[N.ebd], weight.at[pl.ds(D, 128), :])
    c.fetch(N.cosine, N.sine)
    c.fetch_rows(N.w1, pieces, 768, QKV - 768, weight, to=768)
    h1a = c[N.h1a]
    rows = h1a.shape[0]
    lane = lax.broadcasted_iota(jnp.int32, (rows, 128), 1)
    low, first = lane < 64, lane % 64 < 32
    q, kd, vd = near[N.q], near[N.kd], near[N.vd]
    c.wait(N.w0)
    for block in range(5):
        if block == 2:
            c.wait(N.w1)
        value = nn(h1a[...], weight[:, block * 384 : (block + 1) * 384])
        for t in range(3):
            part = value[:, t * 128 : (t + 1) * 128]
            if block < 4:
                part = part * c[N.cosine][...] + swap_halves(part, first) * c[N.sine][...]
            if block < 3:
                at = block * 384 + t * 128
                q[:, at : at + 128] = (part * HEAD_DIM**-0.5).astype(B)
            else:
                out = kd if block == 3 else vd
                rolled = pltpu.roll(part, 64, 1)
                out[:, t * 256 : t * 256 + 128] = jnp.where(low, part, rolled).astype(B)
                out[:, t * 256 + 128 : (t + 1) * 256] = jnp.where(low, rolled, part).astype(B)
    for name in (N.q, N.kd, N.vd):
        c.send(name)


def attend_body(c, pieces):
    near = c.near
    wout = near[N.wout]
    c.fetch(N.q, N.kd, N.bias, N.vd)
    c.fetch_rows(N.wout, pieces, QKV, D, wout)
    c.fetch_into(N.wout, c.far[N.eo], wout.at[pl.ds(D, 128), :])
    c.fetch(N.x, N.ao, N.agu, N.gains)
    q, kd, vd = c[N.q], c[N.kd], c[N.vd]
    rows = q.shape[0]
    masks = [mask.astype(B) for mask in half_masks()]
    bias, oa, lse, x2, h2a = c[N.bias], near[N.oa], near[N.lse], near[N.x2], near[N.h2a]

    def tile(i, _):
        lanes = [pl.ds(pl.multiple_of((3 * i + t) * 128, 128), 128) for t in range(3)]
        outs = {}
        for side in range(2):
            group = pl.ds(pl.multiple_of((2 * i + side) * 128, 128), 128)
            values = vd[:, group] * masks[0] + masks[1]
            for block, (low_row, high_row, keys) in enumerate(BLOCKS):
                count = high_row - low_row
                heads = [divmod(3 * side + slot, 2) for slot in range(3)]
                query = jnp.concatenate(
                    [q[low_row:high_row, lanes[t]] * masks[half] for t, half in heads], axis=0
                )
                scores = nt(query, kd[:keys, group]).reshape(3, count, keys)
                scores = (scores + bias[low_row:high_row, :keys][None]).reshape(3 * count, keys)
                top = jnp.max(scores, axis=1, keepdims=True)
                result = nn(jnp.exp(scores - top).astype(B), values[:keys])
                summed = result[:, 64:65]
                result = result * (1.0 / summed)
                total = top + jnp.log(summed)
                lane = lax.broadcasted_iota(jnp.int32, (count, 128), 1)
                split = lambda v, slot: v[slot * count : (slot + 1) * count]
                lse[i, side, low_row:high_row, :] = jnp.where(
                    lane == 0,
                    split(total, 0),
                    jnp.where(lane == 1, split(total, 1), split(total, 2)),
                )
                for slot in range(3):
                    outs[block, 3 * side + slot] = split(result, slot)
        for block, (low_row, high_row, _) in enumerate(BLOCKS):
            lane = lax.broadcasted_iota(jnp.int32, (high_row - low_row, 128), 1)
            for t in range(3):
                oa[low_row:high_row, lanes[t]] = jnp.where(
                    lane < 64, outs[block, 2 * t], pltpu.roll(outs[block, 2 * t + 1], 64, 1)
                ).astype(B)
        return 0

    lax.fori_loop(0, 3, tile, 0)
    c.send(N.lse)
    oa[:, D:] = nt(oa[:, :D], c[N.ao][...]).astype(B)
    c.send(N.oa)
    c.wait(N.wout)
    square = jnp.zeros((rows, 1), F)
    for block in range(3):
        at = slice(block * 384, (block + 1) * 384)
        value = c[N.x][:, at].astype(F) + nn(oa[...], wout[:, at])
        x2[:, at] = value
        square += jnp.sum(value * value, axis=1, keepdims=True)
    c.send(N.x2)
    scale = lax.rsqrt(square / D + eps)
    h2a[:, :D] = (x2[...] * scale * c[N.gains][1:2, :]).astype(B)
    h2a[:, D:] = nt(h2a[:, :D], c[N.agu][...]).astype(B)
    c.send(N.h2a)


def put(grads, offsets, name, line, value, row, width=None, start=0):
    width = SEG_ROWS[name] if width is None else width
    line[:, : PARTS * width] = value[row : row + RANK, :]
    for j in range(PARTS):
        at = pl.ds(offsets[name] + start, width)
        if not isinstance(start, int):
            at = pl.ds(pl.multiple_of(offsets[name] + start, 128), width)
        grads[j, :, at] = line[:, j * width : (j + 1) * width]


def hand_out(grads, out):
    part = out.shape[3]
    for q in range(QUARTERS):
        out[q] = grads[:, :, q * part : (q + 1) * part].astype(B)


def hidden_body(slices, c, pieces):
    first, last = slices[0] == 0, slices[-1] == SLICES - 1
    near = c.near
    mid, ggt, gup, line = near[N.mid], near[N.ggt], near[N.gup], near[N.line]
    c.fetch(N.h2a)
    number = [c.pos[PARTS], 1 - c.pos[PARTS]] if first else slices
    for n, f in enumerate(slices):
        wgu, wd, tail = near[N.wgu].at[n], near[N.wd].at[n], near[N.tail].at[n]
        own = pieces[n * HELD_COUNT : (n + 1) * HELD_COUNT]
        for part in range(2):
            for side in range(2):
                at = side * SL + part * 512
                c.fetch_rows((N.gu, f, part), own, at, 512, wgu, to=at)
            if part == 0:
                c.fetch_into((N.gu, f, 0), c.far[N.egu].at[number[n]], wgu.at[pl.ds(D, 128), :])
                if n == 0:
                    c.fetch(N.cota)
                c.fetch_rows((N.wd, f), own, 2 * SL, SL, wd, 128)
                c.fetch_rows((N.wd, f), own, 2 * SL, SL, tail, 16, 128)
                c.fetch_into((N.wd, f), c.far[N.ad].at[number[n]], wd.at[:, pl.ds(D, 128)])
    if not first:
        c.fetch(N.y_in, N.g_in, N.early_in)
    if last:
        c.fetch(N.x2, N.agu, N.ed)
    h2a = c[N.h2a]
    y_acc, g_acc = (near[N.y_acc], near[N.g_acc]) if last else (near[N.y], near[N.g])
    early = near[N.early_acc] if last else near[N.early]
    grow = functools.partial(put, early, EARLY_OFF)
    lanes = slice(D, WIDE)
    for n, f in enumerate(slices):
        wgu, wd, tail = near[N.wgu].at[n], near[N.wd].at[n], near[N.tail].at[n]
        for k in range(SL // 256):
            at = slice(k * 256, (k + 1) * 256)
            if k % 2 == 0:
                c.wait((N.gu, f, k // 2))
            gate = nn(h2a[...], wgu[:, at])
            up = nn(h2a[...], wgu[:, SL + k * 256 : SL + (k + 1) * 256])
            sig = jax.nn.sigmoid(gate)
            silu = gate * sig
            if k == 0:
                cota = c[N.cota]
                c.wait((N.wd, f))
                for m in range(PARTS):
                    for b in range(8):
                        wd[m * 128 + b * 16 : m * 128 + (b + 1) * 16, SL:D] = tail[
                            m * 16 : (m + 1) * 16, b * 128 : (b + 1) * 128
                        ]
            gmid = nt(cota[...], wd[at, :])
            mid[:, at] = (silu * up).astype(B)
            ggt[:, at] = (gmid * up * sig * (1.0 + gate * (1.0 - sig))).astype(B)
            gup[:, at] = (gmid * silu).astype(B)
        for k in range(5):
            at = slice(k * 256, (k + 1) * 256)
            value = nn(mid[...], wd[:, at])
            if n:
                value += y_acc[:, at]
            elif not first:
                value += c[N.y_in][:, at]
            y_acc[:, at] = value
            value = nt(ggt[...], wgu[at, :SL]) + nt(gup[...], wgu[at, SL:])
            if n:
                value += g_acc[:, at]
            elif not first:
                value += c[N.g_in][:, at]
            g_acc[:, at] = value
            if not last and n == len(slices) - 1:
                c.send(N.y, at)
                c.send(N.g, at)
        if n == 0:
            early[...] = jnp.zeros(early.shape, F) if first else c[N.early_in][...]
        grow(N.ge, line, tn(h2a[:, lanes], ggt[...]), 0, 128, number[n] * 128)
        grow(N.ue, line, tn(h2a[:, lanes], gup[...]), 16, 128, number[n] * 128)
        grow(N.dr, line, tn(cota[:, lanes], mid[...]), 0, 128, number[n] * 128)
    if last:
        red = g_acc[:, lanes].astype(B)
        near[N.g][...] = g_acc[:, :D] + nn(red, c[N.agu][...])
        c.send(N.g)
        down_red = y_acc[:, lanes].astype(B)
        grow(N.de, line, tn(down_red, cota[:, :D]), 0)
        value = tn(red, h2a[:, :D])
        grow(N.gr, line, value, 0)
        grow(N.ur, line, value, 16)
        hand_out(early, near[N.early])
        c.send(N.early)
        near[N.y][...] = (y_acc[:, :D] + c[N.x2][...] + nn(down_red, c[N.ed][...])).astype(B)
        c.send(N.y)
    else:
        c.send(N.early)


def back_body(c, pieces):
    near, far = c.near, c.far
    c.fetch(N.gh2, N.x2, N.gains, N.cot)
    weight, gx2, go, late, line = (near[k] for k in (N.weight, N.gx2, N.go, N.late_acc, N.line))
    c.fetch_into(N.eo, far[N.eo], weight.at[pl.ds(D, 128), :])
    c.fetch_rows(N.weight, pieces, QKV, D, weight)
    c.fetch(N.ao, N.oa, N.bias, N.q, N.kd, N.vd, N.lse, N.cosine, N.sine, N.h1a, N.ebd)
    late[...] = jnp.zeros(late.shape, F)
    residual = c[N.x2][...]
    scale = lax.rsqrt(jnp.mean(residual * residual, axis=1, keepdims=True) + eps)
    weighted = c[N.gh2][...] * c[N.gains][1:2, :]
    inner = jnp.mean(residual * weighted, axis=1, keepdims=True)
    gx2[...] = (
        c[N.cot][...].astype(F) + scale * weighted - residual * (scale * scale * scale) * inner
    )
    c.send(N.gx2)
    branch = gx2[...].astype(B)
    c.wait(N.eo)
    red = nt(branch, weight[D:, :]).astype(B)
    c.wait(N.weight)
    for block in range(3):
        at = slice(block * 384, (block + 1) * 384)
        go[:, at] = (nt(branch, weight[at, :]) + nn(red, c[N.ao][:, at])).astype(B)
    grow = functools.partial(put, late, LATE_OFF)
    oa = c[N.oa]
    grow(N.wr, line, tn(red, oa[:, :D]), 0)
    grow(N.oe, line, tn(oa[:, D:], branch), 0)
    gqkv, gk, gv = near[N.gqkv], near[N.gk], near[N.gv]
    q, kd, vd, lse, bias, cosine, sine = (
        c[k] for k in (N.q, N.kd, N.vd, N.lse, N.bias, N.cosine, N.sine)
    )
    masks = [mask.astype(B) for mask in half_masks()]
    wide_masks = half_masks()

    def turn_back(value, low_row, high_row):
        first = lax.broadcasted_iota(jnp.int32, value.shape, 1) % 64 < 32
        return (
            value * cosine[low_row:high_row, :]
            - swap_halves(value, first) * sine[low_row:high_row, :]
        )

    def tile(i, _):
        gk[...] = jnp.zeros(gk.shape, F)
        gv[...] = jnp.zeros(gv.shape, F)
        lanes = [pl.ds(pl.multiple_of((3 * i + t) * 128, 128), 128) for t in range(3)]
        outs = {}
        for side in range(2):
            group = pl.ds(pl.multiple_of((2 * i + side) * 128, 128), 128)
            for block, (low_row, high_row, keys) in enumerate(BLOCKS):
                count = high_row - low_row
                query, grad, inner, total = [], [], [], []
                for slot in range(3):
                    t, half = divmod(3 * side + slot, 2)
                    upstream = go[low_row:high_row, lanes[t]]
                    product = upstream.astype(F) * oa[low_row:high_row, lanes[t]].astype(F)
                    query.append(q[low_row:high_row, lanes[t]] * masks[half])
                    grad.append(upstream * masks[half])
                    inner.append(jnp.sum(product * wide_masks[half], axis=1, keepdims=True))
                    total.append(lse[i, side, low_row:high_row, slot : slot + 1])
                query, grad, inner, total = (
                    jnp.concatenate(v, axis=0) for v in (query, grad, inner, total)
                )
                scores = nt(query, kd[:keys, group]).reshape(3, count, keys)
                scores = (scores + bias[low_row:high_row, :keys][None]).reshape(3 * count, keys)
                probs = jnp.exp(scores - total)
                grad_probs = nt(grad, vd[:keys, group])
                ds = (probs * (grad_probs - inner)).astype(B)
                gv[side, :keys, :] += tn(probs.astype(B), grad)
                gk[side, :keys, :] += tn(ds, query)
                result = nn(ds, kd[:keys, group])
                for slot in range(3):
                    outs[block, 3 * side + slot] = result[slot * count : (slot + 1) * count]
        for block, (low_row, high_row, _) in enumerate(BLOCKS):
            low = lax.broadcasted_iota(jnp.int32, (high_row - low_row, 128), 1) < 64
            for t in range(3):
                value = jnp.where(low, outs[block, 2 * t], outs[block, 2 * t + 1])
                gqkv[low_row:high_row, lanes[t]] = turn_back(
                    value * HEAD_DIM**-0.5, low_row, high_row
                ).astype(B)
        rows = gk.shape[1]
        low = lax.broadcasted_iota(jnp.int32, (rows, 128), 1) < 64

        def fold(ref):
            both = [ref[s] + pltpu.roll(ref[s], 64, 1) for s in range(2)]
            return jnp.where(low, both[0], both[1])

        at = pl.multiple_of(i * 128, 128)
        gqkv[:, pl.ds(D + at, 128)] = turn_back(fold(gk), 0, rows).astype(B)
        gqkv[:, pl.ds(D + KVW + at, 128)] = fold(gv).astype(B)
        return 0

    h1a, ebd = c[N.h1a], c[N.ebd]
    lax.fori_loop(0, 3, tile, 0)
    c.send(N.gqkv)
    red = nt(gqkv[...], ebd[...]).astype(B)
    near[N.gred][...] = red
    c.send(N.gred)
    value = tn(red, h1a[:, :D])
    grow(N.qr, line, value, 0)
    grow(N.kr, line, value, 16)
    grow(N.vr, line, value, 32)
    value = tn(h1a[:, D:], gqkv[...])
    grow(N.qe, line, value[:, :D], 0)
    grow(N.ke, line, value[:, D : D + KVW], 16)
    grow(N.ve, line, value[:, D + KVW :], 32)
    hand_out(late, near[N.late])
    c.send(N.late)


def finish_body(c, pieces):
    near = c.near
    weight, out = near[N.weight], near[N.out]
    c.fetch(N.x, N.gqkv, N.gred, N.acat, N.gains)
    c.fetch_rows(N.wq, pieces, 0, D, weight)
    c.fetch_rows(N.wkv, pieces, D, 2 * KVW, weight, to=D)
    c.fetch(N.gx2)
    source = c[N.x][...].astype(F)
    scale = lax.rsqrt(jnp.mean(source * source, axis=1, keepdims=True) + eps)
    inner = jnp.zeros((source.shape[0], 1), F)
    gqkv = c[N.gqkv]
    c.wait(N.wq)
    for block in range(3):
        at = slice(block * 384, (block + 1) * 384)
        out[:, at] = nt(gqkv[:, :D], weight[at, :D]) + nn(c[N.gred][...], c[N.acat][:, at])
    c.wait(N.wkv)
    for block in range(3):
        at = slice(block * 384, (block + 1) * 384)
        value = out[:, at] + nt(gqkv[:, D:], weight[at, D:])
        value = value * c[N.gains][0:1, at]
        out[:, at] = value
        inner += jnp.sum(value * c[N.x][:, at].astype(F), axis=1, keepdims=True)
    inner = inner / D
    out[...] = c[N.gx2][...] + scale * out[...] - source * (scale * scale * scale) * inner
    c.send(N.out)


def after(value, *earlier):
    return lax.optimization_barrier((value, earlier))[0]


def swap(value, bit, what):
    with jax.named_scope(what):
        return lax.ppermute(value, N.shard, [(i, i ^ bit) for i in range(PARTS)])


def halves_kernel(y, x, y_out, x_out, sems):
    copies = [
        pltpu.make_async_copy(y.at[:, pl.ds(0, HALF)], y_out, sems.at[0]),
        pltpu.make_async_copy(x.at[:, pl.ds(HALF, HALF)], x_out, sems.at[1]),
    ]
    for copy in copies:
        copy.start()
    for copy in copies:
        copy.wait()


class Gather:
    def __init__(self):
        self.held = {}
        self.last = None

    def links(self, n, message, *earlier):
        message = after(message, *earlier) if earlier else message
        self.held[n, 2] = swap(message, 2, "x%d" % n)
        self.held[n, 4] = swap(message, 4, "y%d" % n)

    def across(self, n, source, at, *earlier):
        value = self.held[source, at]
        value = after(value, *earlier) if earlier else value
        with jax.named_scope("z%d_%d" % (at, n)):
            pairs = [(i, i ^ 1) for i in range(lax.axis_size(N.rep))]
            self.held[n, at] = lax.ppermute(value, N.rep, pairs)

    def corner(self, n, *earlier):
        x, y = self.held[n, 2], self.held[n, 4]
        if earlier:
            x, y = after(x, *earlier), after(y, *earlier)
        y, x = call(
            halves_kernel,
            [((ROWS, HALF), B)] * 2,
            (y, x),
            spaces={0: pltpu.HBM, 1: pltpu.HBM},
            scratch=[pltpu.SemaphoreType.DMA((2,))],
            name=N.halves,
        )
        self.held[n, 6] = swap(y, 2, "dx%d" % n)
        self.held[n, 8] = swap(x, 4, "dy%d" % n)

    def core(self, n, at, *earlier):
        value = after(self.held[n, at], *earlier) if earlier else self.held[n, at]
        self.held[n, at + 1] = swap(value, 1, "c%d_%d" % (at, n))

    def blocks(self, n):
        return [self.held[n, at] for at in (0, 1, 2, 3, 4, 5, 6, 8, 7, 9)]


def exchange(grads):
    count = PARTS * QUARTERS
    lanes = grads.shape[3]
    received = lax.all_to_all(grads.reshape(count, RANK, lanes), (N.rep, N.shard), 0, 0)
    return received.reshape(count * RANK, lanes)


def add_up(received, trees, slots):
    return call(
        add_up_kernel,
        [((received.shape[1], ADAPTERS * RANK), B)],
        (trees, slots, received),
        spaces={0: pltpu.SMEM, 1: pltpu.SMEM},
        name=N.add_up,
    )[0]


def add_up_kernel(trees, slots, received, out):
    chosen = choose(trees, slots, 0, PARTS * QUARTERS)
    out[...] = tn(received[...], chosen).astype(B)


def share(quarter):
    return [quarter] + [
        lax.ppermute(quarter, N.rep, [(i, i ^ step) for i in range(QUARTERS)])
        for step in range(1, QUARTERS)
    ]


def deliver_kernel(names, offsets, rep, *refs):
    parts, outs, whole = refs[:QUARTERS], refs[QUARTERS:-1], refs[-1]
    rows = parts[0].shape[0]
    for step, part in enumerate(parts):
        at = pl.multiple_of((rep[0] ^ step) * rows, rows)
        whole[pl.ds(at, rows), :] = part[...].astype(F)
    for name, out in zip(names, outs):
        out[...] = whole[offsets[name] : offsets[name] + SEG_ROWS[name], :]


def on_device(*args):
    x, cot, gain_a, gain_h = args[:4]
    weights = args[4:11]
    adapters = args[11:25]
    parents, device_tree, tree_adapter = args[25:]
    count = lax.axis_size(N.shard)
    shard = lax.axis_index(N.shard)
    group = lax.axis_index(N.rep) * count
    rows = x.shape[0]
    direct = count == PARTS and lax.axis_size(N.rep) == QUARTERS

    if direct:
        parity = lax.axis_index(N.rep) % 2
        gather = Gather()
        held = gather.held
        facts = jnp.stack([group, parity]).astype(jnp.int32)
        held[1, 0], held[0, 0], sent = call(
            pack_first_kernel,
            [((ROWS, MSG), B), ((ROWS, MSG), B), ((PARTS * RANK, LANES), B)],
            (facts, device_tree, tree_adapter, *weights, gain_a, gain_h, *adapters),
            spaces={
                **{n: pltpu.SMEM for n in range(3)},
                **{n: pltpu.HBM for n in range(3, 10)},
            },
            scratch=[
                pltpu.VMEM((PARTS * RANK, LANES), F),
                pltpu.SemaphoreType.DMA((SLICE_COPIES + 4,)),
            ],
            name=N.pack_first,
        )
        held[2, 0], held[3, 0] = pack_slices((1 - parity, 2), weights[4:])
        pos = jnp.bitwise_xor(shard, jnp.arange(PARTS, dtype=jnp.int32))
        pos = jnp.concatenate([pos, jnp.full((PARTS,), parity)]).astype(jnp.int32)
        packed = lax.all_to_all(sent.reshape(PARTS, RANK, LANES), N.shard, 0, 0)
        gather.links(1, held[1, 0])
        gather.links(0, held[0, 0])
        for n in range(4):
            gather.core(n, 0)
        early_on = [held[n, 1] for n in range(4)]
        for at in (2, 4):
            gather.across(2, 1, at, held[1, 2], held[1, 4], *early_on)
        gather.corner(0, held[0, 2], held[0, 4], held[2, 2])
    else:
        whole = [lax.all_gather(w, N.shard, axis=0, tiled=True) for w in weights]
        cut = lambda w, j: lax.slice_in_dim(
            w, j * (w.shape[0] // PARTS), (j + 1) * (w.shape[0] // PARTS)
        )
        attention = [pack_attention([cut(w, j) for w in whole[:4]]) for j in range(PARTS)]
        hidden = [
            pack_slices(range(SLICES), [cut(w, j) for w in whole[4:]]) for j in range(PARTS)
        ]
        blocks = [attention] + [[hidden[j][f] for j in range(PARTS)] for f in range(SLICES)]
        blocks = [
            [b[m][:, low:high] if high - low < MSG else b[m] for m, low, high in HELD]
            for b in blocks
        ]
        pos = jnp.arange(PARTS, dtype=jnp.int32)
        pos = jnp.concatenate([pos, jnp.zeros_like(pos)])
        offset = tree_adapter[device_tree[group + shard]] * RANK
        segments = {}
        for name, part in zip(NAMES, adapters):
            full = lax.all_gather(part, N.shard, axis=0, tiled=True)
            own = lax.dynamic_slice_in_dim(full, offset, RANK, 1)
            segments[name] = own.reshape(PARTS, -1, RANK).transpose(0, 2, 1)
        both = jnp.stack(
            [lax.all_gather(g, N.shard, axis=0, tiled=True) for g in (gain_a, gain_h)]
        )
        both = both.reshape(2, PARTS, ROWS).transpose(1, 0, 2)
        segments[N.gain] = jnp.pad(both, ((0, 0), (0, RANK - 2), (0, 0)))
        packed = jnp.concatenate([segments[name] for name in OFF], axis=2)
        packed = jnp.pad(packed, ((0, 0), (0, 0), (0, LANES - packed.shape[2])))

    allowed, positions = tree_layout(parents[0], rows)
    bias = jnp.where(allowed, 0.0, -1e30).astype(F)
    cosine, sine = rope_tables(positions)
    ready = launch(
        N.prepare,
        prepare_body,
        dict(
            acat=((128, D), B),
            ebd=((128, QKV), B),
            ao=((128, D), B),
            eo=((128, D), B),
            agu=((128, D), B),
            ed=((128, D), B),
            egu=((SLICES, 128, 2 * SL), B),
            ad=((SLICES, SL, 128), B),
            gains=((RANK, D), F),
            h1a=((rows, WIDE), B),
            cota=((rows, WIDE), B),
        ),
        dict(packed=packed, x=x, cot=cot),
        scratch=dict(line=((RANK, D), F), wide=((PARTS, RANK, LANES), F)),
    )
    if direct:
        gather.corner(1, held[0, 2], held[0, 4], held[2, 2], ready[N.h1a], bias, cosine, sine)
        for at in (2, 4):
            gather.core(0, at, ready[N.h1a], bias, cosine, sine)
        for at in (6, 8):
            gather.core(0, at)
        blocks = [gather.blocks(0)]
    tables = dict(bias=bias, cosine=cosine, sine=sine)
    some = lambda *names: {name: ready[name] for name in names}
    front = launch(
        N.project,
        project_body,
        dict(q=((rows, D), B), kd=((rows, 2 * KVW), B), vd=((rows, 2 * KVW), B)),
        dict(cosine=cosine, sine=sine, **some(N.h1a, N.ebd)),
        blocks[0],
        pos,
        scratch=dict(weight=((WIDE, QKV), B)),
    )
    if direct:
        ahead = [front[N.q], held[1, 6], held[1, 8], held[2, 4]]
        gather.links(3, held[3, 0], *ahead)
        for at in (6, 8):
            gather.across(2, 1, at, *ahead)
    front.update(
        launch(
            N.attend,
            attend_body,
            dict(
                oa=((rows, WIDE), B),
                lse=((3, 2, rows, 128), F),
                x2=((rows, D), F),
                h2a=((rows, WIDE), B),
            ),
            dict(x=x, bias=bias, **front, **some(N.ao, N.eo, N.agu, N.gains)),
            blocks[0],
            pos,
            scratch=dict(wout=((WIDE, D), B)),
        )
    )
    h2a, x2 = front[N.h2a], front[N.x2]
    if direct:
        both = [held[3, at] for at in (2, 4)]
        gather.corner(3, h2a, *both)
        for n in (1, 2):
            for at in (2, 4, 6, 8):
                gather.core(n, at, h2a, *both)
    state = None
    for slices in RUNS:
        first, last = slices[0] == 0, slices[-1] == SLICES - 1
        if direct:
            if last:
                for at in (2, 4, 6, 8):
                    gather.core(3, at, state[N.early])
            for f in slices:
                if len(blocks) < f + 2:
                    blocks.append(gather.blocks(1 + f))
        ins = dict(h2a=h2a, **some(N.cota, N.egu, N.ad))
        count = len(slices)
        scratch = dict(
            wgu=((count, WIDE, 2 * SL), B),
            wd=((count, SL, WIDE), B),
            tail=((count, PARTS * 16, SL), B),
            mid=((rows, SL), B),
            ggt=((rows, SL), B),
            gup=((rows, SL), B),
            line=((RANK, D), F),
        )
        outs = dict(
            y=((rows, WIDE), F), g=((rows, WIDE), F), early=((PARTS, RANK, EARLY_LANES), F)
        )
        if not first:
            ins.update(y_in=state[N.y], g_in=state[N.g], early_in=state[N.early])
        if last:
            ins.update(x2=x2, **some(N.agu, N.ed))
            scratch.update(y_acc=outs[N.y], g_acc=outs[N.g], early_acc=outs[N.early])
            outs = dict(
                y=((rows, D), B),
                g=((rows, D), F),
                early=((QUARTERS, PARTS, RANK, EARLY_LANES // QUARTERS), B),
            )
        state = launch(
            "hidden_%d" % slices[0],
            functools.partial(hidden_body, slices),
            outs,
            ins,
            [piece for f in slices for piece in blocks[1 + f]],
            pos,
            scratch,
            sems=64 + 80 * count,
        )
    layer_output, gh2, early = state[N.y], state[N.g], state[N.early]
    if direct:
        early_come = exchange(early)
    operands = dict(gh2=gh2, x2=x2, cot=cot, **tables, **some(N.ao, N.eo, N.gains, N.h1a, N.ebd))
    operands.update({name: front[name] for name in (N.q, N.kd, N.vd, N.oa, N.lse)})
    back = launch(
        N.back,
        back_body,
        dict(
            gx2=((rows, D), F),
            gqkv=((rows, QKV), B),
            gred=((rows, 128), B),
            late=((QUARTERS, PARTS, RANK, LATE_LANES // QUARTERS), B),
        ),
        operands,
        blocks[0],
        pos,
        dict(
            weight=((WIDE, D), B),
            go=((rows, D), B),
            gk=((2, rows, 128), F),
            gv=((2, rows, 128), F),
            line=((RANK, D), F),
            late_acc=((PARTS, RANK, LATE_LANES), F),
        ),
    )
    late = back[N.late]
    if direct:
        early_come, late = lax.optimization_barrier((early_come, late))
        late_come = exchange(late)
        early_parts = share(add_up(early_come, device_tree, tree_adapter))
        late_quarter = add_up(late_come, device_tree, tree_adapter)
    input_grad = launch(
        N.finish,
        finish_body,
        dict(out=((rows, D), F)),
        dict(
            x=x, gx2=back[N.gx2], gqkv=back[N.gqkv], gred=back[N.gred], **some(N.acat, N.gains)
        ),
        blocks[0],
        pos,
        dict(weight=((D, QKV), B)),
    )[N.out]
    owned = {}
    if direct:
        rep = lax.axis_index(N.rep).astype(jnp.int32).reshape(1)
        late_parts = share(late_quarter)
    for grads, names, offsets in ((early, EARLY, EARLY_OFF), (late, LATE, LATE_OFF)):
        if direct:
            parts = early_parts if names is EARLY else late_parts
            received = call(
                functools.partial(deliver_kernel, names, offsets),
                [((SEG_ROWS[name], ADAPTERS * RANK), F) for name in names],
                (rep, *parts),
                spaces={0: pltpu.SMEM},
                scratch=[pltpu.VMEM((QUARTERS * parts[0].shape[0], ADAPTERS * RANK), F)],
                name=N.deliver,
            )
            owned.update(zip(names, received))
        else:
            grads = grads.transpose(1, 2, 0, 3).reshape(PARTS, RANK, -1)
            for name in names:
                part = grads[:, :, offsets[name] : offsets[name] + SEG_ROWS[name]]
                part = part.transpose(0, 2, 1).reshape(-1, RANK)
                wide = lax.dynamic_update_slice_in_dim(
                    jnp.zeros((part.shape[0], ADAPTERS * RANK), B), part, offset, 1
                )
                wide = lax.psum_scatter(wide, N.shard, scatter_dimension=0, tiled=True)
                owned[name] = lax.psum(wide, N.rep).astype(F)
    return (layer_output, input_grad) + tuple(owned[name] for name in NAMES)


def solution(mesh):
    token = P((N.rep, N.shard), None)
    row = P(N.shard, None)
    return jax.shard_map(
        on_device,
        mesh=mesh,
        in_specs=(token, token, P(N.shard), P(N.shard)) + (row,) * 21 + (token, P(), P()),
        out_specs=(token, token) + (row,) * 14,
        check_vma=False,
    )
```

```python
import functools

import jax
import jax.numpy as jnp
from jax import lax
from jax.experimental import pallas as pl
from jax.experimental.pallas import tpu as pltpu
from jax.sharding import PartitionSpec as P

D = 1152
Q_HEADS = 18
KV_HEADS = 6
HEAD_DIM = 64
FF = 3072
RANK = 16
ADAPTERS = 8
TRUNK = 128
BRANCH = 24
LEAF = 24
KVW = 384
PARTS = 8
ROWS = D // PARTS
FROWS = FF // PARTS
SLICES = 3
SL = FF // SLICES
WIDE = D + 128
QKV = D + 2 * KVW
MSG = 3072
eps = 1e-05
F = jnp.float32
B = jnp.bfloat16


class Words:
    def __getattr__(self, word):
        return word


N = Words()
VMEM_LIMIT = 58 * 1024 * 1024

NAMES = (N.qr, N.qe, N.kr, N.ke, N.vr, N.ve, N.wr, N.oe, N.gr, N.ge, N.ur, N.ue, N.dr, N.de)
SEG_ROWS = {name: ROWS for name in NAMES}
SEG_ROWS.update(ke=KVW // PARTS, ve=KVW // PARTS, ge=FROWS, ue=FROWS, dr=FROWS)


SEG_ROWS[N.gain] = ROWS
EARLY = (N.ge, N.ue, N.dr, N.gr, N.ur, N.de)
LATE = (N.wr, N.oe, N.qr, N.qe, N.kr, N.ke, N.vr, N.ve)
QUARTERS = 4


def lay_out(names, unit):
    offsets = {}
    total = 0
    for name in names:
        offsets[name] = total
        total += SEG_ROWS[name]
    return offsets, -(-total // unit) * unit


EARLY_OFF, EARLY_LANES = lay_out(EARLY, QUARTERS * 128)
LATE_OFF, LATE_LANES = lay_out(LATE, QUARTERS * 128)
OFF, LANES = lay_out(EARLY + LATE + (N.gain,), 128)
BLOCKS = ((0, 128, 128), (128, 224, 256), (224, 416, 416))


def nn(left, right):
    return lax.dot_general(left, right, (((1,), (0,)), ((), ())), preferred_element_type=F)


def nt(left, right):
    return lax.dot_general(left, right, (((1,), (1,)), ((), ())), preferred_element_type=F)


def tn(left, right):
    return lax.dot_general(left, right, (((0,), (0,)), ((), ())), preferred_element_type=F)


RUNS = ((0, 1), (2,))
COST = dict(flops=1 << 20, bytes_accessed=1 << 16, transcendentals=0)


def call(kernel, out_shape, args, spaces=None, scratch=(), name=None):
    in_specs = [
        pl.BlockSpec(memory_space=(spaces or {}).get(i, pltpu.VMEM)) for i in range(len(args))
    ]
    return pl.pallas_call(
        kernel,
        out_shape=[jax.ShapeDtypeStruct(s, d) for s, d in out_shape],
        in_specs=in_specs,
        out_specs=[pl.BlockSpec(memory_space=pltpu.VMEM) for _ in out_shape],
        scratch_shapes=list(scratch),
        compiler_params=pltpu.CompilerParams(vmem_limit_bytes=VMEM_LIMIT),
        cost_estimate=pl.CostEstimate(**COST),
        name=name,
    )(*args)


class Frame:
    def __init__(self, pos, near, far, outs, sems):
        self.pos, self.near, self.far, self.outs, self.sems = pos, near, far, outs, sems
        self.used = 0
        self.coming = {}
        self.leaving = []

    def copy(self, source, target):
        moved = pltpu.make_async_copy(source, target, self.sems.at[self.used])
        self.used += 1
        moved.start()
        return moved

    def fetch(self, *names):
        for name in names:
            self.coming[name] = [self.copy(self.far[name], self.near[name])]

    def fetch_into(self, key, source, target):
        self.coming.setdefault(key, []).append(self.copy(source, target))

    def fetch_rows(self, key, pieces, low, lanes, target, rows=ROWS, start=0, to=0):
        for piece, (m, begin, end) in zip(pieces, HELD):
            a, b = max(low, begin), min(low + lanes, end)
            if a < b:
                self.fetch_into(
                    key,
                    piece.at[pl.ds(start, rows), pl.ds(a - begin, b - a)],
                    target.at[row_at(self.pos, m, rows), pl.ds(to + a - low, b - a)],
                )

    def wait(self, *keys):
        for key in keys:
            for moved in self.coming.pop(key, ()):
                moved.wait()

    def __getitem__(self, name):
        self.wait(name)
        return self.near[name]

    def send(self, name, at=None):
        near, far = self.near[name], self.outs[name]
        if at is not None:
            near, far = near.at[:, at], far.at[:, at]
        self.leaving.append(self.copy(near, far))

    def close(self):
        for moved in self.leaving:
            moved.wait()


def launch(
    name, body, outs, ins, pieces=(), pos=None, scratch=None, sems=64, weigh=None
):
    scratch = scratch or {}
    operands = ([] if pos is None else [pos]) + list(ins.values()) + list(pieces)

    def kernel(*refs):
        refs = list(refs)
        take = lambda count: [refs.pop(0) for _ in range(count)]
        where = None if pos is None else take(1)[0]
        far = dict(zip(ins, take(len(ins))))
        parts = take(len(pieces))
        results = dict(zip(outs, take(len(outs))))
        near = dict(zip(ins, take(len(ins))))
        near.update(zip(outs, take(len(outs))))
        near.update(zip(scratch, take(len(scratch))))
        frame = Frame(where, near, far, results, refs[0])
        body(frame, parts)
        frame.close()

    hbm = pl.BlockSpec(memory_space=pltpu.HBM)
    specs = [hbm] * (len(ins) + len(pieces))
    if pos is not None:
        specs = [pl.BlockSpec(memory_space=pltpu.SMEM)] + specs
    results = pl.pallas_call(
        kernel,
        out_shape=[jax.ShapeDtypeStruct(s, d) for s, d in outs.values()],
        in_specs=specs,
        out_specs=[hbm] * len(outs),
        scratch_shapes=[pltpu.VMEM(v.shape, v.dtype) for v in ins.values()]
        + [pltpu.VMEM(s, d) for s, d in outs.values()]
        + [pltpu.VMEM(s, d) for s, d in scratch.values()]
        + [pltpu.SemaphoreType.DMA((sems,))],
        compiler_params=pltpu.CompilerParams(vmem_limit_bytes=VMEM_LIMIT),
        cost_estimate=pl.CostEstimate(**(weigh or COST)),
        name=name,
    )(*operands)
    return dict(zip(outs, results))


def tree_layout(parents_row, row_count):
    index = jnp.arange(row_count, dtype=jnp.int32)
    after = index - TRUNK
    leaf_start = TRUNK + 4 * BRANCH
    in_branch = (index >= TRUNK) & (index < leaf_start)
    in_leaf = index >= leaf_start
    segment = jnp.where(
        in_leaf, 5 + (index - leaf_start) // LEAF, jnp.where(in_branch, 1 + after // BRANCH, 0)
    )
    positions = jnp.where(
        in_leaf,
        TRUNK + BRANCH + (index - leaf_start) % LEAF,
        jnp.where(in_branch, TRUNK + after % BRANCH, index),
    )
    numbers = jnp.arange(13, dtype=jnp.int32)
    parent = jnp.sum(
        jnp.where(segment[:, None] == numbers[None, :], parents_row[None, :], 0), axis=1
    )
    grand = jnp.sum(jnp.where(parent[:, None] == numbers[None, :], parents_row[None, :], 0), axis=1)
    same = (segment[:, None] == segment[None, :]) & (index[None, :] <= index[:, None])
    above = (segment[:, None] != 0) & (
        (segment[None, :] == parent[:, None]) | (segment[None, :] == grand[:, None])
    )
    return (same | above, positions)


def rope_tables(positions):
    halfway = HEAD_DIM // 2
    frequency = 10000.0 ** (-jnp.arange(halfway, dtype=F) / halfway)
    angles = positions.astype(F)[:, None] * frequency[None, :]
    cosine, sine = jnp.cos(angles), jnp.sin(angles)
    return (
        jnp.concatenate([cosine] * 4, axis=1),
        jnp.concatenate([-sine, sine, -sine, sine], axis=1),
    )


def attention_copies(weights, out):
    copies = []
    at = 0
    for weight in weights:
        copies.append((weight, out.at[:, pl.ds(at, weight.shape[1])]))
        at += weight.shape[1]
    return copies


def slice_copies(f, g, u, d, out):
    at = pl.multiple_of(f * 128, 128)
    copies = []
    for s in range(PARTS):
        lanes = pl.ds(pl.multiple_of(s * FROWS + at, 128), 128)
        copies.append((g.at[:, lanes], out.at[:, pl.ds(s * 128, 128)]))
        copies.append((u.at[:, lanes], out.at[:, pl.ds(SL + s * 128, 128)]))
    copies.append(
        (d.at[pl.ds(at, 128), pl.ds(0, SL)], out.at[pl.ds(0, 128), pl.ds(2 * SL, SL)])
    )
    for b in range(8):
        rows = pl.ds(pl.multiple_of(at + b * 16, 16), 16)
        copies.append(
            (
                d.at[rows, pl.ds(SL, 128)],
                out.at[pl.ds(128, 16), pl.ds(2 * SL + b * 128, 128)],
            )
        )
    return copies


def start_all(copies, sems, first=0):
    moved = [
        pltpu.make_async_copy(source, target, sems.at[first + k])
        for k, (source, target) in enumerate(copies)
    ]
    for copy in moved:
        copy.start()
    return moved


SLICE_COPIES = 2 * PARTS + 9


def pack_attention_kernel(q, k, v, o, out, sems):
    for copy in start_all(attention_copies((q, k, v, o), out), sems):
        copy.wait()


def pack_slices_kernel(numbers, g, u, d, *refs):
    outs, sems = refs[:-1], refs[-1]
    moved = []
    for n, out in enumerate(outs):
        moved += start_all(slice_copies(numbers[n], g, u, d, out), sems, n * SLICE_COPIES)
    for copy in moved:
        copy.wait()


def pack_attention(weights):
    return call(
        pack_attention_kernel,
        [((ROWS, MSG), B)],
        weights,
        spaces={n: pltpu.HBM for n in range(4)},
        scratch=[pltpu.SemaphoreType.DMA((4,))],
        name=N.pack_attention,
    )[0]


def pack_slices(numbers, weights):
    numbers = jnp.stack([jnp.asarray(f, jnp.int32) for f in numbers])
    return call(
        pack_slices_kernel,
        [((ROWS, MSG), B)] * numbers.shape[0],
        (numbers, *weights),
        spaces={0: pltpu.SMEM, 1: pltpu.HBM, 2: pltpu.HBM, 3: pltpu.HBM},
        scratch=[pltpu.SemaphoreType.DMA((numbers.shape[0] * SLICE_COPIES,))],
        name=N.pack_slices,
    )


def choose(trees, slots, first, count):
    column = lax.broadcasted_iota(jnp.int32, (RANK, ADAPTERS * RANK), 1)
    row = lax.broadcasted_iota(jnp.int32, (RANK, ADAPTERS * RANK), 0)
    parts = [
        jnp.where(column == slots[trees[first + d]] * RANK + row, 1.0, 0.0) for d in range(count)
    ]
    return jnp.concatenate(parts, axis=0).astype(B)


def pack_first_kernel(facts, trees, slots, *refs):
    weights, gains, parts = refs[:7], refs[7:9], refs[9:23]
    first, attention, out, wide, sems = refs[23:]
    moved = start_all(slice_copies(facts[1], *weights[4:], first), sems)
    moved += start_all(attention_copies(weights[:4], attention), sems, SLICE_COPIES)
    chosen = choose(trees, slots, facts[0], PARTS)
    for name, part in zip(NAMES, parts):
        wide[:, OFF[name] : OFF[name] + SEG_ROWS[name]] = nt(chosen, part[...])
    row = lax.broadcasted_iota(jnp.int32, (RANK, ROWS), 0)
    both = jnp.where(
        row == 0,
        gains[0][...].astype(F).reshape(1, ROWS),
        jnp.where(row == 1, gains[1][...].astype(F).reshape(1, ROWS), 0.0),
    )
    for d in range(PARTS):
        wide[d * RANK : (d + 1) * RANK, OFF[N.gain] : OFF[N.gain] + ROWS] = both
    out[...] = wide[...].astype(B)
    for copy in moved:
        copy.wait()


HALF = MSG // 2
HELD = [(m, 0, MSG) for m in range(6)] + [
    (m, low, low + HALF) for m in (6, 7) for low in (0, HALF)
]
HELD_COUNT = len(HELD)


def row_at(pos, m, rows):
    return pl.ds(pl.multiple_of(pos[m] * rows, rows), rows)


def swap_halves(value, first):
    return jnp.where(first, pltpu.roll(value, 96, 1), pltpu.roll(value, 32, 1))


def half_masks():
    lane = lax.broadcasted_iota(jnp.int32, (1, 128), 1)
    low = jnp.where(lane < 64, 1.0, 0.0)
    return low, 1.0 - low


def prepare_body(c, _):
    c.fetch(N.x, N.cot, N.packed)
    near = c.near
    for name in (N.acat, N.ebd, N.ao, N.eo, N.agu, N.ed, N.egu):
        near[name][...] = jnp.zeros(near[name].shape, B)
    source = c[N.x][...].astype(F)
    scale = lax.rsqrt(jnp.mean(source * source, axis=1, keepdims=True) + eps)
    wide = near[N.wide]
    wide[...] = c[N.packed][...].astype(F)
    line = near[N.line]

    def rows_of(name, width=None, start=0):
        rows = SEG_ROWS[name] if width is None else width
        low = OFF[name] + start
        for j in range(PARTS):
            line[:, j * rows : (j + 1) * rows] = wide[j, :, low : low + rows]
        return line[:, : PARTS * rows]

    near[N.gains][...] = rows_of(N.gain)
    acat = near[N.acat]
    acat[:16, :] = rows_of(N.qr).astype(B)
    acat[16:32, :] = rows_of(N.kr).astype(B)
    acat[32:48, :] = rows_of(N.vr).astype(B)
    near[N.ed][:16, :] = rows_of(N.de).astype(B)
    h1 = (source * scale * near[N.gains][0:1, :]).astype(B)
    near[N.h1a][:, :D] = h1
    near[N.h1a][:, D:] = nt(h1, acat[...]).astype(B)
    near[N.cota][:, :D] = c[N.cot][...]
    near[N.cota][:, D:] = nt(c[N.cot][...], near[N.ed][...]).astype(B)
    ebd, agu, egu = near[N.ebd], near[N.agu], near[N.egu]
    ebd[:16, :D] = rows_of(N.qe).astype(B)
    ebd[16:32, D : D + KVW] = rows_of(N.ke).astype(B)
    ebd[32:48, D + KVW :] = rows_of(N.ve).astype(B)
    for name in (N.h1a, N.cota, N.acat, N.ebd, N.gains, N.ed):
        c.send(name)
    near[N.ao][:16, :] = rows_of(N.wr).astype(B)
    near[N.eo][:16, :] = rows_of(N.oe).astype(B)
    agu[:16, :] = rows_of(N.gr).astype(B)
    agu[16:32, :] = rows_of(N.ur).astype(B)
    for name in (N.ao, N.eo, N.agu):
        c.send(name)
    for f in range(SLICES):
        egu[f, :16, :SL] = rows_of(N.ge, 128, f * 128).astype(B)
        egu[f, 16:32, SL:] = rows_of(N.ue, 128, f * 128).astype(B)
        down = rows_of(N.dr, 128, f * 128)
        near[N.ad][f] = jnp.concatenate([down, jnp.zeros((112, SL), F)], axis=0).T.astype(B)
    c.send(N.egu)
    c.send(N.ad)


def project_body(c, pieces):
    near = c.near
    weight = near[N.weight]
    c.fetch(N.h1a)
    c.fetch_rows(N.w0, pieces, 0, 768, weight)
    c.fetch_into(N.w0, c.far[N.ebd], weight.at[pl.ds(D, 128), :])
    c.fetch(N.cosine, N.sine)
    c.fetch_rows(N.w1, pieces, 768, QKV - 768, weight, to=768)
    h1a = c[N.h1a]
    rows = h1a.shape[0]
    lane = lax.broadcasted_iota(jnp.int32, (rows, 128), 1)
    low, first = lane < 64, lane % 64 < 32
    q, kd, vd = near[N.q], near[N.kd], near[N.vd]
    c.wait(N.w0)
    for block in range(5):
        if block == 2:
            c.wait(N.w1)
        value = nn(h1a[...], weight[:, block * 384 : (block + 1) * 384])
        for t in range(3):
            part = value[:, t * 128 : (t + 1) * 128]
            if block < 4:
                part = part * c[N.cosine][...] + swap_halves(part, first) * c[N.sine][...]
            if block < 3:
                at = block * 384 + t * 128
                q[:, at : at + 128] = (part * HEAD_DIM**-0.5).astype(B)
            else:
                out = kd if block == 3 else vd
                rolled = pltpu.roll(part, 64, 1)
                out[:, t * 256 : t * 256 + 128] = jnp.where(low, part, rolled).astype(B)
                out[:, t * 256 + 128 : (t + 1) * 256] = jnp.where(low, rolled, part).astype(B)
    for name in (N.q, N.kd, N.vd):
        c.send(name)


def attend_body(c, pieces):
    near = c.near
    wout = near[N.wout]
    c.fetch(N.q, N.kd, N.bias, N.vd)
    c.fetch_rows(N.wout, pieces, QKV, D, wout)
    c.fetch_into(N.wout, c.far[N.eo], wout.at[pl.ds(D, 128), :])
    c.fetch(N.x, N.ao, N.agu, N.gains)
    q, kd, vd = c[N.q], c[N.kd], c[N.vd]
    rows = q.shape[0]
    masks = [mask.astype(B) for mask in half_masks()]
    bias, oa, lse, x2, h2a = c[N.bias], near[N.oa], near[N.lse], near[N.x2], near[N.h2a]

    def tile(i, _):
        lanes = [pl.ds(pl.multiple_of((3 * i + t) * 128, 128), 128) for t in range(3)]
        outs = {}
        for side in range(2):
            group = pl.ds(pl.multiple_of((2 * i + side) * 128, 128), 128)
            values = vd[:, group] * masks[0] + masks[1]
            for block, (low_row, high_row, keys) in enumerate(BLOCKS):
                count = high_row - low_row
                heads = [divmod(3 * side + slot, 2) for slot in range(3)]
                query = jnp.concatenate(
                    [q[low_row:high_row, lanes[t]] * masks[half] for t, half in heads], axis=0
                )
                scores = nt(query, kd[:keys, group]).reshape(3, count, keys)
                scores = (scores + bias[low_row:high_row, :keys][None]).reshape(3 * count, keys)
                top = jnp.max(scores, axis=1, keepdims=True)
                result = nn(jnp.exp(scores - top).astype(B), values[:keys])
                summed = result[:, 64:65]
                result = result * (1.0 / summed)
                total = top + jnp.log(summed)
                lane = lax.broadcasted_iota(jnp.int32, (count, 128), 1)
                split = lambda v, slot: v[slot * count : (slot + 1) * count]
                lse[i, side, low_row:high_row, :] = jnp.where(
                    lane == 0,
                    split(total, 0),
                    jnp.where(lane == 1, split(total, 1), split(total, 2)),
                )
                for slot in range(3):
                    outs[block, 3 * side + slot] = split(result, slot)
        for block, (low_row, high_row, _) in enumerate(BLOCKS):
            lane = lax.broadcasted_iota(jnp.int32, (high_row - low_row, 128), 1)
            for t in range(3):
                oa[low_row:high_row, lanes[t]] = jnp.where(
                    lane < 64, outs[block, 2 * t], pltpu.roll(outs[block, 2 * t + 1], 64, 1)
                ).astype(B)
        return 0

    lax.fori_loop(0, 3, tile, 0)
    c.send(N.lse)
    oa[:, D:] = nt(oa[:, :D], c[N.ao][...]).astype(B)
    c.send(N.oa)
    c.wait(N.wout)
    square = jnp.zeros((rows, 1), F)
    for block in range(3):
        at = slice(block * 384, (block + 1) * 384)
        value = c[N.x][:, at].astype(F) + nn(oa[...], wout[:, at])
        x2[:, at] = value
        square += jnp.sum(value * value, axis=1, keepdims=True)
    c.send(N.x2)
    scale = lax.rsqrt(square / D + eps)
    h2a[:, :D] = (x2[...] * scale * c[N.gains][1:2, :]).astype(B)
    h2a[:, D:] = nt(h2a[:, :D], c[N.agu][...]).astype(B)
    c.send(N.h2a)


def put(grads, offsets, name, line, value, row, width=None, start=0):
    width = SEG_ROWS[name] if width is None else width
    line[:, : PARTS * width] = value[row : row + RANK, :]
    for j in range(PARTS):
        at = pl.ds(offsets[name] + start, width)
        if not isinstance(start, int):
            at = pl.ds(pl.multiple_of(offsets[name] + start, 128), width)
        grads[j, :, at] = line[:, j * width : (j + 1) * width]


def hand_out(grads, out):
    part = out.shape[3]
    for q in range(QUARTERS):
        out[q] = grads[:, :, q * part : (q + 1) * part].astype(B)


def hidden_body(slices, c, pieces):
    first, last = slices[0] == 0, slices[-1] == SLICES - 1
    near = c.near
    mid, ggt, gup, line = near[N.mid], near[N.ggt], near[N.gup], near[N.line]
    c.fetch(N.h2a)
    number = [c.pos[PARTS], 1 - c.pos[PARTS]] if first else slices
    for n, f in enumerate(slices):
        wgu, wd, tail = near[N.wgu].at[n], near[N.wd].at[n], near[N.tail].at[n]
        own = pieces[n * HELD_COUNT : (n + 1) * HELD_COUNT]
        for part in range(2):
            for side in range(2):
                at = side * SL + part * 512
                c.fetch_rows((N.gu, f, part), own, at, 512, wgu, to=at)
            if part == 0:
                c.fetch_into((N.gu, f, 0), c.far[N.egu].at[number[n]], wgu.at[pl.ds(D, 128), :])
                if n == 0:
                    c.fetch(N.cota)
                c.fetch_rows((N.wd, f), own, 2 * SL, SL, wd, 128)
                c.fetch_rows((N.wd, f), own, 2 * SL, SL, tail, 16, 128)
                c.fetch_into((N.wd, f), c.far[N.ad].at[number[n]], wd.at[:, pl.ds(D, 128)])
    if not first:
        c.fetch(N.y_in, N.g_in, N.early_in)
    if last:
        c.fetch(N.x2, N.agu, N.ed)
    h2a = c[N.h2a]
    y_acc, g_acc, early = near[N.y_acc], near[N.g_acc], near[N.early_acc]
    grow = functools.partial(put, early, EARLY_OFF)
    lanes = slice(D, WIDE)
    for n, f in enumerate(slices):
        wgu, wd, tail = near[N.wgu].at[n], near[N.wd].at[n], near[N.tail].at[n]
        for k in range(SL // 256):
            at = slice(k * 256, (k + 1) * 256)
            if k % 2 == 0:
                c.wait((N.gu, f, k // 2))
            gate = nn(h2a[...], wgu[:, at])
            up = nn(h2a[...], wgu[:, SL + k * 256 : SL + (k + 1) * 256])
            sig = jax.nn.sigmoid(gate)
            silu = gate * sig
            if k == 0:
                cota = c[N.cota]
                c.wait((N.wd, f))
                for m in range(PARTS):
                    for b in range(8):
                        wd[m * 128 + b * 16 : m * 128 + (b + 1) * 16, SL:D] = tail[
                            m * 16 : (m + 1) * 16, b * 128 : (b + 1) * 128
                        ]
            gmid = nt(cota[...], wd[at, :])
            mid[:, at] = (silu * up).astype(B)
            ggt[:, at] = (gmid * up * sig * (1.0 + gate * (1.0 - sig))).astype(B)
            gup[:, at] = (gmid * silu).astype(B)
        for k in range(5):
            at = slice(k * 256, (k + 1) * 256)
            value = nn(mid[...], wd[:, at])
            if n:
                value += y_acc[:, at]
            elif not first:
                value += c[N.y_in][:, at].astype(F)
            if last or n < len(slices) - 1:
                y_acc[:, at] = value
            else:
                near[N.y][:, at] = value.astype(B)
            value = nt(ggt[...], wgu[at, :SL]) + nt(gup[...], wgu[at, SL:])
            if n:
                value += g_acc[:, at]
            elif not first:
                value += c[N.g_in][:, at].astype(F)
            if last or n < len(slices) - 1:
                g_acc[:, at] = value
            else:
                near[N.g][:, at] = value.astype(B)
            if not last and n == len(slices) - 1:
                c.send(N.y, at)
                c.send(N.g, at)
        if n == 0:
            early[...] = jnp.zeros(early.shape, F) if first else c[N.early_in][...].astype(F)
        grow(N.ge, line, tn(h2a[:, lanes], ggt[...]), 0, 128, number[n] * 128)
        grow(N.ue, line, tn(h2a[:, lanes], gup[...]), 16, 128, number[n] * 128)
        grow(N.dr, line, tn(cota[:, lanes], mid[...]), 0, 128, number[n] * 128)
    if last:
        red = g_acc[:, lanes].astype(B)
        near[N.g][...] = g_acc[:, :D] + nn(red, c[N.agu][...])
        c.send(N.g)
        down_red = y_acc[:, lanes].astype(B)
        grow(N.de, line, tn(down_red, cota[:, :D]), 0)
        value = tn(red, h2a[:, :D])
        grow(N.gr, line, value, 0)
        grow(N.ur, line, value, 16)
        hand_out(early, near[N.early])
        c.send(N.early)
        near[N.y][...] = (y_acc[:, :D] + c[N.x2][...] + nn(down_red, c[N.ed][...])).astype(B)
        c.send(N.y)
    else:
        near[N.early][...] = early[...].astype(B)
        c.send(N.early)


def back_body(c, pieces):
    near, far = c.near, c.far
    c.fetch(N.gh2, N.x2, N.gains, N.cot)
    weight, gx2, go, late, line = (near[k] for k in (N.weight, N.gx2, N.go, N.late_acc, N.line))
    c.fetch_into(N.eo, far[N.eo], weight.at[pl.ds(D, 128), :])
    c.fetch_rows(N.weight, pieces, QKV, D, weight)
    c.fetch(N.ao, N.oa, N.bias, N.q, N.kd, N.vd, N.lse, N.cosine, N.sine, N.h1a, N.ebd)
    late[...] = jnp.zeros(late.shape, F)
    residual = c[N.x2][...]
    scale = lax.rsqrt(jnp.mean(residual * residual, axis=1, keepdims=True) + eps)
    weighted = c[N.gh2][...] * c[N.gains][1:2, :]
    inner = jnp.mean(residual * weighted, axis=1, keepdims=True)
    gx2[...] = (
        c[N.cot][...].astype(F) + scale * weighted - residual * (scale * scale * scale) * inner
    )
    c.send(N.gx2)
    branch = gx2[...].astype(B)
    c.wait(N.eo)
    red = nt(branch, weight[D:, :]).astype(B)
    c.wait(N.weight)
    for block in range(3):
        at = slice(block * 384, (block + 1) * 384)
        go[:, at] = (nt(branch, weight[at, :]) + nn(red, c[N.ao][:, at])).astype(B)
    grow = functools.partial(put, late, LATE_OFF)
    oa = c[N.oa]
    grow(N.wr, line, tn(red, oa[:, :D]), 0)
    grow(N.oe, line, tn(oa[:, D:], branch), 0)
    gqkv, gk, gv = near[N.gqkv], near[N.gk], near[N.gv]
    q, kd, vd, lse, bias, cosine, sine = (
        c[k] for k in (N.q, N.kd, N.vd, N.lse, N.bias, N.cosine, N.sine)
    )
    masks = [mask.astype(B) for mask in half_masks()]
    wide_masks = half_masks()

    def turn_back(value, low_row, high_row):
        first = lax.broadcasted_iota(jnp.int32, value.shape, 1) % 64 < 32
        return (
            value * cosine[low_row:high_row, :]
            - swap_halves(value, first) * sine[low_row:high_row, :]
        )

    def tile(i, _):
        gk[...] = jnp.zeros(gk.shape, F)
        gv[...] = jnp.zeros(gv.shape, F)
        lanes = [pl.ds(pl.multiple_of((3 * i + t) * 128, 128), 128) for t in range(3)]
        outs = {}
        for side in range(2):
            group = pl.ds(pl.multiple_of((2 * i + side) * 128, 128), 128)
            for block, (low_row, high_row, keys) in enumerate(BLOCKS):
                count = high_row - low_row
                query, grad, inner, total = [], [], [], []
                for slot in range(3):
                    t, half = divmod(3 * side + slot, 2)
                    upstream = go[low_row:high_row, lanes[t]]
                    product = upstream.astype(F) * oa[low_row:high_row, lanes[t]].astype(F)
                    query.append(q[low_row:high_row, lanes[t]] * masks[half])
                    grad.append(upstream * masks[half])
                    inner.append(jnp.sum(product * wide_masks[half], axis=1, keepdims=True))
                    total.append(lse[i, side, low_row:high_row, slot : slot + 1])
                query, grad, inner, total = (
                    jnp.concatenate(v, axis=0) for v in (query, grad, inner, total)
                )
                scores = nt(query, kd[:keys, group]).reshape(3, count, keys)
                scores = (scores + bias[low_row:high_row, :keys][None]).reshape(3 * count, keys)
                probs = jnp.exp(scores - total)
                grad_probs = nt(grad, vd[:keys, group])
                ds = (probs * (grad_probs - inner)).astype(B)
                gv[side, :keys, :] += tn(probs.astype(B), grad)
                gk[side, :keys, :] += tn(ds, query)
                result = nn(ds, kd[:keys, group])
                for slot in range(3):
                    outs[block, 3 * side + slot] = result[slot * count : (slot + 1) * count]
        for block, (low_row, high_row, _) in enumerate(BLOCKS):
            low = lax.broadcasted_iota(jnp.int32, (high_row - low_row, 128), 1) < 64
            for t in range(3):
                value = jnp.where(low, outs[block, 2 * t], outs[block, 2 * t + 1])
                gqkv[low_row:high_row, lanes[t]] = turn_back(
                    value * HEAD_DIM**-0.5, low_row, high_row
                ).astype(B)
        rows = gk.shape[1]
        low = lax.broadcasted_iota(jnp.int32, (rows, 128), 1) < 64

        def fold(ref):
            both = [ref[s] + pltpu.roll(ref[s], 64, 1) for s in range(2)]
            return jnp.where(low, both[0], both[1])

        at = pl.multiple_of(i * 128, 128)
        gqkv[:, pl.ds(D + at, 128)] = turn_back(fold(gk), 0, rows).astype(B)
        gqkv[:, pl.ds(D + KVW + at, 128)] = fold(gv).astype(B)
        return 0

    h1a, ebd = c[N.h1a], c[N.ebd]
    lax.fori_loop(0, 3, tile, 0)
    c.send(N.gqkv)
    red = nt(gqkv[...], ebd[...]).astype(B)
    near[N.gred][...] = red
    c.send(N.gred)
    value = tn(red, h1a[:, :D])
    grow(N.qr, line, value, 0)
    grow(N.kr, line, value, 16)
    grow(N.vr, line, value, 32)
    value = tn(h1a[:, D:], gqkv[...])
    grow(N.qe, line, value[:, :D], 0)
    grow(N.ke, line, value[:, D : D + KVW], 16)
    grow(N.ve, line, value[:, D + KVW :], 32)
    hand_out(late, near[N.late])
    c.send(N.late)


def finish_body(c, pieces):
    near = c.near
    weight, out = near[N.weight], near[N.out]
    c.fetch(N.x, N.gqkv, N.gred, N.acat, N.gains)
    c.fetch_rows(N.wq, pieces, 0, D, weight)
    c.fetch_rows(N.wkv, pieces, D, 2 * KVW, weight, to=D)
    c.fetch(N.gx2)
    source = c[N.x][...].astype(F)
    scale = lax.rsqrt(jnp.mean(source * source, axis=1, keepdims=True) + eps)
    inner = jnp.zeros((source.shape[0], 1), F)
    gqkv = c[N.gqkv]
    c.wait(N.wq)
    for block in range(3):
        at = slice(block * 384, (block + 1) * 384)
        out[:, at] = nt(gqkv[:, :D], weight[at, :D]) + nn(c[N.gred][...], c[N.acat][:, at])
    c.wait(N.wkv)
    for block in range(3):
        at = slice(block * 384, (block + 1) * 384)
        value = out[:, at] + nt(gqkv[:, D:], weight[at, D:])
        value = value * c[N.gains][0:1, at]
        out[:, at] = value
        inner += jnp.sum(value * c[N.x][:, at].astype(F), axis=1, keepdims=True)
    inner = inner / D
    out[...] = c[N.gx2][...] + scale * out[...] - source * (scale * scale * scale) * inner
    c.send(N.out)


def after(value, *earlier):
    return lax.optimization_barrier((value, earlier))[0]


def swap(value, bit, what):
    with jax.named_scope(what):
        return lax.ppermute(value, N.shard, [(i, i ^ bit) for i in range(PARTS)])


def halves_kernel(y, x, y_out, x_out, sems):
    copies = [
        pltpu.make_async_copy(y.at[:, pl.ds(0, HALF)], y_out, sems.at[0]),
        pltpu.make_async_copy(x.at[:, pl.ds(HALF, HALF)], x_out, sems.at[1]),
    ]
    for copy in copies:
        copy.start()
    for copy in copies:
        copy.wait()


class Gather:
    def __init__(self):
        self.held = {}
        self.halves = {}
        self.last = None

    def links(self, n, message, *earlier):
        message = after(message, *earlier) if earlier else message
        self.held[n, 2] = swap(message, 2, "x%d" % n)
        self.held[n, 4] = swap(message, 4, "y%d" % n)

    def across(self, n, source, at, *earlier):
        value = self.held[source, at]
        value = after(value, *earlier) if earlier else value
        with jax.named_scope("z%d_%d" % (at, n)):
            pairs = [(i, i ^ 1) for i in range(lax.axis_size(N.rep))]
            self.held[n, at] = lax.ppermute(value, N.rep, pairs)

    def cut(self, n, *earlier):
        x, y = self.held[n, 2], self.held[n, 4]
        if earlier:
            x, y = after(x, *earlier), after(y, *earlier)
        self.halves[n] = call(
            halves_kernel,
            [((ROWS, HALF), B)] * 2,
            (y, x),
            spaces={0: pltpu.HBM, 1: pltpu.HBM},
            scratch=[pltpu.SemaphoreType.DMA((2,))],
            name=N.halves,
        )
        return self.halves[n]

    def corner(self, n, *earlier):
        if n in self.halves:
            y, x = (after(half, *earlier) for half in self.halves[n])
        else:
            y, x = self.cut(n, *earlier)
        self.held[n, 6] = swap(y, 2, "dx%d" % n)
        self.held[n, 8] = swap(x, 4, "dy%d" % n)

    def core(self, n, at, *earlier):
        value = after(self.held[n, at], *earlier) if earlier else self.held[n, at]
        self.held[n, at + 1] = swap(value, 1, "c%d_%d" % (at, n))

    def blocks(self, n):
        return [self.held[n, at] for at in (0, 1, 2, 3, 4, 5, 6, 8, 7, 9)]


def exchange(grads):
    count = PARTS * QUARTERS
    lanes = grads.shape[3]
    received = lax.all_to_all(grads.reshape(count, RANK, lanes), (N.rep, N.shard), 0, 0)
    return received.reshape(count * RANK, lanes)


def add_up(received, trees, slots):
    return call(
        add_up_kernel,
        [((received.shape[1], ADAPTERS * RANK), B)],
        (trees, slots, received),
        spaces={0: pltpu.SMEM, 1: pltpu.SMEM},
        name=N.add_up,
    )[0]


def add_up_kernel(trees, slots, received, out):
    chosen = choose(trees, slots, 0, PARTS * QUARTERS)
    out[...] = tn(received[...], chosen).astype(B)


def share(quarter):
    return [quarter] + [
        lax.ppermute(quarter, N.rep, [(i, i ^ step) for i in range(QUARTERS)])
        for step in range(1, QUARTERS)
    ]


def deliver_kernel(kinds, rep, *refs):
    refs = list(refs)
    take = lambda count: [refs.pop(0) for _ in range(count)]
    parts = [take(QUARTERS) for _ in kinds]
    outs = [take(len(names)) for names, _ in kinds]
    for (names, offsets), pieces, results, whole in zip(kinds, parts, outs, refs):
        rows = pieces[0].shape[0]
        for step, part in enumerate(pieces):
            at = pl.multiple_of((rep[0] ^ step) * rows, rows)
            whole[pl.ds(at, rows), :] = part[...].astype(F)
        for name, out in zip(names, results):
            out[...] = whole[offsets[name] : offsets[name] + SEG_ROWS[name], :]


def on_device(*args):
    x, cot, gain_a, gain_h = args[:4]
    weights = args[4:11]
    adapters = args[11:25]
    parents, device_tree, tree_adapter = args[25:]
    count = lax.axis_size(N.shard)
    shard = lax.axis_index(N.shard)
    group = lax.axis_index(N.rep) * count
    rows = x.shape[0]
    direct = count == PARTS and lax.axis_size(N.rep) == QUARTERS

    if direct:
        parity = lax.axis_index(N.rep) % 2
        gather = Gather()
        held = gather.held
        facts = jnp.stack([group, parity]).astype(jnp.int32)
        held[1, 0], held[0, 0], sent = call(
            pack_first_kernel,
            [((ROWS, MSG), B), ((ROWS, MSG), B), ((PARTS * RANK, LANES), B)],
            (facts, device_tree, tree_adapter, *weights, gain_a, gain_h, *adapters),
            spaces={
                **{n: pltpu.SMEM for n in range(3)},
                **{n: pltpu.HBM for n in range(3, 10)},
            },
            scratch=[
                pltpu.VMEM((PARTS * RANK, LANES), F),
                pltpu.SemaphoreType.DMA((SLICE_COPIES + 4,)),
            ],
            name=N.pack_first,
        )
        held[2, 0], held[3, 0] = pack_slices((1 - parity, 2), weights[4:])
        pos = jnp.bitwise_xor(shard, jnp.arange(PARTS, dtype=jnp.int32))
        pos = jnp.concatenate([pos, jnp.full((PARTS,), parity)]).astype(jnp.int32)
        packed = lax.all_to_all(sent.reshape(PARTS, RANK, LANES), N.shard, 0, 0)
        gather.links(1, held[1, 0])
        gather.links(0, held[0, 0])
        for n in range(4):
            gather.core(n, 0)
        first_halves = gather.cut(1)
        early_on = [held[n, 1] for n in range(4)] + list(first_halves)
        for at in (2, 4):
            gather.across(2, 1, at, held[1, 2], held[1, 4], *early_on)
        gather.corner(0, held[0, 2], held[0, 4], held[2, 2], *first_halves)
    else:
        whole = [lax.all_gather(w, N.shard, axis=0, tiled=True) for w in weights]
        cut = lambda w, j: lax.slice_in_dim(
            w, j * (w.shape[0] // PARTS), (j + 1) * (w.shape[0] // PARTS)
        )
        attention = [pack_attention([cut(w, j) for w in whole[:4]]) for j in range(PARTS)]
        hidden = [
            pack_slices(range(SLICES), [cut(w, j) for w in whole[4:]]) for j in range(PARTS)
        ]
        blocks = [attention] + [[hidden[j][f] for j in range(PARTS)] for f in range(SLICES)]
        blocks = [
            [b[m][:, low:high] if high - low < MSG else b[m] for m, low, high in HELD]
            for b in blocks
        ]
        pos = jnp.arange(PARTS, dtype=jnp.int32)
        pos = jnp.concatenate([pos, jnp.zeros_like(pos)])
        offset = tree_adapter[device_tree[group + shard]] * RANK
        segments = {}
        for name, part in zip(NAMES, adapters):
            full = lax.all_gather(part, N.shard, axis=0, tiled=True)
            own = lax.dynamic_slice_in_dim(full, offset, RANK, 1)
            segments[name] = own.reshape(PARTS, -1, RANK).transpose(0, 2, 1)
        both = jnp.stack(
            [lax.all_gather(g, N.shard, axis=0, tiled=True) for g in (gain_a, gain_h)]
        )
        both = both.reshape(2, PARTS, ROWS).transpose(1, 0, 2)
        segments[N.gain] = jnp.pad(both, ((0, 0), (0, RANK - 2), (0, 0)))
        packed = jnp.concatenate([segments[name] for name in OFF], axis=2)
        packed = jnp.pad(packed, ((0, 0), (0, 0), (0, LANES - packed.shape[2])))

    allowed, positions = tree_layout(parents[0], rows)
    bias = jnp.where(allowed, 0.0, -1e30).astype(F)
    cosine, sine = rope_tables(positions)
    ready = launch(
        N.prepare,
        prepare_body,
        dict(
            acat=((128, D), B),
            ebd=((128, QKV), B),
            ao=((128, D), B),
            eo=((128, D), B),
            agu=((128, D), B),
            ed=((128, D), B),
            egu=((SLICES, 128, 2 * SL), B),
            ad=((SLICES, SL, 128), B),
            gains=((RANK, D), F),
            h1a=((rows, WIDE), B),
            cota=((rows, WIDE), B),
        ),
        dict(packed=packed, x=x, cot=cot),
        scratch=dict(line=((RANK, D), F), wide=((PARTS, RANK, LANES), F)),
    )
    if direct:
        gather.corner(1, held[0, 2], held[0, 4], held[2, 2], ready[N.h1a], bias, cosine, sine)
        for at in (2, 4):
            gather.core(0, at, ready[N.h1a], bias, cosine, sine)
        for at in (6, 8):
            gather.core(0, at)
        blocks = [gather.blocks(0)]
    tables = dict(bias=bias, cosine=cosine, sine=sine)
    some = lambda *names: {name: ready[name] for name in names}
    front = launch(
        N.project,
        project_body,
        dict(q=((rows, D), B), kd=((rows, 2 * KVW), B), vd=((rows, 2 * KVW), B)),
        dict(cosine=cosine, sine=sine, **some(N.h1a, N.ebd)),
        blocks[0],
        pos,
        scratch=dict(weight=((WIDE, QKV), B)),
    )
    if direct:
        ahead = [front[N.q], held[1, 6], held[1, 8], held[2, 4]]
        gather.links(3, held[3, 0], *ahead)
        for at in (6, 8):
            gather.across(2, 1, at, *ahead)
    front.update(
        launch(
            N.attend,
            attend_body,
            dict(
                oa=((rows, WIDE), B),
                lse=((3, 2, rows, 128), F),
                x2=((rows, D), F),
                h2a=((rows, WIDE), B),
            ),
            dict(x=x, bias=bias, **front, **some(N.ao, N.eo, N.agu, N.gains)),
            blocks[0],
            pos,
            scratch=dict(wout=((WIDE, D), B)),
        )
    )
    h2a, x2 = front[N.h2a], front[N.x2]
    if direct:
        both = [held[3, at] for at in (2, 4)]
        gather.corner(3, h2a, *both)
        for n in (1, 2):
            for at in (2, 4, 6, 8):
                gather.core(n, at, h2a, *both)
    state = None
    for slices in RUNS:
        first, last = slices[0] == 0, slices[-1] == SLICES - 1
        if direct:
            if last:
                for at in (2, 4, 6, 8):
                    gather.core(3, at, state[N.early])
            for f in slices:
                if len(blocks) < f + 2:
                    blocks.append(gather.blocks(1 + f))
        ins = dict(h2a=h2a, **some(N.cota, N.egu, N.ad))
        count = len(slices)
        scratch = dict(
            wgu=((count, WIDE, 2 * SL), B),
            wd=((count, SL, WIDE), B),
            tail=((count, PARTS * 16, SL), B),
            mid=((rows, SL), B),
            ggt=((rows, SL), B),
            gup=((rows, SL), B),
            line=((RANK, D), F),
        )
        scratch.update(
            y_acc=((rows, WIDE), F),
            g_acc=((rows, WIDE), F),
            early_acc=((PARTS, RANK, EARLY_LANES), F),
        )
        outs = dict(
            y=((rows, WIDE), B), g=((rows, WIDE), B), early=((PARTS, RANK, EARLY_LANES), B)
        )
        if not first:
            ins.update(y_in=state[N.y], g_in=state[N.g], early_in=state[N.early])
        if last:
            ins.update(x2=x2, **some(N.agu, N.ed))
            outs = dict(
                y=((rows, D), B),
                g=((rows, D), F),
                early=((QUARTERS, PARTS, RANK, EARLY_LANES // QUARTERS), B),
            )
        state = launch(
            "hidden_%d" % slices[0],
            functools.partial(hidden_body, slices),
            outs,
            ins,
            [piece for f in slices for piece in blocks[1 + f]],
            pos,
            scratch,
            sems=64 + 80 * count,
        )
    layer_output, gh2, early = state[N.y], state[N.g], state[N.early]
    if direct:
        early_come = exchange(early)
    operands = dict(gh2=gh2, x2=x2, cot=cot, **tables, **some(N.ao, N.eo, N.gains, N.h1a, N.ebd))
    operands.update({name: front[name] for name in (N.q, N.kd, N.vd, N.oa, N.lse)})
    back = launch(
        N.back,
        back_body,
        dict(
            gx2=((rows, D), F),
            gqkv=((rows, QKV), B),
            gred=((rows, 128), B),
            late=((QUARTERS, PARTS, RANK, LATE_LANES // QUARTERS), B),
        ),
        operands,
        blocks[0],
        pos,
        dict(
            weight=((WIDE, D), B),
            go=((rows, D), B),
            gk=((2, rows, 128), F),
            gv=((2, rows, 128), F),
            line=((RANK, D), F),
            late_acc=((PARTS, RANK, LATE_LANES), F),
        ),
    )
    late = back[N.late]
    if direct:
        early_come, late = lax.optimization_barrier((early_come, late))
        late_come = exchange(late)
        early_parts = share(add_up(early_come, device_tree, tree_adapter))
        late_quarter = add_up(late_come, device_tree, tree_adapter)
    input_grad = launch(
        N.finish,
        finish_body,
        dict(out=((rows, D), F)),
        dict(
            x=x, gx2=back[N.gx2], gqkv=back[N.gqkv], gred=back[N.gred], **some(N.acat, N.gains)
        ),
        blocks[0],
        pos,
        dict(weight=((D, QKV), B)),
    )[N.out]
    owned = {}
    kinds = ((EARLY, EARLY_OFF), (LATE, LATE_OFF))
    if direct:
        rep = lax.axis_index(N.rep).astype(jnp.int32).reshape(1)
        late_parts = share(late_quarter)
        received = call(
            functools.partial(deliver_kernel, kinds),
            [((SEG_ROWS[name], ADAPTERS * RANK), F) for name in EARLY + LATE],
            (rep, *early_parts, *late_parts),
            spaces={0: pltpu.SMEM},
            scratch=[
                pltpu.VMEM((QUARTERS * parts[0].shape[0], ADAPTERS * RANK), F)
                for parts in (early_parts, late_parts)
            ],
            name=N.deliver,
        )
        owned.update(zip(EARLY + LATE, received))
    else:
        for grads, (names, offsets) in zip((early, late), kinds):
            grads = grads.transpose(1, 2, 0, 3).reshape(PARTS, RANK, -1)
            for name in names:
                part = grads[:, :, offsets[name] : offsets[name] + SEG_ROWS[name]]
                part = part.transpose(0, 2, 1).reshape(-1, RANK)
                wide = lax.dynamic_update_slice_in_dim(
                    jnp.zeros((part.shape[0], ADAPTERS * RANK), B), part, offset, 1
                )
                wide = lax.psum_scatter(wide, N.shard, scatter_dimension=0, tiled=True)
                owned[name] = lax.psum(wide, N.rep).astype(F)
    return (layer_output, input_grad) + tuple(owned[name] for name in NAMES)


def solution(mesh):
    token = P((N.rep, N.shard), None)
    row = P(N.shard, None)
    return jax.shard_map(
        on_device,
        mesh=mesh,
        in_specs=(token, token, P(N.shard), P(N.shard)) + (row,) * 21 + (token, P(), P()),
        out_specs=(token, token) + (row,) * 14,
        check_vma=False,
    )
```

```python
import functools

import jax
import jax.numpy as jnp
from jax import lax
from jax.experimental import pallas as pl
from jax.experimental.pallas import tpu as pltpu
from jax.sharding import PartitionSpec as P

D = 1152
Q_HEADS = 18
KV_HEADS = 6
HEAD_DIM = 64
FF = 3072
RANK = 16
ADAPTERS = 8
TRUNK = 128
BRANCH = 24
LEAF = 24
KVW = 384
PARTS = 8
ROWS = D // PARTS
FROWS = FF // PARTS
SLICES = 3
SL = FF // SLICES
WIDE = D + 128
QKV = D + 2 * KVW
MSG = 3072
eps = 1e-05
F = jnp.float32
B = jnp.bfloat16


class Words:
    def __getattr__(self, word):
        return word


N = Words()
VMEM_LIMIT = 58 * 1024 * 1024

NAMES = (N.qr, N.qe, N.kr, N.ke, N.vr, N.ve, N.wr, N.oe, N.gr, N.ge, N.ur, N.ue, N.dr, N.de)
SEG_ROWS = {name: ROWS for name in NAMES}
SEG_ROWS.update(ke=KVW // PARTS, ve=KVW // PARTS, ge=FROWS, ue=FROWS, dr=FROWS)


SEG_ROWS[N.gain] = ROWS
EARLY = (N.ge, N.ue, N.dr, N.gr, N.ur, N.de)
LATE = (N.wr, N.oe, N.qr, N.qe, N.kr, N.ke, N.vr, N.ve)
QUARTERS = 4


def lay_out(names, unit):
    offsets = {}
    total = 0
    for name in names:
        offsets[name] = total
        total += SEG_ROWS[name]
    return offsets, -(-total // unit) * unit


EARLY_OFF, EARLY_LANES = lay_out(EARLY, QUARTERS * 128)
LATE_OFF, LATE_LANES = lay_out(LATE, QUARTERS * 128)
OFF, LANES = lay_out(EARLY + LATE + (N.gain,), 128)
BLOCKS = ((0, 128, 128), (128, 224, 256), (224, 416, 416))


def nn(left, right):
    return lax.dot_general(left, right, (((1,), (0,)), ((), ())), preferred_element_type=F)


def nt(left, right):
    return lax.dot_general(left, right, (((1,), (1,)), ((), ())), preferred_element_type=F)


def tn(left, right):
    return lax.dot_general(left, right, (((0,), (0,)), ((), ())), preferred_element_type=F)


RUNS = ((0, 1), (2,))
COST = dict(flops=1 << 20, bytes_accessed=1 << 16, transcendentals=0)


def call(kernel, out_shape, args, spaces=None, scratch=(), name=None):
    in_specs = [
        pl.BlockSpec(memory_space=(spaces or {}).get(i, pltpu.VMEM)) for i in range(len(args))
    ]
    return pl.pallas_call(
        kernel,
        out_shape=[jax.ShapeDtypeStruct(s, d) for s, d in out_shape],
        in_specs=in_specs,
        out_specs=[pl.BlockSpec(memory_space=pltpu.VMEM) for _ in out_shape],
        scratch_shapes=list(scratch),
        compiler_params=pltpu.CompilerParams(vmem_limit_bytes=VMEM_LIMIT),
        cost_estimate=pl.CostEstimate(**COST),
        name=name,
    )(*args)


class Frame:
    def __init__(self, pos, near, far, outs, sems):
        self.pos, self.near, self.far, self.outs, self.sems = pos, near, far, outs, sems
        self.used = 0
        self.coming = {}
        self.leaving = []

    def copy(self, source, target):
        moved = pltpu.make_async_copy(source, target, self.sems.at[self.used])
        self.used += 1
        moved.start()
        return moved

    def fetch(self, *names):
        for name in names:
            self.coming[name] = [self.copy(self.far[name], self.near[name])]

    def fetch_into(self, key, source, target):
        self.coming.setdefault(key, []).append(self.copy(source, target))

    def fetch_rows(self, key, pieces, low, lanes, target, rows=ROWS, start=0, to=0):
        for piece, (m, begin, end) in zip(pieces, HELD):
            a, b = max(low, begin), min(low + lanes, end)
            if a < b:
                self.fetch_into(
                    key,
                    piece.at[pl.ds(start, rows), pl.ds(a - begin, b - a)],
                    target.at[row_at(self.pos, m, rows), pl.ds(to + a - low, b - a)],
                )

    def wait(self, *keys):
        for key in keys:
            for moved in self.coming.pop(key, ()):
                moved.wait()

    def __getitem__(self, name):
        self.wait(name)
        return self.near[name]

    def send(self, name, at=None):
        near, far = self.near[name], self.outs[name]
        if at is not None:
            near, far = near.at[:, at], far.at[:, at]
        self.leaving.append(self.copy(near, far))

    def close(self):
        for moved in self.leaving:
            moved.wait()


def launch(
    name, body, outs, ins, pieces=(), pos=None, scratch=None, sems=64, weigh=None
):
    scratch = scratch or {}
    operands = ([] if pos is None else [pos]) + list(ins.values()) + list(pieces)

    def kernel(*refs):
        refs = list(refs)
        take = lambda count: [refs.pop(0) for _ in range(count)]
        where = None if pos is None else take(1)[0]
        far = dict(zip(ins, take(len(ins))))
        parts = take(len(pieces))
        results = dict(zip(outs, take(len(outs))))
        near = dict(zip(ins, take(len(ins))))
        near.update(zip(outs, take(len(outs))))
        near.update(zip(scratch, take(len(scratch))))
        frame = Frame(where, near, far, results, refs[0])
        body(frame, parts)
        frame.close()

    hbm = pl.BlockSpec(memory_space=pltpu.HBM)
    specs = [hbm] * (len(ins) + len(pieces))
    if pos is not None:
        specs = [pl.BlockSpec(memory_space=pltpu.SMEM)] + specs
    results = pl.pallas_call(
        kernel,
        out_shape=[jax.ShapeDtypeStruct(s, d) for s, d in outs.values()],
        in_specs=specs,
        out_specs=[hbm] * len(outs),
        scratch_shapes=[pltpu.VMEM(v.shape, v.dtype) for v in ins.values()]
        + [pltpu.VMEM(s, d) for s, d in outs.values()]
        + [pltpu.VMEM(s, d) for s, d in scratch.values()]
        + [pltpu.SemaphoreType.DMA((sems,))],
        compiler_params=pltpu.CompilerParams(vmem_limit_bytes=VMEM_LIMIT),
        cost_estimate=pl.CostEstimate(**(weigh or COST)),
        name=name,
    )(*operands)
    return dict(zip(outs, results))


def tree_layout(parents_row, row_count):
    index = jnp.arange(row_count, dtype=jnp.int32)
    after = index - TRUNK
    leaf_start = TRUNK + 4 * BRANCH
    in_branch = (index >= TRUNK) & (index < leaf_start)
    in_leaf = index >= leaf_start
    segment = jnp.where(
        in_leaf, 5 + (index - leaf_start) // LEAF, jnp.where(in_branch, 1 + after // BRANCH, 0)
    )
    positions = jnp.where(
        in_leaf,
        TRUNK + BRANCH + (index - leaf_start) % LEAF,
        jnp.where(in_branch, TRUNK + after % BRANCH, index),
    )
    numbers = jnp.arange(13, dtype=jnp.int32)
    parent = jnp.sum(
        jnp.where(segment[:, None] == numbers[None, :], parents_row[None, :], 0), axis=1
    )
    grand = jnp.sum(jnp.where(parent[:, None] == numbers[None, :], parents_row[None, :], 0), axis=1)
    same = (segment[:, None] == segment[None, :]) & (index[None, :] <= index[:, None])
    above = (segment[:, None] != 0) & (
        (segment[None, :] == parent[:, None]) | (segment[None, :] == grand[:, None])
    )
    return (same | above, positions)


def rope_tables(positions):
    halfway = HEAD_DIM // 2
    frequency = 10000.0 ** (-jnp.arange(halfway, dtype=F) / halfway)
    angles = positions.astype(F)[:, None] * frequency[None, :]
    cosine, sine = jnp.cos(angles), jnp.sin(angles)
    return (
        jnp.concatenate([cosine] * 4, axis=1),
        jnp.concatenate([-sine, sine, -sine, sine], axis=1),
    )


def attention_copies(weights, out):
    copies = []
    at = 0
    for weight in weights:
        copies.append((weight, out.at[:, pl.ds(at, weight.shape[1])]))
        at += weight.shape[1]
    return copies


def slice_copies(f, g, u, d, out):
    at = pl.multiple_of(f * 128, 128)
    copies = []
    for s in range(PARTS):
        lanes = pl.ds(pl.multiple_of(s * FROWS + at, 128), 128)
        copies.append((g.at[:, lanes], out.at[:, pl.ds(s * 128, 128)]))
        copies.append((u.at[:, lanes], out.at[:, pl.ds(SL + s * 128, 128)]))
    copies.append(
        (d.at[pl.ds(at, 128), pl.ds(0, SL)], out.at[pl.ds(0, 128), pl.ds(2 * SL, SL)])
    )
    for b in range(8):
        rows = pl.ds(pl.multiple_of(at + b * 16, 16), 16)
        copies.append(
            (
                d.at[rows, pl.ds(SL, 128)],
                out.at[pl.ds(128, 16), pl.ds(2 * SL + b * 128, 128)],
            )
        )
    return copies


def start_all(copies, sems, first=0):
    moved = [
        pltpu.make_async_copy(source, target, sems.at[first + k])
        for k, (source, target) in enumerate(copies)
    ]
    for copy in moved:
        copy.start()
    return moved


SLICE_COPIES = 2 * PARTS + 9


def pack_attention_kernel(q, k, v, o, out, sems):
    for copy in start_all(attention_copies((q, k, v, o), out), sems):
        copy.wait()


def pack_slices_kernel(numbers, g, u, d, *refs):
    outs, sems = refs[:-1], refs[-1]
    moved = []
    for n, out in enumerate(outs):
        moved += start_all(slice_copies(numbers[n], g, u, d, out), sems, n * SLICE_COPIES)
    for copy in moved:
        copy.wait()


def pack_attention(weights):
    return call(
        pack_attention_kernel,
        [((ROWS, MSG), B)],
        weights,
        spaces={n: pltpu.HBM for n in range(4)},
        scratch=[pltpu.SemaphoreType.DMA((4,))],
        name=N.pack_attention,
    )[0]


def pack_slices(numbers, weights):
    numbers = jnp.stack([jnp.asarray(f, jnp.int32) for f in numbers])
    return call(
        pack_slices_kernel,
        [((ROWS, MSG), B)] * numbers.shape[0],
        (numbers, *weights),
        spaces={0: pltpu.SMEM, 1: pltpu.HBM, 2: pltpu.HBM, 3: pltpu.HBM},
        scratch=[pltpu.SemaphoreType.DMA((numbers.shape[0] * SLICE_COPIES,))],
        name=N.pack_slices,
    )


def choose(trees, slots, first, count):
    column = lax.broadcasted_iota(jnp.int32, (RANK, ADAPTERS * RANK), 1)
    row = lax.broadcasted_iota(jnp.int32, (RANK, ADAPTERS * RANK), 0)
    parts = [
        jnp.where(column == slots[trees[first + d]] * RANK + row, 1.0, 0.0) for d in range(count)
    ]
    return jnp.concatenate(parts, axis=0).astype(B)


def pack_first_kernel(facts, trees, slots, *refs):
    weights, gains, parts = refs[:7], refs[7:9], refs[9:23]
    first, attention, out, wide, sems = refs[23:]
    moved = start_all(slice_copies(facts[1], *weights[4:], first), sems)
    moved += start_all(attention_copies(weights[:4], attention), sems, SLICE_COPIES)
    chosen = choose(trees, slots, facts[0], PARTS)
    for name, part in zip(NAMES, parts):
        wide[:, OFF[name] : OFF[name] + SEG_ROWS[name]] = nt(chosen, part[...])
    row = lax.broadcasted_iota(jnp.int32, (RANK, ROWS), 0)
    both = jnp.where(
        row == 0,
        gains[0][...].astype(F).reshape(1, ROWS),
        jnp.where(row == 1, gains[1][...].astype(F).reshape(1, ROWS), 0.0),
    )
    for d in range(PARTS):
        wide[d * RANK : (d + 1) * RANK, OFF[N.gain] : OFF[N.gain] + ROWS] = both
    out[...] = wide[...].astype(B)
    for copy in moved:
        copy.wait()


HALF = MSG // 2
HELD = [(m, 0, MSG) for m in range(6)] + [
    (m, low, low + HALF) for m in (6, 7) for low in (0, HALF)
]
HELD_COUNT = len(HELD)


def row_at(pos, m, rows):
    return pl.ds(pl.multiple_of(pos[m] * rows, rows), rows)


def swap_halves(value, first):
    return jnp.where(first, pltpu.roll(value, 96, 1), pltpu.roll(value, 32, 1))


def half_masks():
    lane = lax.broadcasted_iota(jnp.int32, (1, 128), 1)
    low = jnp.where(lane < 64, 1.0, 0.0)
    return low, 1.0 - low


def prepare_body(c, _):
    c.fetch(N.x, N.cot, N.packed)
    near = c.near
    for name in (N.acat, N.ebd, N.ao, N.eo, N.agu, N.ed, N.egu):
        near[name][...] = jnp.zeros(near[name].shape, B)
    source = c[N.x][...].astype(F)
    scale = lax.rsqrt(jnp.mean(source * source, axis=1, keepdims=True) + eps)
    wide = near[N.wide]
    wide[...] = c[N.packed][...].astype(F)
    line = near[N.line]

    def rows_of(name, width=None, start=0):
        rows = SEG_ROWS[name] if width is None else width
        low = OFF[name] + start
        for j in range(PARTS):
            line[:, j * rows : (j + 1) * rows] = wide[j, :, low : low + rows]
        return line[:, : PARTS * rows]

    near[N.gains][...] = rows_of(N.gain)
    acat = near[N.acat]
    acat[:16, :] = rows_of(N.qr).astype(B)
    acat[16:32, :] = rows_of(N.kr).astype(B)
    acat[32:48, :] = rows_of(N.vr).astype(B)
    near[N.ed][:16, :] = rows_of(N.de).astype(B)
    h1 = (source * scale * near[N.gains][0:1, :]).astype(B)
    near[N.h1a][:, :D] = h1
    near[N.h1a][:, D:] = nt(h1, acat[...]).astype(B)
    near[N.cota][:, :D] = c[N.cot][...]
    near[N.cota][:, D:] = nt(c[N.cot][...], near[N.ed][...]).astype(B)
    ebd, agu, egu = near[N.ebd], near[N.agu], near[N.egu]
    ebd[:16, :D] = rows_of(N.qe).astype(B)
    ebd[16:32, D : D + KVW] = rows_of(N.ke).astype(B)
    ebd[32:48, D + KVW :] = rows_of(N.ve).astype(B)
    for name in (N.h1a, N.cota, N.acat, N.ebd, N.gains, N.ed):
        c.send(name)
    near[N.ao][:16, :] = rows_of(N.wr).astype(B)
    near[N.eo][:16, :] = rows_of(N.oe).astype(B)
    agu[:16, :] = rows_of(N.gr).astype(B)
    agu[16:32, :] = rows_of(N.ur).astype(B)
    for name in (N.ao, N.eo, N.agu):
        c.send(name)
    for f in range(SLICES):
        egu[f, :16, :SL] = rows_of(N.ge, 128, f * 128).astype(B)
        egu[f, 16:32, SL:] = rows_of(N.ue, 128, f * 128).astype(B)
        down = rows_of(N.dr, 128, f * 128)
        near[N.ad][f] = jnp.concatenate([down, jnp.zeros((112, SL), F)], axis=0).T.astype(B)
    c.send(N.egu)
    c.send(N.ad)


def project_body(c, pieces):
    near = c.near
    weight = near[N.weight]
    c.fetch(N.h1a)
    c.fetch_rows(N.w0, pieces, 0, 768, weight)
    c.fetch_into(N.w0, c.far[N.ebd], weight.at[pl.ds(D, 128), :])
    c.fetch(N.cosine, N.sine)
    c.fetch_rows(N.w1, pieces, 768, QKV - 768, weight, to=768)
    h1a = c[N.h1a]
    rows = h1a.shape[0]
    lane = lax.broadcasted_iota(jnp.int32, (rows, 128), 1)
    low, first = lane < 64, lane % 64 < 32
    q, kd, vd = near[N.q], near[N.kd], near[N.vd]
    c.wait(N.w0)
    for block in range(5):
        if block == 2:
            c.wait(N.w1)
        value = nn(h1a[...], weight[:, block * 384 : (block + 1) * 384])
        for t in range(3):
            part = value[:, t * 128 : (t + 1) * 128]
            if block < 4:
                part = part * c[N.cosine][...] + swap_halves(part, first) * c[N.sine][...]
            if block < 3:
                at = block * 384 + t * 128
                q[:, at : at + 128] = (part * HEAD_DIM**-0.5).astype(B)
            else:
                out = kd if block == 3 else vd
                rolled = pltpu.roll(part, 64, 1)
                out[:, t * 256 : t * 256 + 128] = jnp.where(low, part, rolled).astype(B)
                out[:, t * 256 + 128 : (t + 1) * 256] = jnp.where(low, rolled, part).astype(B)
    for name in (N.q, N.kd, N.vd):
        c.send(name)


def attend_body(c, pieces):
    near = c.near
    wout = near[N.wout]
    c.fetch(N.q, N.kd, N.bias, N.vd)
    c.fetch_rows(N.wout, pieces, QKV, D, wout)
    c.fetch_into(N.wout, c.far[N.eo], wout.at[pl.ds(D, 128), :])
    c.fetch(N.x, N.ao, N.agu, N.gains)
    q, kd, vd = c[N.q], c[N.kd], c[N.vd]
    rows = q.shape[0]
    masks = [mask.astype(B) for mask in half_masks()]
    bias, oa, lse, x2, h2a = c[N.bias], near[N.oa], near[N.lse], near[N.x2], near[N.h2a]

    def tile(i, _):
        lanes = [pl.ds(pl.multiple_of((3 * i + t) * 128, 128), 128) for t in range(3)]
        outs = {}
        for side in range(2):
            group = pl.ds(pl.multiple_of((2 * i + side) * 128, 128), 128)
            values = vd[:, group] * masks[0] + masks[1]
            for block, (low_row, high_row, keys) in enumerate(BLOCKS):
                count = high_row - low_row
                heads = [divmod(3 * side + slot, 2) for slot in range(3)]
                query = jnp.concatenate(
                    [q[low_row:high_row, lanes[t]] * masks[half] for t, half in heads], axis=0
                )
                scores = nt(query, kd[:keys, group]).reshape(3, count, keys)
                scores = (scores + bias[low_row:high_row, :keys][None]).reshape(3 * count, keys)
                top = jnp.max(scores, axis=1, keepdims=True)
                result = nn(jnp.exp(scores - top).astype(B), values[:keys])
                summed = result[:, 64:65]
                result = result * (1.0 / summed)
                total = top + jnp.log(summed)
                lane = lax.broadcasted_iota(jnp.int32, (count, 128), 1)
                split = lambda v, slot: v[slot * count : (slot + 1) * count]
                lse[i, side, low_row:high_row, :] = jnp.where(
                    lane == 0,
                    split(total, 0),
                    jnp.where(lane == 1, split(total, 1), split(total, 2)),
                )
                for slot in range(3):
                    outs[block, 3 * side + slot] = split(result, slot)
        for block, (low_row, high_row, _) in enumerate(BLOCKS):
            lane = lax.broadcasted_iota(jnp.int32, (high_row - low_row, 128), 1)
            for t in range(3):
                oa[low_row:high_row, lanes[t]] = jnp.where(
                    lane < 64, outs[block, 2 * t], pltpu.roll(outs[block, 2 * t + 1], 64, 1)
                ).astype(B)
        return 0

    lax.fori_loop(0, 3, tile, 0)
    c.send(N.lse)
    oa[:, D:] = nt(oa[:, :D], c[N.ao][...]).astype(B)
    c.send(N.oa)
    c.wait(N.wout)
    square = jnp.zeros((rows, 1), F)
    for block in range(3):
        at = slice(block * 384, (block + 1) * 384)
        value = c[N.x][:, at].astype(F) + nn(oa[...], wout[:, at])
        x2[:, at] = value
        square += jnp.sum(value * value, axis=1, keepdims=True)
    c.send(N.x2)
    scale = lax.rsqrt(square / D + eps)
    h2a[:, :D] = (x2[...] * scale * c[N.gains][1:2, :]).astype(B)
    h2a[:, D:] = nt(h2a[:, :D], c[N.agu][...]).astype(B)
    c.send(N.h2a)


def put(grads, offsets, name, line, value, row, width=None, start=0):
    width = SEG_ROWS[name] if width is None else width
    line[:, : PARTS * width] = value[row : row + RANK, :]
    for j in range(PARTS):
        at = pl.ds(offsets[name] + start, width)
        if not isinstance(start, int):
            at = pl.ds(pl.multiple_of(offsets[name] + start, 128), width)
        grads[j, :, at] = line[:, j * width : (j + 1) * width]


def hand_out(grads, out):
    part = out.shape[3]
    for q in range(QUARTERS):
        out[q] = grads[:, :, q * part : (q + 1) * part].astype(B)


def hidden_body(slices, c, pieces):
    first, last = slices[0] == 0, slices[-1] == SLICES - 1
    near = c.near
    mid, ggt, gup, line = near[N.mid], near[N.ggt], near[N.gup], near[N.line]
    c.fetch(N.h2a)
    number = [c.pos[PARTS], 1 - c.pos[PARTS]] if first else slices
    for n, f in enumerate(slices):
        wgu, wd, tail = near[N.wgu].at[n], near[N.wd].at[n], near[N.tail].at[n]
        own = pieces[n * HELD_COUNT : (n + 1) * HELD_COUNT]
        for part in range(2):
            for side in range(2):
                at = side * SL + part * 512
                c.fetch_rows((N.gu, f, part), own, at, 512, wgu, to=at)
            if part == 0:
                c.fetch_into((N.gu, f, 0), c.far[N.egu].at[number[n]], wgu.at[pl.ds(D, 128), :])
                if n == 0:
                    c.fetch(N.cota)
                c.fetch_rows((N.wd, f), own, 2 * SL, SL, wd, 128)
                c.fetch_rows((N.wd, f), own, 2 * SL, SL, tail, 16, 128)
                c.fetch_into((N.wd, f), c.far[N.ad].at[number[n]], wd.at[:, pl.ds(D, 128)])
    if not first:
        c.fetch(N.y_in, N.g_in, N.early_in)
    if last:
        c.fetch(N.x2, N.agu, N.ed)
    h2a = c[N.h2a]
    y_acc, g_acc, early = near[N.y_acc], near[N.g_acc], near[N.early_acc]
    grow = functools.partial(put, early, EARLY_OFF)
    lanes = slice(D, WIDE)
    for n, f in enumerate(slices):
        wgu, wd, tail = near[N.wgu].at[n], near[N.wd].at[n], near[N.tail].at[n]
        for k in range(SL // 256):
            at = slice(k * 256, (k + 1) * 256)
            if k % 2 == 0:
                c.wait((N.gu, f, k // 2))
            gate = nn(h2a[...], wgu[:, at])
            up = nn(h2a[...], wgu[:, SL + k * 256 : SL + (k + 1) * 256])
            sig = jax.nn.sigmoid(gate)
            silu = gate * sig
            if k == 0:
                cota = c[N.cota]
                c.wait((N.wd, f))
                for m in range(PARTS):
                    for b in range(8):
                        wd[m * 128 + b * 16 : m * 128 + (b + 1) * 16, SL:D] = tail[
                            m * 16 : (m + 1) * 16, b * 128 : (b + 1) * 128
                        ]
            gmid = nt(cota[...], wd[at, :])
            mid[:, at] = (silu * up).astype(B)
            ggt[:, at] = (gmid * up * sig * (1.0 + gate * (1.0 - sig))).astype(B)
            gup[:, at] = (gmid * silu).astype(B)
        for k in range(5):
            at = slice(k * 256, (k + 1) * 256)
            value = nn(mid[...], wd[:, at])
            if n:
                value += y_acc[:, at]
            elif not first:
                value += c[N.y_in][:, at].astype(F)
            if last or n < len(slices) - 1:
                y_acc[:, at] = value
            else:
                near[N.y][:, at] = value.astype(B)
            value = nt(ggt[...], wgu[at, :SL]) + nt(gup[...], wgu[at, SL:])
            if n:
                value += g_acc[:, at]
            elif not first:
                value += c[N.g_in][:, at].astype(F)
            if last or n < len(slices) - 1:
                g_acc[:, at] = value
            else:
                near[N.g][:, at] = value.astype(B)
            if not last and n == len(slices) - 1:
                c.send(N.y, at)
                c.send(N.g, at)
        if n == 0:
            early[...] = jnp.zeros(early.shape, F) if first else c[N.early_in][...].astype(F)
        grow(N.ge, line, tn(h2a[:, lanes], ggt[...]), 0, 128, number[n] * 128)
        grow(N.ue, line, tn(h2a[:, lanes], gup[...]), 16, 128, number[n] * 128)
        grow(N.dr, line, tn(cota[:, lanes], mid[...]), 0, 128, number[n] * 128)
    if last:
        red = g_acc[:, lanes].astype(B)
        near[N.g][...] = g_acc[:, :D] + nn(red, c[N.agu][...])
        c.send(N.g)
        down_red = y_acc[:, lanes].astype(B)
        grow(N.de, line, tn(down_red, cota[:, :D]), 0)
        value = tn(red, h2a[:, :D])
        grow(N.gr, line, value, 0)
        grow(N.ur, line, value, 16)
        hand_out(early, near[N.early])
        c.send(N.early)
        near[N.y][...] = (y_acc[:, :D] + c[N.x2][...] + nn(down_red, c[N.ed][...])).astype(B)
        c.send(N.y)
    else:
        near[N.early][...] = early[...].astype(B)
        c.send(N.early)


def back_body(c, pieces):
    near, far = c.near, c.far
    c.fetch(N.gh2, N.x2, N.gains, N.cot)
    weight, gx2, go, late, line = (near[k] for k in (N.weight, N.gx2, N.go, N.late_acc, N.line))
    c.fetch_into(N.eo, far[N.eo], weight.at[pl.ds(D, 128), :])
    c.fetch_rows(N.weight, pieces, QKV, D, weight)
    c.fetch(N.ao, N.oa, N.bias, N.q, N.kd, N.vd, N.lse, N.cosine, N.sine, N.h1a, N.ebd)
    late[...] = jnp.zeros(late.shape, F)
    residual = c[N.x2][...]
    scale = lax.rsqrt(jnp.mean(residual * residual, axis=1, keepdims=True) + eps)
    weighted = c[N.gh2][...] * c[N.gains][1:2, :]
    inner = jnp.mean(residual * weighted, axis=1, keepdims=True)
    gx2[...] = (
        c[N.cot][...].astype(F) + scale * weighted - residual * (scale * scale * scale) * inner
    )
    c.send(N.gx2)
    branch = gx2[...].astype(B)
    c.wait(N.eo)
    red = nt(branch, weight[D:, :]).astype(B)
    c.wait(N.weight)
    for block in range(3):
        at = slice(block * 384, (block + 1) * 384)
        go[:, at] = (nt(branch, weight[at, :]) + nn(red, c[N.ao][:, at])).astype(B)
    grow = functools.partial(put, late, LATE_OFF)
    oa = c[N.oa]
    grow(N.wr, line, tn(red, oa[:, :D]), 0)
    grow(N.oe, line, tn(oa[:, D:], branch), 0)
    gqkv, gk, gv = near[N.gqkv], near[N.gk], near[N.gv]
    q, kd, vd, lse, bias, cosine, sine = (
        c[k] for k in (N.q, N.kd, N.vd, N.lse, N.bias, N.cosine, N.sine)
    )
    masks = [mask.astype(B) for mask in half_masks()]
    wide_masks = half_masks()

    def turn_back(value, low_row, high_row):
        first = lax.broadcasted_iota(jnp.int32, value.shape, 1) % 64 < 32
        return (
            value * cosine[low_row:high_row, :]
            - swap_halves(value, first) * sine[low_row:high_row, :]
        )

    def tile(i, _):
        gk[...] = jnp.zeros(gk.shape, F)
        gv[...] = jnp.zeros(gv.shape, F)
        lanes = [pl.ds(pl.multiple_of((3 * i + t) * 128, 128), 128) for t in range(3)]
        outs = {}
        for side in range(2):
            group = pl.ds(pl.multiple_of((2 * i + side) * 128, 128), 128)
            for block, (low_row, high_row, keys) in enumerate(BLOCKS):
                count = high_row - low_row
                query, grad, inner, total = [], [], [], []
                for slot in range(3):
                    t, half = divmod(3 * side + slot, 2)
                    upstream = go[low_row:high_row, lanes[t]]
                    product = upstream.astype(F) * oa[low_row:high_row, lanes[t]].astype(F)
                    query.append(q[low_row:high_row, lanes[t]] * masks[half])
                    grad.append(upstream * masks[half])
                    inner.append(jnp.sum(product * wide_masks[half], axis=1, keepdims=True))
                    total.append(lse[i, side, low_row:high_row, slot : slot + 1])
                query, grad, inner, total = (
                    jnp.concatenate(v, axis=0) for v in (query, grad, inner, total)
                )
                scores = nt(query, kd[:keys, group]).reshape(3, count, keys)
                scores = (scores + bias[low_row:high_row, :keys][None]).reshape(3 * count, keys)
                probs = jnp.exp(scores - total)
                grad_probs = nt(grad, vd[:keys, group])
                ds = (probs * (grad_probs - inner)).astype(B)
                gv[side, :keys, :] += tn(probs.astype(B), grad)
                gk[side, :keys, :] += tn(ds, query)
                result = nn(ds, kd[:keys, group])
                for slot in range(3):
                    outs[block, 3 * side + slot] = result[slot * count : (slot + 1) * count]
        for block, (low_row, high_row, _) in enumerate(BLOCKS):
            low = lax.broadcasted_iota(jnp.int32, (high_row - low_row, 128), 1) < 64
            for t in range(3):
                value = jnp.where(low, outs[block, 2 * t], outs[block, 2 * t + 1])
                gqkv[low_row:high_row, lanes[t]] = turn_back(
                    value * HEAD_DIM**-0.5, low_row, high_row
                ).astype(B)
        rows = gk.shape[1]
        low = lax.broadcasted_iota(jnp.int32, (rows, 128), 1) < 64

        def fold(ref):
            both = [ref[s] + pltpu.roll(ref[s], 64, 1) for s in range(2)]
            return jnp.where(low, both[0], both[1])

        at = pl.multiple_of(i * 128, 128)
        gqkv[:, pl.ds(D + at, 128)] = turn_back(fold(gk), 0, rows).astype(B)
        gqkv[:, pl.ds(D + KVW + at, 128)] = fold(gv).astype(B)
        return 0

    h1a, ebd = c[N.h1a], c[N.ebd]
    lax.fori_loop(0, 3, tile, 0)
    c.send(N.gqkv)
    red = nt(gqkv[...], ebd[...]).astype(B)
    near[N.gred][...] = red
    c.send(N.gred)
    value = tn(red, h1a[:, :D])
    grow(N.qr, line, value, 0)
    grow(N.kr, line, value, 16)
    grow(N.vr, line, value, 32)
    value = tn(h1a[:, D:], gqkv[...])
    grow(N.qe, line, value[:, :D], 0)
    grow(N.ke, line, value[:, D : D + KVW], 16)
    grow(N.ve, line, value[:, D + KVW :], 32)
    hand_out(late, near[N.late])
    c.send(N.late)


def finish_body(c, pieces):
    near = c.near
    weight, out = near[N.weight], near[N.out]
    c.fetch(N.x, N.gqkv, N.gred, N.acat, N.gains)
    c.fetch_rows(N.wq, pieces, 0, D, weight)
    c.fetch_rows(N.wkv, pieces, D, 2 * KVW, weight, to=D)
    c.fetch(N.gx2)
    source = c[N.x][...].astype(F)
    scale = lax.rsqrt(jnp.mean(source * source, axis=1, keepdims=True) + eps)
    inner = jnp.zeros((source.shape[0], 1), F)
    gqkv = c[N.gqkv]
    c.wait(N.wq)
    for block in range(3):
        at = slice(block * 384, (block + 1) * 384)
        out[:, at] = nt(gqkv[:, :D], weight[at, :D]) + nn(c[N.gred][...], c[N.acat][:, at])
    c.wait(N.wkv)
    for block in range(3):
        at = slice(block * 384, (block + 1) * 384)
        value = out[:, at] + nt(gqkv[:, D:], weight[at, D:])
        value = value * c[N.gains][0:1, at]
        out[:, at] = value
        inner += jnp.sum(value * c[N.x][:, at].astype(F), axis=1, keepdims=True)
    inner = inner / D
    out[...] = c[N.gx2][...] + scale * out[...] - source * (scale * scale * scale) * inner
    c.send(N.out)


def after(value, *earlier):
    return lax.optimization_barrier((value, earlier))[0]


def swap(value, bit, what):
    with jax.named_scope(what):
        return lax.ppermute(value, N.shard, [(i, i ^ bit) for i in range(PARTS)])


def halves_kernel(y, x, y_out, x_out, sems):
    copies = [
        pltpu.make_async_copy(y.at[:, pl.ds(0, HALF)], y_out, sems.at[0]),
        pltpu.make_async_copy(x.at[:, pl.ds(HALF, HALF)], x_out, sems.at[1]),
    ]
    for copy in copies:
        copy.start()
    for copy in copies:
        copy.wait()


class Gather:
    def __init__(self):
        self.held = {}
        self.halves = {}
        self.last = None

    def links(self, n, message, *earlier):
        message = after(message, *earlier) if earlier else message
        self.held[n, 2] = swap(message, 2, "x%d" % n)
        self.held[n, 4] = swap(message, 4, "y%d" % n)

    def across(self, n, source, at, *earlier):
        value = self.held[source, at]
        value = after(value, *earlier) if earlier else value
        with jax.named_scope("z%d_%d" % (at, n)):
            pairs = [(i, i ^ 1) for i in range(lax.axis_size(N.rep))]
            self.held[n, at] = lax.ppermute(value, N.rep, pairs)

    def cut(self, n, *earlier):
        x, y = self.held[n, 2], self.held[n, 4]
        if earlier:
            x, y = after(x, *earlier), after(y, *earlier)
        self.halves[n] = call(
            halves_kernel,
            [((ROWS, HALF), B)] * 2,
            (y, x),
            spaces={0: pltpu.HBM, 1: pltpu.HBM},
            scratch=[pltpu.SemaphoreType.DMA((2,))],
            name=N.halves,
        )
        return self.halves[n]

    def corner(self, n, *earlier):
        if n in self.halves:
            y, x = (after(half, *earlier) for half in self.halves[n])
        else:
            y, x = self.cut(n, *earlier)
        self.held[n, 6] = swap(y, 2, "dx%d" % n)
        self.held[n, 8] = swap(x, 4, "dy%d" % n)

    def core(self, n, at, *earlier):
        value = after(self.held[n, at], *earlier) if earlier else self.held[n, at]
        self.held[n, at + 1] = swap(value, 1, "c%d_%d" % (at, n))

    def blocks(self, n):
        return [self.held[n, at] for at in (0, 1, 2, 3, 4, 5, 6, 8, 7, 9)]


def exchange(grads):
    count = PARTS * QUARTERS
    lanes = grads.shape[3]
    received = lax.all_to_all(grads.reshape(count, RANK, lanes), (N.rep, N.shard), 0, 0)
    return received.reshape(count * RANK, lanes)


def add_up(received, trees, slots):
    return call(
        add_up_kernel,
        [((received.shape[1], ADAPTERS * RANK), B)],
        (trees, slots, received),
        spaces={0: pltpu.SMEM, 1: pltpu.SMEM},
        name=N.add_up,
    )[0]


def add_up_kernel(trees, slots, received, out):
    chosen = choose(trees, slots, 0, PARTS * QUARTERS)
    out[...] = tn(received[...], chosen).astype(B)


def share(quarter):
    return [quarter] + [
        lax.ppermute(quarter, N.rep, [(i, i ^ step) for i in range(QUARTERS)])
        for step in range(1, QUARTERS)
    ]


def deliver_kernel(kinds, rep, *refs):
    refs = list(refs)
    take = lambda count: [refs.pop(0) for _ in range(count)]
    parts = [take(QUARTERS) for _ in kinds]
    outs = [take(len(names)) for names, _ in kinds]
    for (names, offsets), pieces, results, whole in zip(kinds, parts, outs, refs):
        rows = pieces[0].shape[0]
        for step, part in enumerate(pieces):
            at = pl.multiple_of((rep[0] ^ step) * rows, rows)
            whole[pl.ds(at, rows), :] = part[...].astype(F)
        for name, out in zip(names, results):
            out[...] = whole[offsets[name] : offsets[name] + SEG_ROWS[name], :]


def on_device(*args):
    x, cot, gain_a, gain_h = args[:4]
    weights = args[4:11]
    adapters = args[11:25]
    parents, device_tree, tree_adapter = args[25:]
    count = lax.axis_size(N.shard)
    shard = lax.axis_index(N.shard)
    group = lax.axis_index(N.rep) * count
    rows = x.shape[0]
    direct = count == PARTS and lax.axis_size(N.rep) == QUARTERS

    if direct:
        parity = lax.axis_index(N.rep) % 2
        gather = Gather()
        held = gather.held
        facts = jnp.stack([group, parity]).astype(jnp.int32)
        held[1, 0], held[0, 0], sent = call(
            pack_first_kernel,
            [((ROWS, MSG), B), ((ROWS, MSG), B), ((PARTS * RANK, LANES), B)],
            (facts, device_tree, tree_adapter, *weights, gain_a, gain_h, *adapters),
            spaces={
                **{n: pltpu.SMEM for n in range(3)},
                **{n: pltpu.HBM for n in range(3, 10)},
            },
            scratch=[
                pltpu.VMEM((PARTS * RANK, LANES), F),
                pltpu.SemaphoreType.DMA((SLICE_COPIES + 4,)),
            ],
            name=N.pack_first,
        )
        held[2, 0], held[3, 0] = pack_slices((1 - parity, 2), weights[4:])
        pos = jnp.bitwise_xor(shard, jnp.arange(PARTS, dtype=jnp.int32))
        pos = jnp.concatenate([pos, jnp.full((PARTS,), parity)]).astype(jnp.int32)
        packed = lax.all_to_all(sent.reshape(PARTS, RANK, LANES), N.shard, 0, 0)
        gather.links(1, held[1, 0])
        gather.links(0, held[0, 0])
        for n in range(4):
            gather.core(n, 0)
        first_halves = gather.cut(1)
        early_on = [held[n, 1] for n in range(4)] + list(first_halves)
        for at in (2, 4):
            gather.across(2, 1, at, held[1, 2], held[1, 4], *early_on)
        gather.corner(0, held[0, 2], held[0, 4], held[2, 2], *first_halves)
    else:
        whole = [lax.all_gather(w, N.shard, axis=0, tiled=True) for w in weights]
        cut = lambda w, j: lax.slice_in_dim(
            w, j * (w.shape[0] // PARTS), (j + 1) * (w.shape[0] // PARTS)
        )
        attention = [pack_attention([cut(w, j) for w in whole[:4]]) for j in range(PARTS)]
        hidden = [
            pack_slices(range(SLICES), [cut(w, j) for w in whole[4:]]) for j in range(PARTS)
        ]
        blocks = [attention] + [[hidden[j][f] for j in range(PARTS)] for f in range(SLICES)]
        blocks = [
            [b[m][:, low:high] if high - low < MSG else b[m] for m, low, high in HELD]
            for b in blocks
        ]
        pos = jnp.arange(PARTS, dtype=jnp.int32)
        pos = jnp.concatenate([pos, jnp.zeros_like(pos)])
        offset = tree_adapter[device_tree[group + shard]] * RANK
        segments = {}
        for name, part in zip(NAMES, adapters):
            full = lax.all_gather(part, N.shard, axis=0, tiled=True)
            own = lax.dynamic_slice_in_dim(full, offset, RANK, 1)
            segments[name] = own.reshape(PARTS, -1, RANK).transpose(0, 2, 1)
        both = jnp.stack(
            [lax.all_gather(g, N.shard, axis=0, tiled=True) for g in (gain_a, gain_h)]
        )
        both = both.reshape(2, PARTS, ROWS).transpose(1, 0, 2)
        segments[N.gain] = jnp.pad(both, ((0, 0), (0, RANK - 2), (0, 0)))
        packed = jnp.concatenate([segments[name] for name in OFF], axis=2)
        packed = jnp.pad(packed, ((0, 0), (0, 0), (0, LANES - packed.shape[2])))

    allowed, positions = tree_layout(parents[0], rows)
    bias = jnp.where(allowed, 0.0, -1e30).astype(F)
    cosine, sine = rope_tables(positions)
    ready = launch(
        N.prepare,
        prepare_body,
        dict(
            acat=((128, D), B),
            ebd=((128, QKV), B),
            ao=((128, D), B),
            eo=((128, D), B),
            agu=((128, D), B),
            ed=((128, D), B),
            egu=((SLICES, 128, 2 * SL), B),
            ad=((SLICES, SL, 128), B),
            gains=((RANK, D), F),
            h1a=((rows, WIDE), B),
            cota=((rows, WIDE), B),
        ),
        dict(packed=packed, x=x, cot=cot),
        scratch=dict(line=((RANK, D), F), wide=((PARTS, RANK, LANES), F)),
    )
    if direct:
        gather.corner(1, held[0, 2], held[0, 4], held[2, 2], ready[N.h1a], bias, cosine, sine)
        for at in (2, 4):
            gather.core(0, at, ready[N.h1a], bias, cosine, sine)
        for at in (6, 8):
            gather.core(0, at)
        blocks = [gather.blocks(0)]
    tables = dict(bias=bias, cosine=cosine, sine=sine)
    some = lambda *names: {name: ready[name] for name in names}
    front = launch(
        N.project,
        project_body,
        dict(q=((rows, D), B), kd=((rows, 2 * KVW), B), vd=((rows, 2 * KVW), B)),
        dict(cosine=cosine, sine=sine, **some(N.h1a, N.ebd)),
        blocks[0],
        pos,
        scratch=dict(weight=((WIDE, QKV), B)),
    )
    if direct:
        ahead = [front[N.q], held[1, 6], held[1, 8], held[2, 4]]
        gather.core(1, 2, *ahead)
        gather.links(3, held[3, 0], *ahead)
        for at in (6, 8):
            gather.across(2, 1, at, *ahead)
    front.update(
        launch(
            N.attend,
            attend_body,
            dict(
                oa=((rows, WIDE), B),
                lse=((3, 2, rows, 128), F),
                x2=((rows, D), F),
                h2a=((rows, WIDE), B),
            ),
            dict(x=x, bias=bias, **front, **some(N.ao, N.eo, N.agu, N.gains)),
            blocks[0],
            pos,
            scratch=dict(wout=((WIDE, D), B)),
        )
    )
    h2a, x2 = front[N.h2a], front[N.x2]
    if direct:
        both = [held[3, at] for at in (2, 4)]
        gather.corner(3, h2a, *both)
        for n in (1, 2):
            for at in (4, 6, 8) if n == 1 else (2, 4, 6, 8):
                gather.core(n, at, h2a, *both)
    state = None
    for slices in RUNS:
        first, last = slices[0] == 0, slices[-1] == SLICES - 1
        if direct:
            if last:
                for at in (2, 4, 6, 8):
                    gather.core(3, at, state[N.early])
            for f in slices:
                if len(blocks) < f + 2:
                    blocks.append(gather.blocks(1 + f))
        ins = dict(h2a=h2a, **some(N.cota, N.egu, N.ad))
        count = len(slices)
        scratch = dict(
            wgu=((count, WIDE, 2 * SL), B),
            wd=((count, SL, WIDE), B),
            tail=((count, PARTS * 16, SL), B),
            mid=((rows, SL), B),
            ggt=((rows, SL), B),
            gup=((rows, SL), B),
            line=((RANK, D), F),
        )
        scratch.update(
            y_acc=((rows, WIDE), F),
            g_acc=((rows, WIDE), F),
            early_acc=((PARTS, RANK, EARLY_LANES), F),
        )
        outs = dict(
            y=((rows, WIDE), B), g=((rows, WIDE), B), early=((PARTS, RANK, EARLY_LANES), B)
        )
        if not first:
            ins.update(y_in=state[N.y], g_in=state[N.g], early_in=state[N.early])
        if last:
            ins.update(x2=x2, **some(N.agu, N.ed))
            outs = dict(
                y=((rows, D), B),
                g=((rows, D), F),
                early=((QUARTERS, PARTS, RANK, EARLY_LANES // QUARTERS), B),
            )
        state = launch(
            "hidden_%d" % slices[0],
            functools.partial(hidden_body, slices),
            outs,
            ins,
            [piece for f in slices for piece in blocks[1 + f]],
            pos,
            scratch,
            sems=64 + 80 * count,
        )
    layer_output, gh2, early = state[N.y], state[N.g], state[N.early]
    if direct:
        early_come = exchange(early)
    operands = dict(gh2=gh2, x2=x2, cot=cot, **tables, **some(N.ao, N.eo, N.gains, N.h1a, N.ebd))
    operands.update({name: front[name] for name in (N.q, N.kd, N.vd, N.oa, N.lse)})
    back = launch(
        N.back,
        back_body,
        dict(
            gx2=((rows, D), F),
            gqkv=((rows, QKV), B),
            gred=((rows, 128), B),
            late=((QUARTERS, PARTS, RANK, LATE_LANES // QUARTERS), B),
        ),
        operands,
        blocks[0],
        pos,
        dict(
            weight=((WIDE, D), B),
            go=((rows, D), B),
            gk=((2, rows, 128), F),
            gv=((2, rows, 128), F),
            line=((RANK, D), F),
            late_acc=((PARTS, RANK, LATE_LANES), F),
        ),
    )
    late = back[N.late]
    if direct:
        early_come, late = lax.optimization_barrier((early_come, late))
        late_come = exchange(late)
        early_parts = share(add_up(early_come, device_tree, tree_adapter))
        late_quarter = add_up(late_come, device_tree, tree_adapter)
    input_grad = launch(
        N.finish,
        finish_body,
        dict(out=((rows, D), F)),
        dict(
            x=x, gx2=back[N.gx2], gqkv=back[N.gqkv], gred=back[N.gred], **some(N.acat, N.gains)
        ),
        blocks[0],
        pos,
        dict(weight=((D, QKV), B)),
    )[N.out]
    owned = {}
    kinds = ((EARLY, EARLY_OFF), (LATE, LATE_OFF))
    if direct:
        rep = lax.axis_index(N.rep).astype(jnp.int32).reshape(1)
        late_parts = share(late_quarter)
        received = call(
            functools.partial(deliver_kernel, kinds),
            [((SEG_ROWS[name], ADAPTERS * RANK), F) for name in EARLY + LATE],
            (rep, *early_parts, *late_parts),
            spaces={0: pltpu.SMEM},
            scratch=[
                pltpu.VMEM((QUARTERS * parts[0].shape[0], ADAPTERS * RANK), F)
                for parts in (early_parts, late_parts)
            ],
            name=N.deliver,
        )
        owned.update(zip(EARLY + LATE, received))
    else:
        for grads, (names, offsets) in zip((early, late), kinds):
            grads = grads.transpose(1, 2, 0, 3).reshape(PARTS, RANK, -1)
            for name in names:
                part = grads[:, :, offsets[name] : offsets[name] + SEG_ROWS[name]]
                part = part.transpose(0, 2, 1).reshape(-1, RANK)
                wide = lax.dynamic_update_slice_in_dim(
                    jnp.zeros((part.shape[0], ADAPTERS * RANK), B), part, offset, 1
                )
                wide = lax.psum_scatter(wide, N.shard, scatter_dimension=0, tiled=True)
                owned[name] = lax.psum(wide, N.rep).astype(F)
    return (layer_output, input_grad) + tuple(owned[name] for name in NAMES)


def solution(mesh):
    token = P((N.rep, N.shard), None)
    row = P(N.shard, None)
    return jax.shard_map(
        on_device,
        mesh=mesh,
        in_specs=(token, token, P(N.shard), P(N.shard)) + (row,) * 21 + (token, P(), P()),
        out_specs=(token, token) + (row,) * 14,
        check_vma=False,
    )
```
